32 devices in a mesh: dp: 8 (over z, y), row: 2 (over core), col: 2 (over x).
Axes of the slice: x: 2, y: 2, z: 4, core: 2. Of those that a mesh axis runs over, the one named last changes fastest.
Arguments:
- tokens: bfloat16 [8192, 2048], P('dp', 'row'), may hold values from -6 to 6
- segment_ids: int32 [8192], P('dp'), may hold values from 0 to 31, never falling along the last dimension, each value on 1 to 1024 neighbouring positions
- cotangent: bfloat16 [8192, 2048], P('dp', 'row'), may hold values from -6 to 6
- g_attn: float32 [2048], P('row'), may hold values from 0.5 to 1.5
- query_weight: bfloat16 [2048, 2048], P('row', 'col'), may hold values from -0.125 to 0.125
- key_weight: bfloat16 [2048, 256], P('row', 'col'), may hold values from -0.125 to 0.125
- value_weight: bfloat16 [2048, 256], P('row', 'col'), may hold values from -0.125 to 0.125
- w_o: bfloat16 [2048, 2048], P('col', 'row'), may hold values from -0.5 to 0.5
- g_mlp: float32 [2048], P('row'), may hold values from 0.5 to 1.5
- w_gate: bfloat16 [2048, 5632], P('row', 'col'), may hold values from -0.125 to 0.125
- w_up: bfloat16 [2048, 5632], P('row', 'col'), may hold values from -0.125 to 0.125
- w_down: bfloat16 [5632, 2048], P('col', 'row'), may hold values from -0.15625 to 0.15625
Outputs:
- mixed: bfloat16 [8192, 2048], P('dp', 'row')
- d_tokens: float32 [8192, 2048], P('dp', 'row')
- d_g_attn: float32 [2048], P(('row', 'dp'))
- d_w_q: float32 [2048, 2048], P(('row', 'dp'), 'col')
- d_w_k: float32 [2048, 256], P(('row', 'dp'), 'col')
- d_w_v: float32 [2048, 256], P(('row', 'dp'), 'col')
- d_w_o: float32 [2048, 2048], P('col', ('row', 'dp'))
- d_g_mlp: float32 [2048], P(('row', 'dp'))
- d_w_gate: float32 [2048, 5632], P(('row', 'dp'), 'col')
- d_w_up: float32 [2048, 5632], P(('row', 'dp'), 'col')
- d_w_down: float32 [5632, 2048], P('col', ('row', 'dp'))
The draws below stay inside these ranges and needn't reach their ends.
Inputs may be any that keep to these rules, and one draw needn't show every extreme that they name: `segment_ids`: segment ids never fall along the tokens; each segment has 1 to 1024 tokens and one has exactly 1024.
All inputs are finite; a program needn't handle non-finite values.
Results may differ from the reference program's by a relative error of at most 0.033.
Values may be sent and summed in bfloat16 or wider, within the bound.
No kernel may reach another device: no remote copies, remote signals or barrier semaphores. Data moves between devices by JAX's collectives and lax.ppermute only.
A program may use at most 256 MiB of HBM per device.

```python
import math
import jax
import jax.numpy as jnp
import numpy as np
from jax import lax

MODEL_WIDTH = 2048
QUERY_HEADS = 32
KEY_VALUE_HEADS = 4
HEAD_SIZE = 64
FF = 5632
SEQ = 1024
TOKENS = 8192


def raised(entries, own_key, source, target, blocks, factor):
    def block_of(axis_at):
        return (jnp.arange(entries.shape[axis_at]) // (entries.shape[axis_at] // blocks)).reshape((-1,) + (1,) * (entries.ndim - 1 - axis_at))

    first = jax.random.permutation(own_key, blocks)[block_of(target)]
    other_side = (block_of(target) + blocks // 2) % blocks
    return jnp.where((block_of(source) == first) | (block_of(source) == other_side), factor * entries, entries)


def block_levels(stream_key, shape, cuts, smallest, top_value):
    factor_of = 1.0
    for position, shards_of in cuts:
        steps = jax.random.uniform(jax.random.fold_in(jax.random.fold_in(stream_key, 6), position), (shards_of,), jnp.float32, smallest / len(cuts), top_value / len(cuts))
        factor_of = factor_of * jnp.repeat(jnp.exp(steps), shape[position] // shards_of).reshape((-1,) + (1,) * (len(shape) - 1 - position))
    return factor_of


def length_profile(count, total, reach, slope):
    loads = [(1 << 20) // math.isqrt(standing ** slope) + 1 for standing in range(2, count + 1)]
    rest, given = total - reach - (count - 1), [1] * (count - 1)
    while rest > 0:
        candidates = [i for i in range(count - 1) if given[i] < reach]
        pool, left = sum([loads[i] for i in candidates]), rest
        for i in candidates:
            more = min(reach - given[i], max(1, left * loads[i] // pool), rest)
            given[i] = given[i] + more
            rest = rest - more
    return np.array([reach] + given)


def uneven_parts(own_key, amount, total, reach, slope):
    if amount == 2:
        one = jax.random.randint(own_key, (), max(1, total - reach), min(reach, total - 1) + 1)
        return jnp.stack([one, total - one])
    tallies = jnp.asarray(length_profile(amount, total, reach, slope), jnp.int32)
    couples = (amount - 1) // 2
    source_of, taker = tallies[1:1 + 2 * couples:2], tallies[2:2 + 2 * couples:2]
    slack = jnp.minimum(source_of - 1, reach - taker)
    passed = jax.random.randint(jax.random.fold_in(own_key, 1), (couples,), 0, 1 << 20) % (slack + 1)
    tallies = tallies.at[1:1 + 2 * couples:2].set(source_of - passed).at[2:2 + 2 * couples:2].set(taker + passed)
    return tallies[jax.random.permutation(jax.random.fold_in(own_key, 2), amount)]


def centred(key, dims, deviation, limit, cuts=(), kind=jnp.bfloat16):
    drawn = jax.random.normal(key, dims, jnp.float32) * deviation
    if len(cuts) > 0:
        drawn = block_levels(key, dims, cuts, -0.22, 0.18) * drawn
    return jnp.clip(drawn, min=-limit, max=limit).astype(kind)


def heavy_noise(rng, dims, width, bound, split, heavy, kind=jnp.bfloat16):
    entries = width * jax.random.normal(rng, dims, jnp.float32)
    if split:
        entries = entries * block_levels(rng, dims, split, -0.22, 0.18)
    return jnp.clip(raised(entries, jax.random.fold_in(rng, 3), *heavy), -bound, bound).astype(kind)


def setup_inputs(seed: int = 0) -> dict:
    key_list = jax.random.split(jax.random.key(seed), 13)
    tokens = heavy_noise(key_list[0], (TOKENS, MODEL_WIDTH), 1.0, 6.0, ((0, 8), (1, 2)), (0, 1, 8, 2.0))
    segment_ids = jnp.searchsorted(jnp.cumsum(uneven_parts(key_list[1], TOKENS // (SEQ // 4), TOKENS, SEQ, 1)), jnp.arange(TOKENS), side="right").astype(jnp.int32)
    cotangent = heavy_noise(key_list[2], (TOKENS, MODEL_WIDTH), 1.0, 6.0, ((0, 8), (1, 2)), (0, 1, 8, 2.0))
    g_attn = jnp.clip(1.0 + 0.1 * jax.random.normal(key_list[3], (MODEL_WIDTH,), jnp.float32), 0.5, 1.5)
    query_weight = centred(key_list[4], (MODEL_WIDTH, QUERY_HEADS * HEAD_SIZE), MODEL_WIDTH ** -0.5, 0.125, ((0, 2), (1, 2)))
    key_weight = centred(key_list[5], (MODEL_WIDTH, KEY_VALUE_HEADS * HEAD_SIZE), MODEL_WIDTH ** -0.5, 0.125, ((0, 2), (1, 2)))
    value_weight = centred(key_list[6], (MODEL_WIDTH, KEY_VALUE_HEADS * HEAD_SIZE), MODEL_WIDTH ** -0.5, 0.125, ((0, 2), (1, 2)))
    w_o = centred(key_list[7], (QUERY_HEADS * HEAD_SIZE, MODEL_WIDTH), (QUERY_HEADS * HEAD_SIZE // 16) ** -0.5, 0.5, ((0, 2), (1, 2)))
    g_mlp = jnp.clip(1.0 + 0.1 * jax.random.normal(key_list[8], (MODEL_WIDTH,), jnp.float32), 0.5, 1.5)
    w_gate = centred(key_list[9], (MODEL_WIDTH, FF), MODEL_WIDTH ** -0.5, 0.125, ((0, 2), (1, 2)))
    w_up = centred(key_list[10], (MODEL_WIDTH, FF), MODEL_WIDTH ** -0.5, 0.125, ((0, 2), (1, 2)))
    w_down = centred(key_list[11], (FF, MODEL_WIDTH), (FF // 4) ** -0.5, 0.15625, ((0, 2), (1, 2)))
    return {"tokens": tokens, "segment_ids": segment_ids, "cotangent": cotangent, "g_attn": g_attn, "query_weight": query_weight, "key_weight": key_weight, "value_weight": value_weight, "w_o": w_o, "g_mlp": g_mlp, "w_gate": w_gate, "w_up": w_up, "w_down": w_down}


EPS = 1e-05
THETA = 10000.0

@jax.custom_vjp
def lowered_forward(v):
    return lax.optimization_barrier(v.astype(jnp.bfloat16)).astype(jnp.float32)

@jax.custom_vjp
def lowered_backward(v):
    return v

def low_keep(v):
    return (lowered_forward(v), None)

def low_pass(kept, grad):
    return (grad,)

def back_keep(v):
    return (v, None)

def back_low(kept, grad):
    return (lowered_forward(grad),)
lowered_forward.defvjp(low_keep, low_pass)
lowered_backward.defvjp(back_keep, back_low)

def head_product(left, right):
    return jnp.dot(left, right, precision=lax.Precision.HIGHEST)

def norm(value_rows, gain):
    return value_rows * lax.rsqrt(lax.optimization_barrier(jnp.mean(value_rows * value_rows, axis=-1, keepdims=True)) + EPS) * gain

def angles(places):
    half = HEAD_SIZE // 2
    freq = jnp.exp(jnp.arange(half, dtype=jnp.float32) * (-2.0 * math.log(THETA) / HEAD_SIZE))
    turn = places.astype(jnp.float32)[:, None] * freq
    return (jnp.cos(turn), jnp.sin(turn))

def rotate(value_rows, cosine, sine):
    half = value_rows.shape[-1] // 2
    first = value_rows[..., :half]
    second = value_rows[..., half:]
    return jnp.concatenate([first * cosine - second * sine, second * cosine + first * sine], axis=-1)

def attend(query, key, value_rows, allowed, scale):
    raw = jnp.einsum('ikrd,jkd->krij', query, key, precision=lax.Precision.HIGHEST) * scale
    raw = jnp.where(allowed, lowered_backward(raw), -1e+30)
    probs = lowered_forward(jax.nn.softmax(raw, axis=-1))
    return jnp.einsum('krij,jkd->ikrd', probs, value_rows, precision=lax.Precision.HIGHEST)

def layer(x, seg, g_attn, query_weight, key_weight, value_weight, w_o, g_mlp, w_gate, w_up, w_down):
    sequence_length = x.shape[0]
    repeat_heads = QUERY_HEADS // KEY_VALUE_HEADS
    index = jnp.arange(sequence_length, dtype=jnp.int32)
    change = jnp.concatenate([jnp.ones((1,), jnp.int32), (seg[1:] != seg[:-1]).astype(jnp.int32)])
    places = index - lax.cummax(jnp.where(change > 0, index, 0), axis=0)
    cosine, sine = angles(places)
    allowed = (seg[:, None] == seg[None, :]) & (index[None, :] <= index[:, None])
    scale = HEAD_SIZE ** (-0.5)
    normed_input = lowered_forward(norm(x, g_attn))
    query_rotated = lowered_backward(head_product(normed_input, query_weight)).reshape(sequence_length, KEY_VALUE_HEADS, repeat_heads, HEAD_SIZE)
    key_rotated = lowered_backward(head_product(normed_input, key_weight)).reshape(sequence_length, KEY_VALUE_HEADS, HEAD_SIZE)
    value_rows = lowered_backward(lowered_forward(head_product(normed_input, value_weight))).reshape(sequence_length, KEY_VALUE_HEADS, HEAD_SIZE)
    query = lowered_forward(rotate(query_rotated, cosine[:, None, None, :], sine[:, None, None, :]))
    key = lowered_forward(rotate(key_rotated, cosine[:, None, :], sine[:, None, :]))
    heads = attend(query, key, value_rows, allowed, scale).reshape(sequence_length, QUERY_HEADS * HEAD_SIZE)
    heads = lowered_forward(lowered_backward(heads))
    hidden = x + lowered_backward(head_product(heads, w_o))
    xm = lowered_forward(norm(hidden, g_mlp))
    gate = lowered_backward(head_product(xm, w_gate))
    up = lowered_backward(head_product(xm, w_up))
    act = lowered_forward(jax.nn.silu(gate) * up)
    return hidden + head_product(act, w_down)

def reference(tokens, segment_ids, cotangent, g_attn, query_weight, key_weight, value_weight, w_o, g_mlp, w_gate, w_up, w_down):
    seqs = tokens.shape[0] // SEQ
    params = tuple((p.astype(jnp.float32) for p in (g_attn, query_weight, key_weight, value_weight, w_o, g_mlp, w_gate, w_up, w_down)))
    inputs = tokens.astype(jnp.float32).reshape(seqs, SEQ, MODEL_WIDTH)
    segs = segment_ids.reshape(seqs, SEQ)
    cots = cotangent.astype(jnp.float32).reshape(seqs, SEQ, MODEL_WIDTH)

    def one(carry, item):
        x, seg, cot = item

        def run(xx, *ps):
            return layer(xx, seg, *ps)
        out, pull = jax.vjp(run, x, *params)
        grads = pull(cot)
        return (tuple((c + g for c, g in zip(carry, grads[1:]))), (out, grads[0]))
    init = tuple((jnp.zeros_like(p) for p in params))
    sums, (outs, d_inputs) = lax.scan(one, init, (inputs, segs, cots))
    mixed = outs.reshape(seqs * SEQ, MODEL_WIDTH).astype(jnp.bfloat16)
    d_tokens = d_inputs.reshape(seqs * SEQ, MODEL_WIDTH)
    return (mixed, d_tokens, sums[0], sums[1], sums[2], sums[3], sums[4], sums[5], sums[6], sums[7], sums[8])
```

```python
import math

import jax
import jax.numpy as jnp
from jax import lax
from jax.experimental import pallas as pl
from jax.experimental.pallas import tpu as pltpu
from jax.sharding import PartitionSpec as P

MODEL_WIDTH = 2048
QUERY_HEADS = 32
KEY_VALUE_HEADS = 4
HEAD_SIZE = 64
SEQ = 1024

EPS = 1e-05
THETA = 10000.0
HALF = HEAD_SIZE // 2
CHUNK = SEQ // 4
OWN = SEQ // 2
PAIR = 2 * HEAD_SIZE
SCALE = HEAD_SIZE ** (-0.5)
NEG = -1e30
F32 = jnp.float32
BF16 = jnp.bfloat16


def dot_plain(left, right):
    return jnp.dot(left, right, preferred_element_type=F32)


def dot_right(left, right):
    return lax.dot_general(left, right, (((1,), (1,)), ((), ())), preferred_element_type=F32)


def dot_left(left, right):
    return lax.dot_general(left, right, (((0,), (0,)), ((), ())), preferred_element_type=F32)


def own_rows(value, row):
    a, b, c, d = (value[i * CHUNK : (i + 1) * CHUNK] for i in range(4))
    return jnp.concatenate([jnp.where(row == 0, a, b), jnp.where(row == 0, d, c)], axis=0)


def other_rows(value, row):
    a, b, c, d = (value[i * CHUNK : (i + 1) * CHUNK] for i in range(4))
    return jnp.concatenate([jnp.where(row == 0, b, a), jnp.where(row == 0, c, d)], axis=0)


def merge_rows(own, other, row):
    a, b = own[:CHUNK], own[CHUNK:]
    c, d = other[:CHUNK], other[CHUNK:]
    return jnp.concatenate(
        [
            jnp.where(row == 0, a, c),
            jnp.where(row == 0, c, a),
            jnp.where(row == 0, d, b),
            jnp.where(row == 0, b, d),
        ],
        axis=0,
    )


def chunk_bias(start_ref, bias, row):
    for c in range(2):
        place = jnp.where(row == 0, 3 * c, 1 + c) * CHUNK
        lanes = slice(c * CHUNK, (c + 1) * CHUNK)
        keys = lax.broadcasted_iota(jnp.int32, (SEQ, CHUNK), 0)
        queries = lax.broadcasted_iota(jnp.int32, (SEQ, CHUNK), 1) + place
        allowed = (keys >= start_ref[:, lanes]) & (keys <= queries)
        bias[:, lanes] = jnp.where(allowed, 0.0, NEG)


def place_keys(own_ref, other_ref, row, put):
    @pl.when(row == 0)
    def _():
        for i, (ref, half) in enumerate(((own_ref, 0), (other_ref, 0), (other_ref, 1), (own_ref, 1))):
            put(i, ref[half * CHUNK : (half + 1) * CHUNK, :])

    @pl.when(row == 1)
    def _():
        for i, (ref, half) in enumerate(((other_ref, 0), (own_ref, 0), (own_ref, 1), (other_ref, 1))):
            put(i, ref[half * CHUNK : (half + 1) * CHUNK, :])


def attend_kernel(
    row_ref, q_ref, cos_ref, sin_ref, start_ref, own_ref, other_ref, o_ref, lse_ref, qt_ref, bias, keys, values_t
):
    step = pl.program_id(0)
    kv = step // 4
    row = row_ref[0]

    @pl.when(step == 0)
    def _():
        chunk_bias(start_ref, bias, row)

        def put(i, block):
            span = slice(i * CHUNK, (i + 1) * CHUNK)
            for h in range(2):
                keys[h, span, :] = block[:, h * HEAD_SIZE : (h + 1) * HEAD_SIZE]
            turned = jnp.transpose(block[:, PAIR:].astype(F32)).astype(BF16)
            for h in range(2):
                values_t[h, :, span] = turned[h * HEAD_SIZE : (h + 1) * HEAD_SIZE]

        place_keys(own_ref, other_ref, row, put)

    turned = jnp.transpose(q_ref[...])
    cosine, sine = cos_ref[...], sin_ref[...]
    for h in range(2):
        a = turned[h * HEAD_SIZE : h * HEAD_SIZE + HALF]
        b = turned[h * HEAD_SIZE + HALF : (h + 1) * HEAD_SIZE]
        rot = jnp.concatenate([a * cosine - b * sine, b * cosine + a * sine], axis=0)
        qt_ref[h * HEAD_SIZE : (h + 1) * HEAD_SIZE, :] = (rot * SCALE).astype(BF16)

    def unit(c, blocks):
        lanes = slice(c * CHUNK, (c + 1) * CHUNK)
        count = blocks * CHUNK
        outs, sums = [], []
        for h in range(2):
            query = qt_ref[h * HEAD_SIZE : (h + 1) * HEAD_SIZE, lanes]
            scores = dot_plain(keys[kv, :count, :], query) + bias[:count, lanes]
            top = jnp.max(scores, axis=0, keepdims=True)
            expo = jnp.exp(scores - top)
            total = jnp.sum(expo, axis=0, keepdims=True)
            head = dot_plain(values_t[kv, :, :count], expo.astype(BF16))
            outs.append(head * (1.0 / total))
            sums.append(top + jnp.log(total))
        o_ref[lanes, :] = jnp.transpose(jnp.concatenate(outs, axis=0)).astype(BF16)
        lse_ref[0, :, lanes] = jnp.concatenate(sums, axis=0)

    @pl.when(row == 0)
    def _():
        unit(0, 1)
        unit(1, 4)

    @pl.when(row == 1)
    def _():
        unit(0, 2)
        unit(1, 3)


def attend(row, q, cosine, sine, start, own_kv, other_kv):
    heads = q.shape[1] // HEAD_SIZE
    pairs = heads // 2
    whole = lambda shape: pl.BlockSpec(shape, lambda i: (0,) * len(shape))
    return pl.pallas_call(
        attend_kernel,
        grid=(pairs,),
        in_specs=[
            pl.BlockSpec(memory_space=pltpu.SMEM),
            pl.BlockSpec((OWN, PAIR), lambda i: (0, i)),
            whole((HALF, OWN)),
            whole((HALF, OWN)),
            whole((1, OWN)),
            whole((OWN, 2 * PAIR)),
            whole((OWN, 2 * PAIR)),
        ],
        out_specs=[
            pl.BlockSpec((OWN, PAIR), lambda i: (0, i)),
            pl.BlockSpec((1, 2, OWN), lambda i: (i, 0, 0)),
            pl.BlockSpec((PAIR, OWN), lambda i: (i, 0)),
        ],
        out_shape=[
            jax.ShapeDtypeStruct((OWN, heads * HEAD_SIZE), BF16),
            jax.ShapeDtypeStruct((pairs, 2, OWN), F32),
            jax.ShapeDtypeStruct((heads * HEAD_SIZE, OWN), BF16),
        ],
        scratch_shapes=[
            pltpu.VMEM((SEQ, OWN), F32),
            pltpu.VMEM((2, SEQ, HEAD_SIZE), BF16),
            pltpu.VMEM((2, HEAD_SIZE, SEQ), BF16),
        ],
        compiler_params=pltpu.CompilerParams(vmem_limit_bytes=40 * 1024 * 1024),
        cost_estimate=pl.CostEstimate(flops=20_000_000_000, bytes_accessed=8_000_000, transcendentals=0),
        name="attend",
    )(row, q, cosine, sine, start, own_kv, other_kv)


def attend_back_kernel(
    row_ref,
    qt_ref,
    do_ref,
    o_ref,
    lse_ref,
    cos_ref,
    sin_ref,
    start_ref,
    own_ref,
    other_ref,
    dq_ref,
    dk_ref,
    dv_ref,
    bias,
    keys,
    keys_t,
    values,
):
    step = pl.program_id(0)
    kv = step // 4
    row = row_ref[0]

    @pl.when(step == 0)
    def _():
        chunk_bias(start_ref, bias, row)

        def put(i, block):
            span = slice(i * CHUNK, (i + 1) * CHUNK)
            for h in range(2):
                keys[h, span, :] = block[:, h * HEAD_SIZE : (h + 1) * HEAD_SIZE]
                values[h, span, :] = block[:, PAIR + h * HEAD_SIZE : PAIR + (h + 1) * HEAD_SIZE]
            turned = jnp.transpose(block[:, :PAIR].astype(F32)).astype(BF16)
            for h in range(2):
                keys_t[h, :, span] = turned[h * HEAD_SIZE : (h + 1) * HEAD_SIZE]

        place_keys(own_ref, other_ref, row, put)

    @pl.when(step % 4 == 0)
    def _():
        dk_ref[...] = jnp.zeros_like(dk_ref)
        dv_ref[...] = jnp.zeros_like(dv_ref)

    grad = do_ref[...].astype(F32)
    grad_t = jnp.transpose(grad)
    mixed_t = jnp.transpose(grad * o_ref[...].astype(F32))
    cosine, sine = cos_ref[...], sin_ref[...]

    def unit(c, blocks):
        lanes = slice(c * CHUNK, (c + 1) * CHUNK)
        count = blocks * CHUNK
        outs = []
        for h in range(2):
            rows = slice(h * HEAD_SIZE, (h + 1) * HEAD_SIZE)
            query = qt_ref[rows, lanes]
            d_head = grad_t[rows, lanes].astype(BF16)
            delta = jnp.sum(mixed_t[rows, lanes], axis=0, keepdims=True)
            scores = dot_plain(keys[kv, :count, :], query) + bias[:count, lanes]
            probs = jnp.exp(scores - lse_ref[0, h : h + 1, lanes])
            dv_ref[0, :count, :] += dot_right(probs.astype(BF16), d_head)
            d_probs = dot_plain(values[kv, :count, :], d_head)
            d_raw = (probs * (d_probs - delta)).astype(BF16)
            d_query = dot_plain(keys_t[kv, :, :count], d_raw) * SCALE
            dk_ref[0, :count, :] += dot_right(d_raw, query)
            a, b = d_query[:HALF], d_query[HALF:]
            co, si = cosine[:, lanes], sine[:, lanes]
            outs.append(a * co + b * si)
            outs.append(b * co - a * si)
        dq_ref[lanes, :] = jnp.transpose(jnp.concatenate(outs, axis=0)).astype(BF16)

    @pl.when(row == 0)
    def _():
        unit(0, 1)
        unit(1, 4)

    @pl.when(row == 1)
    def _():
        unit(0, 2)
        unit(1, 3)


def attend_back(row, qt, d_o, o, lse, cosine, sine, start, own_kv, other_kv):
    heads = qt.shape[0] // HEAD_SIZE
    pairs = heads // 2
    whole = lambda shape: pl.BlockSpec(shape, lambda i: (0,) * len(shape))
    return pl.pallas_call(
        attend_back_kernel,
        grid=(pairs,),
        in_specs=[
            pl.BlockSpec(memory_space=pltpu.SMEM),
            pl.BlockSpec((PAIR, OWN), lambda i: (i, 0)),
            pl.BlockSpec((OWN, PAIR), lambda i: (0, i)),
            pl.BlockSpec((OWN, PAIR), lambda i: (0, i)),
            pl.BlockSpec((1, 2, OWN), lambda i: (i, 0, 0)),
            whole((HALF, OWN)),
            whole((HALF, OWN)),
            whole((1, OWN)),
            whole((OWN, 2 * PAIR)),
            whole((OWN, 2 * PAIR)),
        ],
        out_specs=[
            pl.BlockSpec((OWN, PAIR), lambda i: (0, i)),
            pl.BlockSpec((1, SEQ, HEAD_SIZE), lambda i: (i // 4, 0, 0)),
            pl.BlockSpec((1, SEQ, HEAD_SIZE), lambda i: (i // 4, 0, 0)),
        ],
        out_shape=[
            jax.ShapeDtypeStruct((OWN, heads * HEAD_SIZE), BF16),
            jax.ShapeDtypeStruct((2, SEQ, HEAD_SIZE), F32),
            jax.ShapeDtypeStruct((2, SEQ, HEAD_SIZE), F32),
        ],
        scratch_shapes=[
            pltpu.VMEM((SEQ, OWN), F32),
            pltpu.VMEM((2, SEQ, HEAD_SIZE), BF16),
            pltpu.VMEM((2, HEAD_SIZE, SEQ), BF16),
            pltpu.VMEM((2, SEQ, HEAD_SIZE), BF16),
        ],
        compiler_params=pltpu.CompilerParams(vmem_limit_bytes=40 * 1024 * 1024),
        cost_estimate=pl.CostEstimate(flops=40_000_000_000, bytes_accessed=8_000_000, transcendentals=0),
        name="attend_back",
    )(row, qt, d_o, o, lse, cosine, sine, start, own_kv, other_kv)


def shards(
    count,
    tokens,
    segment_ids,
    cotangent,
    g_attn,
    query_weight,
    key_weight,
    value_weight,
    w_o,
    g_mlp,
    w_gate,
    w_up,
    w_down,
):
    row = lax.axis_index("row")
    dp = lax.axis_index("dp")
    bits = count.bit_length() - 1

    def swap(value):
        return lax.ppermute(value, "row", [(0, 1), (1, 0)])

    def cross(value):
        return lax.ppermute(value, "col", [(0, 1), (1, 0)])

    def flip(value, bit):
        return lax.ppermute(value, "dp", [(i, i ^ (1 << bit)) for i in range(count)])

    def order_of(first):
        return ([first] + [b for b in range(bits) if b != first]) if bits else []

    def relative(value, order):
        width = value.shape[1] // count
        blocks = []
        for place in range(count):
            differs = 0
            for at, bit in enumerate(order):
                differs |= ((place >> (len(order) - 1 - at)) & 1) << bit
            blocks.append(lax.dynamic_slice_in_dim(value, (dp ^ differs) * width, width, axis=1))
        return jnp.concatenate(blocks, axis=1)

    def half_of(value, axis, upper):
        size = value.shape[axis] // 2
        return lax.slice_in_dim(value, size if upper else 0, 2 * size if upper else size, axis=axis)

    def scatter_sum(left, right, axis, order):
        if not order:
            return dot_left(left, right)
        if axis == 0:
            send = dot_left(half_of(left, 1, True), right)
            keep = dot_left(half_of(left, 1, False), right)
        else:
            send = dot_left(left, half_of(right, 1, True))
            keep = dot_left(left, half_of(right, 1, False))
        for at, bit in enumerate(order):
            came = flip(send.astype(BF16), bit)
            total = keep + came.astype(F32)
            if at + 1 < len(order):
                send = half_of(total, axis, True)
                keep = half_of(total, axis, False)
        return total

    wqkv = jnp.concatenate([query_weight, key_weight, value_weight], axis=1)
    x_m = own_rows(tokens, row)
    x_o = swap(other_rows(tokens, row))
    wqkv_o = swap(wqkv)
    gains = jnp.stack([g_attn, g_mlp])
    gains_o = swap(gains)
    w_o_x = cross(w_o)
    c_m = own_rows(cotangent, row)
    c_t = other_rows(cotangent, row)
    c_o = swap(c_t)
    w_o_o = swap(w_o)
    wg_o = swap(w_gate)
    wu_o = swap(w_up)
    wd_o = swap(w_down)
    w_o_xo = swap(w_o_x)

    start = jnp.sum((segment_ids[None, :] < segment_ids[:, None]).astype(jnp.int32), axis=1)
    index = lax.iota(jnp.int32, SEQ)
    start_own = own_rows(start, row)
    places = own_rows(index, row) - start_own
    freq = jnp.exp(jnp.arange(HALF, dtype=F32) * (-2.0 * math.log(THETA) / HEAD_SIZE))
    turn_t = freq[:, None] * places.astype(F32)[None, :]
    cosine_t, sine_t = jnp.cos(turn_t), jnp.sin(turn_t)
    cosine, sine = cosine_t.T[:, None, :], sine_t.T[:, None, :]

    x_m, x_o = x_m.astype(F32), x_o.astype(F32)
    square = jnp.sum(x_m * x_m, axis=-1, keepdims=True) + jnp.sum(x_o * x_o, axis=-1, keepdims=True)
    inv_one = lax.rsqrt(square / MODEL_WIDTH + EPS)
    xn_m = (x_m * inv_one * gains[0]).astype(BF16)
    xn_o = (x_o * inv_one * gains_o[0]).astype(BF16)
    qkv = dot_plain(xn_m, wqkv) + dot_plain(xn_o, wqkv_o)
    wide = query_weight.shape[1]
    narrow = key_weight.shape[1]
    q = qkv[:, :wide]
    kp = qkv[:, wide : wide + narrow].reshape(OWN, -1, HEAD_SIZE)
    first, second = kp[..., :HALF], kp[..., HALF:]
    key = jnp.concatenate([first * cosine - second * sine, second * cosine + first * sine], axis=-1)
    own_kv = jnp.concatenate([key.reshape(OWN, narrow), qkv[:, wide + narrow :]], axis=1).astype(BF16)
    other_kv = swap(own_kv)
    row_arg = row.astype(jnp.int32).reshape(1)
    start_arg = start_own.reshape(1, OWN)
    o, lse, qt = attend(row_arg, q, cosine_t, sine_t, start_arg, own_kv, other_kv)

    o_x = cross(o)
    hidden_m = x_m + (dot_plain(o, w_o) + dot_plain(o_x, w_o_x))
    hidden_o = x_o + (dot_plain(o, w_o_o) + dot_plain(o_x, w_o_xo))
    square = jnp.sum(hidden_m * hidden_m, axis=-1, keepdims=True) + jnp.sum(
        hidden_o * hidden_o, axis=-1, keepdims=True
    )
    inv_two = lax.rsqrt(square / MODEL_WIDTH + EPS)
    unit_m, unit_o = hidden_m * inv_two, hidden_o * inv_two
    xn2_m = (unit_m * gains[1]).astype(BF16)
    xn2_o = (unit_o * gains_o[1]).astype(BF16)

    d_act = dot_right(c_m, w_down) + dot_right(c_o, wd_o)
    gate = dot_plain(xn2_m, w_gate) + dot_plain(xn2_o, wg_o)
    up = dot_plain(xn2_m, w_up) + dot_plain(xn2_o, wu_o)
    sigma = jax.nn.sigmoid(gate)
    swish = gate * sigma
    act = (swish * up).astype(BF16)
    d_gate = (d_act * up * (sigma * (1.0 + gate * (1.0 - sigma)))).astype(BF16)
    d_up = (d_act * swish).astype(BF16)
    part_m = (dot_right(d_gate, w_gate) + dot_right(d_up, w_up)).astype(BF16)
    part_o = (dot_right(d_gate, wg_o) + dot_right(d_up, wu_o)).astype(BF16)
    d_xn2_m = part_m.astype(F32) + cross(part_m).astype(F32)
    d_xn2_o = part_o.astype(F32) + cross(part_o).astype(F32)

    order_y, order_z = order_of(0), order_of(min(1, max(bits - 1, 0)))
    both = lambda own, other: jnp.concatenate([own, other], axis=0)
    act_all = both(act, swap(act))
    gw_down = scatter_sum(act_all, relative(both(c_m, c_t), order_y), 1, order_y)
    xn2_all = both(xn2_m, swap(xn2_o))
    gw_gate = scatter_sum(relative(xn2_all, order_y), both(d_gate, swap(d_gate)), 0, order_y)
    gw_up = scatter_sum(relative(xn2_all, order_z), both(d_up, swap(d_up)), 0, order_z)

    mix_m = dot_plain(act, w_down).astype(BF16)
    mix_o = dot_plain(act, wd_o).astype(BF16)

    e_m, e_o = d_xn2_m * gains[1], d_xn2_o * gains_o[1]
    mean = (
        jnp.sum(e_m * unit_m, axis=-1, keepdims=True) + jnp.sum(e_o * unit_o, axis=-1, keepdims=True)
    ) / MODEL_WIDTH
    gg_mlp_m = jnp.sum(d_xn2_m * unit_m, axis=0)
    gg_mlp_o = jnp.sum(d_xn2_o * unit_o, axis=0)
    d_hid_m = c_m.astype(F32) + inv_two * (e_m - unit_m * mean)
    d_hid_o = c_o.astype(F32) + inv_two * (e_o - unit_o * mean)
    dh_m, dh_o = d_hid_m.astype(BF16), d_hid_o.astype(BF16)
    d_o = (dot_right(dh_m, w_o) + dot_right(dh_o, w_o_o)).astype(BF16)
    gw_o = scatter_sum(both(o, swap(o)), relative(both(dh_m, swap(dh_o)), order_y), 1, order_y)

    d_q, d_k, d_v = attend_back(row_arg, qt, d_o, o, lse, cosine_t, sine_t, start_arg, own_kv, other_kv)
    d_kv = jnp.concatenate([d_k[0], d_k[1], d_v[0], d_v[1]], axis=1)
    d_kv = own_rows(d_kv, row) + swap(other_rows(d_kv, row))
    d_key = d_kv[:, :narrow].reshape(OWN, -1, HEAD_SIZE)
    first, second = d_key[..., :HALF], d_key[..., HALF:]
    d_key = jnp.concatenate([first * cosine + second * sine, second * cosine - first * sine], axis=-1)
    d_qkv = jnp.concatenate(
        [d_q, d_key.reshape(OWN, narrow).astype(BF16), d_kv[:, narrow:].astype(BF16)], axis=1
    )
    part_m = dot_right(d_qkv, wqkv).astype(BF16)
    part_o = dot_right(d_qkv, wqkv_o).astype(BF16)
    d_xn_m = part_m.astype(F32) + cross(part_m).astype(F32)
    d_xn_o = part_o.astype(F32) + cross(part_o).astype(F32)
    xn_all = both(xn_m, swap(xn_o))
    gw_qkv = scatter_sum(relative(xn_all, order_y), both(d_qkv, swap(d_qkv)), 0, order_y)

    out_m = (hidden_m + (mix_m.astype(F32) + cross(mix_m).astype(F32))).astype(BF16)
    out_o = (hidden_o + (mix_o.astype(F32) + cross(mix_o).astype(F32))).astype(BF16)
    mixed = merge_rows(out_m, swap(out_o), row)

    unit_m, unit_o = x_m * inv_one, x_o * inv_one
    e_m, e_o = d_xn_m * gains[0], d_xn_o * gains_o[0]
    mean = (
        jnp.sum(e_m * unit_m, axis=-1, keepdims=True) + jnp.sum(e_o * unit_o, axis=-1, keepdims=True)
    ) / MODEL_WIDTH
    gg_attn_m = jnp.sum(d_xn_m * unit_m, axis=0)
    gg_attn_o = jnp.sum(d_xn_o * unit_o, axis=0)
    d_tok_m = d_hid_m + inv_one * (e_m - unit_m * mean)
    d_tok_o = d_hid_o + inv_one * (e_o - unit_o * mean)
    d_tokens = merge_rows(d_tok_m, swap(d_tok_o), row)

    gg = jnp.stack([gg_attn_m, gg_mlp_m]) + swap(jnp.stack([gg_attn_o, gg_mlp_o]))
    gg = lax.psum_scatter(gg, "dp", scatter_dimension=1, tiled=True)
    return (
        mixed,
        d_tokens,
        gg[0],
        gw_qkv[:, :wide],
        gw_qkv[:, wide : wide + narrow],
        gw_qkv[:, wide + narrow :],
        gw_o,
        gg[1],
        gw_gate,
        gw_up,
        gw_down,
    )


def solution(mesh):
    count = mesh.shape["dp"]
    placed = (
        P("dp", "row"),
        P("dp"),
        P("dp", "row"),
        P("row"),
        P("row", "col"),
        P("row", "col"),
        P("row", "col"),
        P("col", "row"),
        P("row"),
        P("row", "col"),
        P("row", "col"),
        P("col", "row"),
    )

    def body(*args):
        return shards(count, *args)

    return jax.shard_map(
        body,
        mesh=mesh,
        in_specs=placed,
        out_specs=(
            P("dp", "row"),
            P("dp", "row"),
            P(("row", "dp")),
            P(("row", "dp"), "col"),
            P(("row", "dp"), "col"),
            P(("row", "dp"), "col"),
            P("col", ("row", "dp")),
            P(("row", "dp")),
            P(("row", "dp"), "col"),
            P(("row", "dp"), "col"),
            P("col", ("row", "dp")),
        ),
        check_vma=False,
    )
```

```python
import math

import jax
import jax.numpy as jnp
from jax import lax
from jax.experimental import pallas as pl
from jax.experimental.pallas import tpu as pltpu
from jax.sharding import PartitionSpec as P

MODEL_WIDTH = 2048
QUERY_HEADS = 32
KEY_VALUE_HEADS = 4
HEAD_SIZE = 64
SEQ = 1024

EPS = 1e-05
THETA = 10000.0
HALF = HEAD_SIZE // 2
CHUNK = SEQ // 4
OWN = SEQ // 2
PAIR = 2 * HEAD_SIZE
SCALE = HEAD_SIZE ** (-0.5)
NEG = -1e30
F32 = jnp.float32
BF16 = jnp.bfloat16


def dot_plain(left, right):
    return jnp.dot(left, right, preferred_element_type=F32)


def dot_right(left, right):
    return lax.dot_general(left, right, (((1,), (1,)), ((), ())), preferred_element_type=F32)


def dot_left(left, right):
    return lax.dot_general(left, right, (((0,), (0,)), ((), ())), preferred_element_type=F32)


def own_rows(value, row):
    a, b, c, d = (value[i * CHUNK : (i + 1) * CHUNK] for i in range(4))
    return jnp.concatenate([jnp.where(row == 0, a, b), jnp.where(row == 0, d, c)], axis=0)


def other_rows(value, row):
    a, b, c, d = (value[i * CHUNK : (i + 1) * CHUNK] for i in range(4))
    return jnp.concatenate([jnp.where(row == 0, b, a), jnp.where(row == 0, c, d)], axis=0)


def merge_rows(own, other, row):
    a, b = own[:CHUNK], own[CHUNK:]
    c, d = other[:CHUNK], other[CHUNK:]
    return jnp.concatenate(
        [
            jnp.where(row == 0, a, c),
            jnp.where(row == 0, c, a),
            jnp.where(row == 0, d, b),
            jnp.where(row == 0, b, d),
        ],
        axis=0,
    )


def chunk_bias(start_ref, bias, row):
    for c in range(2):
        place = jnp.where(row == 0, 3 * c, 1 + c) * CHUNK
        lanes = slice(c * CHUNK, (c + 1) * CHUNK)
        keys = lax.broadcasted_iota(jnp.int32, (SEQ, CHUNK), 0)
        queries = lax.broadcasted_iota(jnp.int32, (SEQ, CHUNK), 1) + place
        allowed = (keys >= start_ref[:, lanes]) & (keys <= queries)
        bias[:, lanes] = jnp.where(allowed, 0.0, NEG)


def place_keys(own_ref, other_ref, row, put):
    @pl.when(row == 0)
    def _():
        for i, (ref, half) in enumerate(((own_ref, 0), (other_ref, 0), (other_ref, 1), (own_ref, 1))):
            put(i, ref[half * CHUNK : (half + 1) * CHUNK, :])

    @pl.when(row == 1)
    def _():
        for i, (ref, half) in enumerate(((other_ref, 0), (own_ref, 0), (own_ref, 1), (other_ref, 1))):
            put(i, ref[half * CHUNK : (half + 1) * CHUNK, :])


def attend_kernel(
    row_ref, q_ref, cos_ref, sin_ref, start_ref, own_ref, other_ref, o_ref, lse_ref, qt_ref, bias, keys, values_t
):
    step = pl.program_id(0)
    kv = step // 4
    row = row_ref[0]

    @pl.when(step == 0)
    def _():
        chunk_bias(start_ref, bias, row)

        def put(i, block):
            span = slice(i * CHUNK, (i + 1) * CHUNK)
            for h in range(2):
                keys[h, span, :] = block[:, h * HEAD_SIZE : (h + 1) * HEAD_SIZE]
            turned = jnp.transpose(block[:, PAIR:].astype(F32)).astype(BF16)
            for h in range(2):
                values_t[h, :, span] = turned[h * HEAD_SIZE : (h + 1) * HEAD_SIZE]

        place_keys(own_ref, other_ref, row, put)

    turned = jnp.transpose(q_ref[...])
    cosine, sine = cos_ref[...], sin_ref[...]
    for h in range(2):
        a = turned[h * HEAD_SIZE : h * HEAD_SIZE + HALF]
        b = turned[h * HEAD_SIZE + HALF : (h + 1) * HEAD_SIZE]
        rot = jnp.concatenate([a * cosine - b * sine, b * cosine + a * sine], axis=0)
        qt_ref[h * HEAD_SIZE : (h + 1) * HEAD_SIZE, :] = (rot * SCALE).astype(BF16)

    def unit(c, blocks):
        lanes = slice(c * CHUNK, (c + 1) * CHUNK)
        count = blocks * CHUNK
        outs, sums = [], []
        for h in range(2):
            query = qt_ref[h * HEAD_SIZE : (h + 1) * HEAD_SIZE, lanes]
            scores = dot_plain(keys[kv, :count, :], query) + bias[:count, lanes]
            top = jnp.max(scores, axis=0, keepdims=True)
            expo = jnp.exp(scores - top)
            total = jnp.sum(expo, axis=0, keepdims=True)
            head = dot_plain(values_t[kv, :, :count], expo.astype(BF16))
            outs.append(head * (1.0 / total))
            sums.append(top + jnp.log(total))
        o_ref[lanes, :] = jnp.transpose(jnp.concatenate(outs, axis=0)).astype(BF16)
        lse_ref[0, :, lanes] = jnp.concatenate(sums, axis=0)

    @pl.when(row == 0)
    def _():
        unit(0, 1)
        unit(1, 4)

    @pl.when(row == 1)
    def _():
        unit(0, 2)
        unit(1, 3)


def attend(row, q, cosine, sine, start, own_kv, other_kv):
    heads = q.shape[1] // HEAD_SIZE
    pairs = heads // 2
    whole = lambda shape: pl.BlockSpec(shape, lambda i: (0,) * len(shape))
    return pl.pallas_call(
        attend_kernel,
        grid=(pairs,),
        in_specs=[
            pl.BlockSpec(memory_space=pltpu.SMEM),
            pl.BlockSpec((OWN, PAIR), lambda i: (0, i)),
            whole((HALF, OWN)),
            whole((HALF, OWN)),
            whole((1, OWN)),
            whole((OWN, 2 * PAIR)),
            whole((OWN, 2 * PAIR)),
        ],
        out_specs=[
            pl.BlockSpec((OWN, PAIR), lambda i: (0, i)),
            pl.BlockSpec((1, 2, OWN), lambda i: (i, 0, 0)),
            pl.BlockSpec((PAIR, OWN), lambda i: (i, 0)),
        ],
        out_shape=[
            jax.ShapeDtypeStruct((OWN, heads * HEAD_SIZE), BF16),
            jax.ShapeDtypeStruct((pairs, 2, OWN), F32),
            jax.ShapeDtypeStruct((heads * HEAD_SIZE, OWN), BF16),
        ],
        scratch_shapes=[
            pltpu.VMEM((SEQ, OWN), F32),
            pltpu.VMEM((2, SEQ, HEAD_SIZE), BF16),
            pltpu.VMEM((2, HEAD_SIZE, SEQ), BF16),
        ],
        compiler_params=pltpu.CompilerParams(vmem_limit_bytes=40 * 1024 * 1024),
        cost_estimate=pl.CostEstimate(flops=20_000_000_000, bytes_accessed=8_000_000, transcendentals=0),
        name="attend",
    )(row, q, cosine, sine, start, own_kv, other_kv)


def attend_back_kernel(
    row_ref,
    qt_ref,
    do_ref,
    o_ref,
    lse_ref,
    cos_ref,
    sin_ref,
    start_ref,
    own_ref,
    other_ref,
    dq_ref,
    dk_ref,
    dv_ref,
    bias,
    keys,
    keys_t,
    values,
):
    step = pl.program_id(0)
    kv = step // 4
    row = row_ref[0]

    @pl.when(step == 0)
    def _():
        chunk_bias(start_ref, bias, row)

        def put(i, block):
            span = slice(i * CHUNK, (i + 1) * CHUNK)
            for h in range(2):
                keys[h, span, :] = block[:, h * HEAD_SIZE : (h + 1) * HEAD_SIZE]
                values[h, span, :] = block[:, PAIR + h * HEAD_SIZE : PAIR + (h + 1) * HEAD_SIZE]
            turned = jnp.transpose(block[:, :PAIR].astype(F32)).astype(BF16)
            for h in range(2):
                keys_t[h, :, span] = turned[h * HEAD_SIZE : (h + 1) * HEAD_SIZE]

        place_keys(own_ref, other_ref, row, put)

    @pl.when(step % 4 == 0)
    def _():
        dk_ref[...] = jnp.zeros_like(dk_ref)
        dv_ref[...] = jnp.zeros_like(dv_ref)

    grad = do_ref[...].astype(F32)
    grad_t = jnp.transpose(grad)
    mixed_t = jnp.transpose(grad * o_ref[...].astype(F32))
    cosine, sine = cos_ref[...], sin_ref[...]

    def unit(c, blocks):
        lanes = slice(c * CHUNK, (c + 1) * CHUNK)
        count = blocks * CHUNK
        outs = []
        for h in range(2):
            rows = slice(h * HEAD_SIZE, (h + 1) * HEAD_SIZE)
            query = qt_ref[rows, lanes]
            d_head = grad_t[rows, lanes].astype(BF16)
            delta = jnp.sum(mixed_t[rows, lanes], axis=0, keepdims=True)
            scores = dot_plain(keys[kv, :count, :], query) + bias[:count, lanes]
            probs = jnp.exp(scores - lse_ref[0, h : h + 1, lanes])
            dv_ref[0, :count, :] += dot_right(probs.astype(BF16), d_head)
            d_probs = dot_plain(values[kv, :count, :], d_head)
            d_raw = (probs * (d_probs - delta)).astype(BF16)
            d_query = dot_plain(keys_t[kv, :, :count], d_raw) * SCALE
            dk_ref[0, :count, :] += dot_right(d_raw, query)
            a, b = d_query[:HALF], d_query[HALF:]
            co, si = cosine[:, lanes], sine[:, lanes]
            outs.append(a * co + b * si)
            outs.append(b * co - a * si)
        dq_ref[lanes, :] = jnp.transpose(jnp.concatenate(outs, axis=0)).astype(BF16)

    @pl.when(row == 0)
    def _():
        unit(0, 1)
        unit(1, 4)

    @pl.when(row == 1)
    def _():
        unit(0, 2)
        unit(1, 3)


def attend_back(row, qt, d_o, o, lse, cosine, sine, start, own_kv, other_kv):
    heads = qt.shape[0] // HEAD_SIZE
    pairs = heads // 2
    whole = lambda shape: pl.BlockSpec(shape, lambda i: (0,) * len(shape))
    return pl.pallas_call(
        attend_back_kernel,
        grid=(pairs,),
        in_specs=[
            pl.BlockSpec(memory_space=pltpu.SMEM),
            pl.BlockSpec((PAIR, OWN), lambda i: (i, 0)),
            pl.BlockSpec((OWN, PAIR), lambda i: (0, i)),
            pl.BlockSpec((OWN, PAIR), lambda i: (0, i)),
            pl.BlockSpec((1, 2, OWN), lambda i: (i, 0, 0)),
            whole((HALF, OWN)),
            whole((HALF, OWN)),
            whole((1, OWN)),
            whole((OWN, 2 * PAIR)),
            whole((OWN, 2 * PAIR)),
        ],
        out_specs=[
            pl.BlockSpec((OWN, PAIR), lambda i: (0, i)),
            pl.BlockSpec((1, SEQ, HEAD_SIZE), lambda i: (i // 4, 0, 0)),
            pl.BlockSpec((1, SEQ, HEAD_SIZE), lambda i: (i // 4, 0, 0)),
        ],
        out_shape=[
            jax.ShapeDtypeStruct((OWN, heads * HEAD_SIZE), BF16),
            jax.ShapeDtypeStruct((2, SEQ, HEAD_SIZE), F32),
            jax.ShapeDtypeStruct((2, SEQ, HEAD_SIZE), F32),
        ],
        scratch_shapes=[
            pltpu.VMEM((SEQ, OWN), F32),
            pltpu.VMEM((2, SEQ, HEAD_SIZE), BF16),
            pltpu.VMEM((2, HEAD_SIZE, SEQ), BF16),
            pltpu.VMEM((2, SEQ, HEAD_SIZE), BF16),
        ],
        compiler_params=pltpu.CompilerParams(vmem_limit_bytes=40 * 1024 * 1024),
        cost_estimate=pl.CostEstimate(flops=40_000_000_000, bytes_accessed=8_000_000, transcendentals=0),
        name="attend_back",
    )(row, qt, d_o, o, lse, cosine, sine, start, own_kv, other_kv)


def hidden_units_kernel(
    xm_ref, xo_ref, cm_ref, co_ref, gm_ref, go_ref, um_ref, uo_ref, dm_ref, do_ref, act_ref, dg_ref, du_ref
):
    gate = dot_plain(xm_ref[...], gm_ref[...]) + dot_plain(xo_ref[...], go_ref[...])
    up = dot_plain(xm_ref[...], um_ref[...]) + dot_plain(xo_ref[...], uo_ref[...])
    d_act = dot_right(cm_ref[...], dm_ref[...]) + dot_right(co_ref[...], do_ref[...])
    sigma = jax.nn.sigmoid(gate)
    swish = gate * sigma
    act_ref[...] = (swish * up).astype(BF16)
    dg_ref[...] = (d_act * up * (sigma * (1.0 + gate * (1.0 - sigma)))).astype(BF16)
    du_ref[...] = (d_act * swish).astype(BF16)


def hidden_units(xm, xo, cm, co, gm, go, um, uo, dm, do):
    rows, depth = xm.shape
    wide = gm.shape[1]
    tile = 256
    full = pl.BlockSpec((rows, depth), lambda i: (0, 0))
    column = pl.BlockSpec((depth, tile), lambda i: (0, i))
    line = pl.BlockSpec((tile, depth), lambda i: (i, 0))
    out = pl.BlockSpec((rows, tile), lambda i: (0, i))
    return pl.pallas_call(
        hidden_units_kernel,
        grid=(wide // tile,),
        in_specs=[full] * 4 + [column] * 4 + [line] * 2,
        out_specs=[out] * 3,
        out_shape=[jax.ShapeDtypeStruct((rows, wide), BF16)] * 3,
        compiler_params=pltpu.CompilerParams(vmem_limit_bytes=48 * 1024 * 1024),
        cost_estimate=pl.CostEstimate(
            flops=12 * rows * depth * wide, bytes_accessed=12 * depth * wide, transcendentals=0
        ),
        name="hidden_units",
    )(xm, xo, cm, co, gm, go, um, uo, dm, do)


def input_grad_kernel(dg_ref, du_ref, g_ref, u_ref, out_ref):
    out_ref[...] = (dot_right(dg_ref[...], g_ref[...]) + dot_right(du_ref[...], u_ref[...])).astype(BF16)


def input_grad(dg, du, g, u):
    rows, wide = dg.shape
    depth = g.shape[0]
    tile = 256
    full = pl.BlockSpec((rows, wide), lambda i: (0, 0))
    line = pl.BlockSpec((tile, wide), lambda i: (i, 0))
    return pl.pallas_call(
        input_grad_kernel,
        grid=(depth // tile,),
        in_specs=[full] * 2 + [line] * 2,
        out_specs=pl.BlockSpec((rows, tile), lambda i: (0, i)),
        out_shape=jax.ShapeDtypeStruct((rows, depth), BF16),
        compiler_params=pltpu.CompilerParams(vmem_limit_bytes=48 * 1024 * 1024),
        cost_estimate=pl.CostEstimate(flops=4 * rows * depth * wide, bytes_accessed=4 * depth * wide, transcendentals=0),
        name="input_grad",
    )(dg, du, g, u)


class Halving:
    def __init__(self, left, right, axis, order, flip):
        self.left, self.right, self.axis, self.order, self.flip = left, right, axis, list(order), flip
        self.at = 0

    def part(self, upper):
        if not self.order:
            return dot_left(self.left, self.right)
        if self.axis == 0:
            return dot_left(half_of(self.left, 1, upper), self.right)
        return dot_left(self.left, half_of(self.right, 1, upper))

    def begin(self):
        self.send = self.part(True).astype(BF16)
        return self.send

    def stay(self):
        self.keep = self.part(False)
        return self.keep

    def go(self):
        if self.at < len(self.order):
            self.came = self.flip(self.send, self.order[self.at])
        else:
            self.came = self.send
        return self.came

    def add(self):
        if self.at < len(self.order):
            self.total = self.keep + self.came.astype(F32)
            self.at += 1
            if self.at < len(self.order):
                self.send = half_of(self.total, self.axis, True).astype(BF16)
                self.keep = half_of(self.total, self.axis, False)
        elif not self.order:
            self.total = self.keep

    def rest(self):
        self.add()
        while self.at < len(self.order):
            self.go()
            self.add()
        return self.total


def half_of(value, axis, upper):
    size = value.shape[axis] // 2
    return lax.slice_in_dim(value, size if upper else 0, 2 * size if upper else size, axis=axis)


def tie(*values):
    return lax.optimization_barrier(values)


def shards(
    count,
    tokens,
    segment_ids,
    cotangent,
    g_attn,
    query_weight,
    key_weight,
    value_weight,
    w_o,
    g_mlp,
    w_gate,
    w_up,
    w_down,
):
    row = lax.axis_index("row")
    dp = lax.axis_index("dp")
    bits = count.bit_length() - 1

    def swap(value):
        return lax.ppermute(value, "row", [(0, 1), (1, 0)])

    def cross(value):
        return lax.ppermute(value, "col", [(0, 1), (1, 0)])

    def flip(value, bit):
        return lax.ppermute(value, "dp", [(i, i ^ (1 << bit)) for i in range(count)])

    def order_of(first):
        return ([first] + [b for b in range(bits) if b != first]) if bits else []

    def relative(value, order):
        width = value.shape[1] // count
        blocks = []
        for place in range(count):
            differs = 0
            for at, bit in enumerate(order):
                differs |= ((place >> (len(order) - 1 - at)) & 1) << bit
            blocks.append(lax.dynamic_slice_in_dim(value, (dp ^ differs) * width, width, axis=1))
        return jnp.concatenate(blocks, axis=1)

    x_m = own_rows(tokens, row)
    x_o = swap(other_rows(tokens, row))
    wkv = jnp.concatenate([key_weight, value_weight], axis=1)
    wkv_o = swap(wkv)
    wq_o = swap(query_weight)
    gains = jnp.stack([g_attn, g_mlp])
    gains_o = swap(gains)
    w_o_x = cross(w_o)
    x_m, x_o = x_m.astype(F32), x_o.astype(F32)
    square = jnp.sum(x_m * x_m, axis=-1, keepdims=True) + jnp.sum(x_o * x_o, axis=-1, keepdims=True)
    inv_one = lax.rsqrt(square / MODEL_WIDTH + EPS)
    xn_m = (x_m * inv_one * gains[0]).astype(BF16)
    xn_o = (x_o * inv_one * gains_o[0]).astype(BF16)

    start = jnp.sum((segment_ids[None, :] < segment_ids[:, None]).astype(jnp.int32), axis=1)
    index = lax.iota(jnp.int32, SEQ)
    start_own = own_rows(start, row)
    places = own_rows(index, row) - start_own
    freq = jnp.exp(jnp.arange(HALF, dtype=F32) * (-2.0 * math.log(THETA) / HEAD_SIZE))
    turn_t = freq[:, None] * places.astype(F32)[None, :]
    cosine_t, sine_t = jnp.cos(turn_t), jnp.sin(turn_t)
    cosine, sine = cosine_t.T[:, None, :], sine_t.T[:, None, :]

    kv = dot_plain(xn_m, wkv) + dot_plain(xn_o, wkv_o)
    narrow = key_weight.shape[1]
    wide = query_weight.shape[1]
    kp = kv[:, :narrow].reshape(OWN, -1, HEAD_SIZE)
    first, second = kp[..., :HALF], kp[..., HALF:]
    key = jnp.concatenate([first * cosine - second * sine, second * cosine + first * sine], axis=-1)
    own_kv = jnp.concatenate([key.reshape(OWN, narrow), kv[:, narrow:]], axis=1).astype(BF16)
    other_kv = swap(own_kv)
    xn_m, xn_o, own_kv = tie(xn_m, xn_o, own_kv)
    q = dot_plain(xn_m, query_weight) + dot_plain(xn_o, wq_o)

    cotangent, w_gate, w_up, w_down, w_o, xn_o = tie(cotangent, w_gate, w_up, w_down, w_o, xn_o)
    w_o_o = swap(w_o)
    wg_o = swap(w_gate)
    wu_o = swap(w_up)
    c_m = own_rows(cotangent, row)
    c_t = other_rows(cotangent, row)
    c_o = swap(c_t)
    wd_o = swap(w_down)
    xn_t = swap(xn_o)

    row_arg = row.astype(jnp.int32).reshape(1)
    start_arg = start_own.reshape(1, OWN)
    o, lse, qt = attend(row_arg, q, cosine_t, sine_t, start_arg, own_kv, other_kv)
    o, w_o_x = tie(o, w_o_x)
    w_o_xo = swap(w_o_x)

    o_x = cross(o)
    o_t = swap(o)
    near_m, near_o = dot_plain(o, w_o), dot_plain(o, w_o_o)
    near_m, near_o, o_x = tie(near_m, near_o, o_x)
    hidden_m = x_m + (near_m + dot_plain(o_x, w_o_x))
    hidden_o = x_o + (near_o + dot_plain(o_x, w_o_xo))
    square = jnp.sum(hidden_m * hidden_m, axis=-1, keepdims=True) + jnp.sum(
        hidden_o * hidden_o, axis=-1, keepdims=True
    )
    inv_two = lax.rsqrt(square / MODEL_WIDTH + EPS)
    unit_m, unit_o = hidden_m * inv_two, hidden_o * inv_two
    xn2_m = (unit_m * gains[1]).astype(BF16)
    xn2_o = (unit_o * gains_o[1]).astype(BF16)

    order_y, order_z = order_of(0), order_of(min(1, max(bits - 1, 0)))
    both = lambda own, other: jnp.concatenate([own, other], axis=0)
    xn2_all = both(xn2_m, swap(xn2_o))
    xn2_y, xn2_z = relative(xn2_all, order_y), relative(xn2_all, order_z)
    c_y = relative(both(c_m, c_t), order_y)
    act, d_gate, d_up = hidden_units(xn2_m, xn2_o, c_m, c_o, w_gate, wg_o, w_up, wu_o, w_down, wd_o)
    act_t, d_up_t, d_gate_t = swap(act), swap(d_up), swap(d_gate)
    part_m = input_grad(d_gate, d_up, w_gate, w_up)
    came_m = cross(part_m)
    act_t, d_up_t, part_m = tie(act_t, d_up_t, part_m)
    down = Halving(both(act, act_t), c_y, 1, order_y, flip)
    upper = Halving(xn2_z, both(d_up, d_up_t), 0, order_z, flip)
    gater = Halving(xn2_y, both(d_gate, d_gate_t), 0, order_y, flip)
    down.begin()
    down.go()
    upper.begin()
    upper.go()
    down.send, upper.send, d_gate_late = tie(down.send, upper.send, d_gate)
    part_o = input_grad(d_gate_late, d_up, wg_o, wu_o)
    came_o = cross(part_o)
    down.left, upper.left, part_o = tie(down.left, upper.left, part_o)
    down.stay()
    upper.stay()
    gater.begin()
    gater.stay()
    mix_m = dot_plain(act, w_down).astype(BF16)
    mix_o = dot_plain(act, wd_o).astype(BF16)

    came_m, came_o, down.keep, upper.keep, gater.send, gater.keep, mix_m, mix_o = tie(
        came_m, came_o, down.keep, upper.keep, gater.send, gater.keep, mix_m, mix_o
    )
    d_xn2_m = part_m.astype(F32) + came_m.astype(F32)
    d_xn2_o = part_o.astype(F32) + came_o.astype(F32)
    e_m, e_o = d_xn2_m * gains[1], d_xn2_o * gains_o[1]
    mean = (
        jnp.sum(e_m * unit_m, axis=-1, keepdims=True) + jnp.sum(e_o * unit_o, axis=-1, keepdims=True)
    ) / MODEL_WIDTH
    gg_mlp_m = jnp.sum(d_xn2_m * unit_m, axis=0)
    gg_mlp_o = jnp.sum(d_xn2_o * unit_o, axis=0)
    d_hid_m = c_m.astype(F32) + inv_two * (e_m - unit_m * mean)
    d_hid_o = c_o.astype(F32) + inv_two * (e_o - unit_o * mean)
    dh_m, dh_o = d_hid_m.astype(BF16), d_hid_o.astype(BF16)
    dh_t = swap(dh_o)
    d_o = (dot_right(dh_m, w_o) + dot_right(dh_o, w_o_o)).astype(BF16)

    d_q, d_k, d_v = attend_back(row_arg, qt, d_o, o, lse, cosine_t, sine_t, start_arg, own_kv, other_kv)
    d_kv = jnp.concatenate([d_k[0], d_k[1], d_v[0], d_v[1]], axis=1)
    d_kv_t = swap(other_rows(d_kv, row))
    d_kv_own = own_rows(d_kv, row)
    d_kv_own, down.came, upper.came, gater.send = tie(d_kv_own, down.came, upper.came, gater.send)
    gater.go()
    down.add()
    down.go()
    upper.add()
    upper.go()
    d_kv_t, down.send, down.keep, upper.send, upper.keep = tie(
        d_kv_t, down.send, down.keep, upper.send, upper.keep
    )
    d_kv = d_kv_own + d_kv_t
    d_key = d_kv[:, :narrow].reshape(OWN, -1, HEAD_SIZE)
    first, second = d_key[..., :HALF], d_key[..., HALF:]
    d_key = jnp.concatenate([first * cosine + second * sine, second * cosine - first * sine], axis=-1)
    d_kv = jnp.concatenate([d_key.reshape(OWN, narrow).astype(BF16), d_kv[:, narrow:].astype(BF16)], axis=1)
    d_qkv = jnp.concatenate([d_q, d_kv], axis=1)
    part_m = (dot_right(d_q, query_weight) + dot_right(d_kv, wkv)).astype(BF16)
    came_m = cross(part_m)
    part_o = (dot_right(d_q, wq_o) + dot_right(d_kv, wkv_o)).astype(BF16)
    came_o = cross(part_o)
    d_qkv_t = swap(d_qkv)
    d_qkv_t, dh_t, part_o = tie(d_qkv_t, dh_t, part_o)
    outer = Halving(both(o, o_t), relative(both(dh_m, dh_t), order_y), 1, order_y, flip)
    inner = Halving(relative(both(xn_m, xn_t), order_y), both(d_qkv, d_qkv_t), 0, order_y, flip)
    inner.begin()
    inner.go()
    outer.begin()
    outer.go()
    inner.stay()
    outer.stay()

    came_m, came_o, inner.keep, outer.keep, gater.came, mix_m, mix_o = tie(
        came_m, came_o, inner.keep, outer.keep, gater.came, mix_m, mix_o
    )
    gater.add()
    gater.go()
    mix_cm, mix_co = cross(mix_m), cross(mix_o)
    d_xn_m = part_m.astype(F32) + came_m.astype(F32)
    d_xn_o = part_o.astype(F32) + came_o.astype(F32)
    unit_m, unit_o = x_m * inv_one, x_o * inv_one
    e_m, e_o = d_xn_m * gains[0], d_xn_o * gains_o[0]
    mean = (
        jnp.sum(e_m * unit_m, axis=-1, keepdims=True) + jnp.sum(e_o * unit_o, axis=-1, keepdims=True)
    ) / MODEL_WIDTH
    gg_attn_m = jnp.sum(d_xn_m * unit_m, axis=0)
    gg_attn_o = jnp.sum(d_xn_o * unit_o, axis=0)
    d_tok_m = d_hid_m + inv_one * (e_m - unit_m * mean)
    d_tok_o = d_hid_o + inv_one * (e_o - unit_o * mean)
    d_tokens = merge_rows(d_tok_m, swap(d_tok_o), row)

    out_m = (hidden_m + (mix_m.astype(F32) + mix_cm.astype(F32))).astype(BF16)
    out_o = (hidden_o + (mix_o.astype(F32) + mix_co.astype(F32))).astype(BF16)
    mixed = merge_rows(out_m, swap(out_o), row)

    gg = jnp.stack([gg_attn_m, gg_mlp_m]) + swap(jnp.stack([gg_attn_o, gg_mlp_o]))
    gg = relative(gg, order_y)
    for bit in order_y:
        gg = half_of(gg, 1, False) + flip(half_of(gg, 1, True), bit)

    gw_down, gw_up, gw_gate, gw_o, gw_qkv = (h.rest() for h in (down, upper, gater, outer, inner))
    return (
        mixed,
        d_tokens,
        gg[0],
        gw_qkv[:, :wide],
        gw_qkv[:, wide : wide + narrow],
        gw_qkv[:, wide + narrow :],
        gw_o,
        gg[1],
        gw_gate,
        gw_up,
        gw_down,
    )


def solution(mesh):
    count = mesh.shape["dp"]
    placed = (
        P("dp", "row"),
        P("dp"),
        P("dp", "row"),
        P("row"),
        P("row", "col"),
        P("row", "col"),
        P("row", "col"),
        P("col", "row"),
        P("row"),
        P("row", "col"),
        P("row", "col"),
        P("col", "row"),
    )

    def body(*args):
        return shards(count, *args)

    return jax.shard_map(
        body,
        mesh=mesh,
        in_specs=placed,
        out_specs=(
            P("dp", "row"),
            P("dp", "row"),
            P(("row", "dp")),
            P(("row", "dp"), "col"),
            P(("row", "dp"), "col"),
            P(("row", "dp"), "col"),
            P("col", ("row", "dp")),
            P(("row", "dp")),
            P(("row", "dp"), "col"),
            P(("row", "dp"), "col"),
            P("col", ("row", "dp")),
        ),
        check_vma=False,
    )
```

```python
import functools
import math

import jax
import jax.numpy as jnp
from jax import lax
from jax.experimental import pallas as pl
from jax.experimental.pallas import tpu as pltpu
from jax.sharding import PartitionSpec as P

MODEL_WIDTH = 2048
QUERY_HEADS = 32
KEY_VALUE_HEADS = 4
HEAD_SIZE = 64
SEQ = 1024

EPS = 1e-05
THETA = 10000.0
HALF = HEAD_SIZE // 2
CHUNK = SEQ // 4
OWN = SEQ // 2
PAIR = 2 * HEAD_SIZE
SCALE = HEAD_SIZE ** (-0.5)
NEG = -1e30
F32 = jnp.float32
BF16 = jnp.bfloat16


def dot_plain(left, right):
    return jnp.dot(left, right, preferred_element_type=F32)


def dot_right(left, right):
    return lax.dot_general(left, right, (((1,), (1,)), ((), ())), preferred_element_type=F32)


def dot_left(left, right):
    return lax.dot_general(left, right, (((0,), (0,)), ((), ())), preferred_element_type=F32)


def own_rows(value, row):
    a, b, c, d = (value[i * CHUNK : (i + 1) * CHUNK] for i in range(4))
    return jnp.concatenate([jnp.where(row == 0, a, b), jnp.where(row == 0, d, c)], axis=0)


def other_rows(value, row):
    a, b, c, d = (value[i * CHUNK : (i + 1) * CHUNK] for i in range(4))
    return jnp.concatenate([jnp.where(row == 0, b, a), jnp.where(row == 0, c, d)], axis=0)


def merge_rows(own, other, row):
    a, b = own[:CHUNK], own[CHUNK:]
    c, d = other[:CHUNK], other[CHUNK:]
    return jnp.concatenate(
        [
            jnp.where(row == 0, a, c),
            jnp.where(row == 0, c, a),
            jnp.where(row == 0, d, b),
            jnp.where(row == 0, b, d),
        ],
        axis=0,
    )


def chunk_bias(start_ref, bias, row):
    for c in range(2):
        place = jnp.where(row == 0, 3 * c, 1 + c) * CHUNK
        lanes = slice(c * CHUNK, (c + 1) * CHUNK)
        keys = lax.broadcasted_iota(jnp.int32, (SEQ, CHUNK), 0)
        queries = lax.broadcasted_iota(jnp.int32, (SEQ, CHUNK), 1) + place
        allowed = (keys >= start_ref[:, lanes]) & (keys <= queries)
        bias[:, lanes] = jnp.where(allowed, 0.0, NEG)


def place_keys(own_ref, other_ref, row, put):
    @pl.when(row == 0)
    def _():
        for i, (ref, half) in enumerate(((own_ref, 0), (other_ref, 0), (other_ref, 1), (own_ref, 1))):
            put(i, ref[half * CHUNK : (half + 1) * CHUNK, :])

    @pl.when(row == 1)
    def _():
        for i, (ref, half) in enumerate(((other_ref, 0), (own_ref, 0), (own_ref, 1), (other_ref, 1))):
            put(i, ref[half * CHUNK : (half + 1) * CHUNK, :])


def attend_kernel(
    group, row_ref, q_ref, cos_ref, sin_ref, start_ref, own_ref, other_ref, o_ref, lse_ref, qt_ref, bias, keys, values_t
):
    step = pl.program_id(0)
    row = row_ref[0]

    @pl.when(step == 0)
    def _():
        chunk_bias(start_ref, bias, row)

        def put(i, block):
            span = slice(i * CHUNK, (i + 1) * CHUNK)
            lanes = slice(group * HEAD_SIZE, (group + 1) * HEAD_SIZE)
            keys[span, :] = block[:, lanes]
            values_t[:, span] = jnp.transpose(block[:, PAIR:].astype(F32)).astype(BF16)[lanes]

        place_keys(own_ref, other_ref, row, put)

    turned = jnp.transpose(q_ref[...])
    cosine, sine = cos_ref[...], sin_ref[...]
    for h in range(2):
        a = turned[h * HEAD_SIZE : h * HEAD_SIZE + HALF]
        b = turned[h * HEAD_SIZE + HALF : (h + 1) * HEAD_SIZE]
        rot = jnp.concatenate([a * cosine - b * sine, b * cosine + a * sine], axis=0)
        qt_ref[h * HEAD_SIZE : (h + 1) * HEAD_SIZE, :] = (rot * SCALE).astype(BF16)

    def unit(c, blocks):
        lanes = slice(c * CHUNK, (c + 1) * CHUNK)
        count = blocks * CHUNK
        outs, sums = [], []
        for h in range(2):
            query = qt_ref[h * HEAD_SIZE : (h + 1) * HEAD_SIZE, lanes]
            scores = dot_plain(keys[:count, :], query) + bias[:count, lanes]
            top = jnp.max(scores, axis=0, keepdims=True)
            expo = jnp.exp(scores - top)
            total = jnp.sum(expo, axis=0, keepdims=True)
            head = dot_plain(values_t[:, :count], expo.astype(BF16))
            outs.append(head * (1.0 / total))
            sums.append(top + jnp.log(total))
        o_ref[lanes, :] = jnp.transpose(jnp.concatenate(outs, axis=0)).astype(BF16)
        lse_ref[0, :, lanes] = jnp.concatenate(sums, axis=0)

    @pl.when(row == 0)
    def _():
        unit(0, 1)
        unit(1, 4)

    @pl.when(row == 1)
    def _():
        unit(0, 2)
        unit(1, 3)


def attend(group, row, q, cosine, sine, start, own_kv, other_kv):
    pairs = q.shape[1] // (2 * PAIR)
    whole = lambda shape: pl.BlockSpec(shape, lambda i: (0,) * len(shape))
    return pl.pallas_call(
        functools.partial(attend_kernel, group),
        grid=(pairs,),
        in_specs=[
            pl.BlockSpec(memory_space=pltpu.SMEM),
            pl.BlockSpec((OWN, PAIR), lambda i: (0, i + group * pairs)),
            whole((HALF, OWN)),
            whole((HALF, OWN)),
            whole((1, OWN)),
            whole((OWN, 2 * PAIR)),
            whole((OWN, 2 * PAIR)),
        ],
        out_specs=[
            pl.BlockSpec((OWN, PAIR), lambda i: (0, i)),
            pl.BlockSpec((1, 2, OWN), lambda i: (i, 0, 0)),
            pl.BlockSpec((PAIR, OWN), lambda i: (i, 0)),
        ],
        out_shape=[
            jax.ShapeDtypeStruct((OWN, pairs * PAIR), BF16),
            jax.ShapeDtypeStruct((pairs, 2, OWN), F32),
            jax.ShapeDtypeStruct((pairs * PAIR, OWN), BF16),
        ],
        scratch_shapes=[
            pltpu.VMEM((SEQ, OWN), F32),
            pltpu.VMEM((SEQ, HEAD_SIZE), BF16),
            pltpu.VMEM((HEAD_SIZE, SEQ), BF16),
        ],
        compiler_params=pltpu.CompilerParams(vmem_limit_bytes=40 * 1024 * 1024),
        cost_estimate=pl.CostEstimate(flops=1000, bytes_accessed=1000, transcendentals=0),
        name="attend",
    )(row, q, cosine, sine, start, own_kv, other_kv)


def attend_back_kernel(
    row_ref,
    qt_ref,
    do_ref,
    o_ref,
    lse_ref,
    cos_ref,
    sin_ref,
    start_ref,
    own_ref,
    other_ref,
    dq_ref,
    dk_ref,
    dv_ref,
    bias,
    keys,
    keys_t,
    values,
):
    step = pl.program_id(0)
    kv = step // 4
    row = row_ref[0]

    @pl.when(step == 0)
    def _():
        chunk_bias(start_ref, bias, row)

        def put(i, block):
            span = slice(i * CHUNK, (i + 1) * CHUNK)
            for h in range(2):
                keys[h, span, :] = block[:, h * HEAD_SIZE : (h + 1) * HEAD_SIZE]
                values[h, span, :] = block[:, PAIR + h * HEAD_SIZE : PAIR + (h + 1) * HEAD_SIZE]
            turned = jnp.transpose(block[:, :PAIR].astype(F32)).astype(BF16)
            for h in range(2):
                keys_t[h, :, span] = turned[h * HEAD_SIZE : (h + 1) * HEAD_SIZE]

        place_keys(own_ref, other_ref, row, put)

    @pl.when(step % 4 == 0)
    def _():
        dk_ref[...] = jnp.zeros_like(dk_ref)
        dv_ref[...] = jnp.zeros_like(dv_ref)

    grad = do_ref[...].astype(F32)
    grad_t = jnp.transpose(grad)
    mixed_t = jnp.transpose(grad * o_ref[...].astype(F32))
    cosine, sine = cos_ref[...], sin_ref[...]

    def unit(c, blocks):
        lanes = slice(c * CHUNK, (c + 1) * CHUNK)
        count = blocks * CHUNK
        outs = []
        for h in range(2):
            rows = slice(h * HEAD_SIZE, (h + 1) * HEAD_SIZE)
            query = qt_ref[rows, lanes]
            d_head = grad_t[rows, lanes].astype(BF16)
            delta = jnp.sum(mixed_t[rows, lanes], axis=0, keepdims=True)
            scores = dot_plain(keys[kv, :count, :], query) + bias[:count, lanes]
            probs = jnp.exp(scores - lse_ref[0, h : h + 1, lanes])
            dv_ref[0, :count, :] += dot_right(probs.astype(BF16), d_head)
            d_probs = dot_plain(values[kv, :count, :], d_head)
            d_raw = (probs * (d_probs - delta)).astype(BF16)
            d_query = dot_plain(keys_t[kv, :, :count], d_raw) * SCALE
            dk_ref[0, :count, :] += dot_right(d_raw, query)
            a, b = d_query[:HALF], d_query[HALF:]
            co, si = cosine[:, lanes], sine[:, lanes]
            outs.append(a * co + b * si)
            outs.append(b * co - a * si)
        dq_ref[lanes, :] = jnp.transpose(jnp.concatenate(outs, axis=0)).astype(BF16)

    @pl.when(row == 0)
    def _():
        unit(0, 1)
        unit(1, 4)

    @pl.when(row == 1)
    def _():
        unit(0, 2)
        unit(1, 3)


def attend_back(row, qt, d_o, o, lse, cosine, sine, start, own_kv, other_kv):
    heads = qt.shape[0] // HEAD_SIZE
    pairs = heads // 2
    whole = lambda shape: pl.BlockSpec(shape, lambda i: (0,) * len(shape))
    return pl.pallas_call(
        attend_back_kernel,
        grid=(pairs,),
        in_specs=[
            pl.BlockSpec(memory_space=pltpu.SMEM),
            pl.BlockSpec((PAIR, OWN), lambda i: (i, 0)),
            pl.BlockSpec((OWN, PAIR), lambda i: (0, i)),
            pl.BlockSpec((OWN, PAIR), lambda i: (0, i)),
            pl.BlockSpec((1, 2, OWN), lambda i: (i, 0, 0)),
            whole((HALF, OWN)),
            whole((HALF, OWN)),
            whole((1, OWN)),
            whole((OWN, 2 * PAIR)),
            whole((OWN, 2 * PAIR)),
        ],
        out_specs=[
            pl.BlockSpec((OWN, PAIR), lambda i: (0, i)),
            pl.BlockSpec((1, SEQ, HEAD_SIZE), lambda i: (i // 4, 0, 0)),
            pl.BlockSpec((1, SEQ, HEAD_SIZE), lambda i: (i // 4, 0, 0)),
        ],
        out_shape=[
            jax.ShapeDtypeStruct((OWN, heads * HEAD_SIZE), BF16),
            jax.ShapeDtypeStruct((2, SEQ, HEAD_SIZE), F32),
            jax.ShapeDtypeStruct((2, SEQ, HEAD_SIZE), F32),
        ],
        scratch_shapes=[
            pltpu.VMEM((SEQ, OWN), F32),
            pltpu.VMEM((2, SEQ, HEAD_SIZE), BF16),
            pltpu.VMEM((2, HEAD_SIZE, SEQ), BF16),
            pltpu.VMEM((2, SEQ, HEAD_SIZE), BF16),
        ],
        compiler_params=pltpu.CompilerParams(vmem_limit_bytes=40 * 1024 * 1024),
        cost_estimate=pl.CostEstimate(flops=1000, bytes_accessed=1000, transcendentals=0),
        name="attend_back",
    )(row, qt, d_o, o, lse, cosine, sine, start, own_kv, other_kv)


def hidden_units_kernel(
    xm_ref, xo_ref, cm_ref, co_ref, gm_ref, go_ref, um_ref, uo_ref, dm_ref, do_ref, out_ref
):
    gate = dot_plain(xm_ref[...], gm_ref[...]) + dot_plain(xo_ref[...], go_ref[...])
    up = dot_plain(xm_ref[...], um_ref[...]) + dot_plain(xo_ref[...], uo_ref[...])
    d_act = dot_right(cm_ref[...], dm_ref[...]) + dot_right(co_ref[...], do_ref[...])
    sigma = jax.nn.sigmoid(gate)
    swish = gate * sigma
    out_ref[0] = (swish * up).astype(BF16)
    out_ref[1] = (d_act * up * (sigma * (1.0 + gate * (1.0 - sigma)))).astype(BF16)
    out_ref[2] = (d_act * swish).astype(BF16)


def hidden_units(first, tiles, xm, xo, cm, co, gm, go, um, uo, dm, do):
    rows, depth = xm.shape
    tile = 256
    wide = tiles * tile
    full = pl.BlockSpec((rows, depth), lambda i: (0, 0))
    column = pl.BlockSpec((depth, tile), lambda i: (0, i + first))
    line = pl.BlockSpec((tile, depth), lambda i: (i + first, 0))
    out = pl.BlockSpec((3, rows, tile), lambda i: (0, 0, i))
    return pl.pallas_call(
        hidden_units_kernel,
        grid=(tiles,),
        in_specs=[full] * 4 + [column] * 4 + [line] * 2,
        out_specs=out,
        out_shape=jax.ShapeDtypeStruct((3, rows, wide), BF16),
        compiler_params=pltpu.CompilerParams(vmem_limit_bytes=48 * 1024 * 1024),
        cost_estimate=pl.CostEstimate(flops=1000, bytes_accessed=1000, transcendentals=0),
        name="hidden_units",
    )(xm, xo, cm, co, gm, go, um, uo, dm, do)


def input_grad_kernel(a_ref, b_ref, gm_ref, um_ref, go_ref, uo_ref, out_ref):
    cut = a_ref.shape[2]

    def fill(g_ref, u_ref):
        total = dot_right(a_ref[1], g_ref[:, :cut]) + dot_right(b_ref[1], g_ref[:, cut:])
        total += dot_right(a_ref[2], u_ref[:, :cut]) + dot_right(b_ref[2], u_ref[:, cut:])
        out_ref[...] = total.astype(BF16)

    step, half = pl.program_id(0), pl.num_programs(0) // 2
    pl.when(step < half)(lambda: fill(gm_ref, um_ref))
    pl.when(step >= half)(lambda: fill(go_ref, uo_ref))


def input_grad(a, b, gm, um, go, uo):
    rows = a.shape[1]
    depth, wide = gm.shape
    tile = 256
    tiles = depth // tile
    full = lambda value: pl.BlockSpec(value.shape, lambda i: (0, 0, 0))
    line_m = pl.BlockSpec((tile, wide), lambda i: (jnp.minimum(i, tiles - 1), 0))
    line_o = pl.BlockSpec((tile, wide), lambda i: (jnp.maximum(i - tiles, 0), 0))
    return pl.pallas_call(
        input_grad_kernel,
        grid=(2 * tiles,),
        in_specs=[full(a), full(b), line_m, line_m, line_o, line_o],
        out_specs=pl.BlockSpec((rows, tile), lambda i: (0, i)),
        out_shape=jax.ShapeDtypeStruct((rows, 2 * depth), BF16),
        compiler_params=pltpu.CompilerParams(vmem_limit_bytes=48 * 1024 * 1024),
        cost_estimate=pl.CostEstimate(flops=1000, bytes_accessed=1000, transcendentals=0),
        name="input_grad",
    )(a, b, gm, um, go, uo)


class Halving:
    def __init__(self, pairs, order, flip):
        self.pairs, self.order, self.flip, self.at, self.open = pairs, list(order), flip, 0, False

    def part(self, upper):
        parts = [dot_left(half_of(a, upper, 1) if self.order else a, b) for a, b in self.pairs]
        if upper:
            parts = [p.astype(BF16) for p in parts]
        return parts[0] if len(parts) == 1 else jnp.concatenate(parts, axis=1)

    def begin(self, *deps):
        if deps:
            a, b = self.pairs[0]
            a, *_ = tie(a, *deps)
            self.pairs[0] = (a, b)
        self.send = self.part(True)
        return self.send

    def stay(self, *deps):
        if deps:
            a, b = self.pairs[0]
            a, *_ = tie(a, *deps)
            self.pairs[0] = (a, b)
        self.keep = self.part(False)
        return self.keep

    def go(self):
        self.came, self.open = self.send, self.at < len(self.order)
        if self.open:
            self.came = self.flip(self.send, self.order[self.at])

    def add(self):
        if self.open:
            self.open = False
            self.total = self.keep + self.came.astype(F32)
            self.at += 1
            if self.at < len(self.order):
                self.send = half_of(self.total, True).astype(BF16)
                self.keep = half_of(self.total, False)
        elif not self.order:
            self.total = self.keep

    def rest(self):
        self.add()
        while self.at < len(self.order):
            self.go()
            self.add()
        return self.total


def half_of(value, upper, axis=0):
    size = value.shape[axis] // 2
    return lax.slice_in_dim(value, size if upper else 0, 2 * size if upper else size, axis=axis)


def tie(*values):
    return lax.optimization_barrier(values)


def serve(value, done=(), ready=()):
    out = tie(value, *[h.came for h in done], *ready)
    for h, came in zip(done, out[1:]):
        h.came = came
    return out[0]


def shards(
    count,
    tokens,
    segment_ids,
    cotangent,
    g_attn,
    query_weight,
    key_weight,
    value_weight,
    w_o,
    g_mlp,
    w_gate,
    w_up,
    w_down,
):
    row = lax.axis_index("row")
    dp = lax.axis_index("dp")
    bits = count.bit_length() - 1

    def swap(value):
        return lax.ppermute(value, "row", [(0, 1), (1, 0)])

    def cross(value):
        return lax.ppermute(value, "col", [(0, 1), (1, 0)])

    def flip(value, bit):
        return lax.ppermute(value, "dp", [(i, i ^ (1 << bit)) for i in range(count)])

    def order_of(first):
        return ([first] + [b for b in range(bits) if b != first]) if bits else []

    def relative(value, order):
        width = value.shape[1] // count
        blocks = []
        for place in range(count):
            differs = 0
            for at, bit in enumerate(order):
                differs |= ((place >> (len(order) - 1 - at)) & 1) << bit
            blocks.append(lax.dynamic_slice_in_dim(value, (dp ^ differs) * width, width, axis=1))
        return jnp.concatenate(blocks, axis=1)

    low = (dp & 1) == 0
    half = w_o.shape[0] // 2
    far_a = cross(jnp.where(low, w_o[:half], w_o[half:]))
    x_m = own_rows(tokens, row)
    x_o = swap(other_rows(tokens, row))
    wkv = jnp.concatenate([key_weight, value_weight], axis=1)
    wkv_o = swap(wkv)
    wq_o = swap(query_weight)
    gains = jnp.stack([g_attn, g_mlp])
    gains_o = swap(gains)
    x_m, x_o = x_m.astype(F32), x_o.astype(F32)
    square = jnp.sum(x_m * x_m, axis=-1, keepdims=True) + jnp.sum(x_o * x_o, axis=-1, keepdims=True)
    inv_one = lax.rsqrt(square / MODEL_WIDTH + EPS)
    xn_m = (x_m * inv_one * gains[0]).astype(BF16)
    xn_o = (x_o * inv_one * gains_o[0]).astype(BF16)

    start = jnp.sum((segment_ids[None, :] < segment_ids[:, None]).astype(jnp.int32), axis=1)
    index = lax.iota(jnp.int32, SEQ)
    start_own = own_rows(start, row)
    places = own_rows(index, row) - start_own
    freq = jnp.exp(jnp.arange(HALF, dtype=F32) * (-2.0 * math.log(THETA) / HEAD_SIZE))
    turn_t = freq[:, None] * places.astype(F32)[None, :]
    cosine_t, sine_t = jnp.cos(turn_t), jnp.sin(turn_t)
    cosine, sine = cosine_t.T[:, None, :], sine_t.T[:, None, :]

    kv = dot_plain(xn_m, wkv) + dot_plain(xn_o, wkv_o)
    narrow = key_weight.shape[1]
    wide = query_weight.shape[1]
    kp = kv[:, :narrow].reshape(OWN, -1, HEAD_SIZE)
    first, second = kp[..., :HALF], kp[..., HALF:]
    key = jnp.concatenate([first * cosine - second * sine, second * cosine + first * sine], axis=-1)
    own_kv = jnp.concatenate([key.reshape(OWN, narrow), kv[:, narrow:]], axis=1).astype(BF16)
    other_kv = swap(own_kv)
    xn_m, xn_o, own_kv = tie(xn_m, xn_o, own_kv)
    q = dot_plain(xn_m, query_weight) + dot_plain(xn_o, wq_o)

    cotangent, w_gate, w_up, w_down, w_o, xn_o = tie(cotangent, w_gate, w_up, w_down, w_o, xn_o)
    wg_o = swap(w_gate)
    wu_o = swap(w_up)
    w_o_o = swap(w_o)
    c_m = own_rows(cotangent, row)
    c_t = other_rows(cotangent, row)
    q, far_a, other_kv, c_m, c_t = tie(q, far_a, other_kv, c_m, c_t)
    far_b = flip(far_a, 0)
    row_arg = row.astype(jnp.int32).reshape(1)
    start_arg = start_own.reshape(1, OWN)
    o_1, lse_1, qt_1 = attend(0, row_arg, q, cosine_t, sine_t, start_arg, own_kv, other_kv)
    o_1, q, wg_o, wu_o, w_o_o, w_down, c_t, far_a = tie(o_1, q, wg_o, wu_o, w_o_o, w_down, c_t, far_a)
    o_x1 = cross(o_1)
    c_o = swap(c_t)
    wd_o = swap(w_down)
    far_ao = swap(far_a)
    o_2, lse_2, qt_2 = attend(1, row_arg, q, cosine_t, sine_t, start_arg, own_kv, other_kv)
    o_2, o_1, c_o, wd_o, far_ao, xn_o = tie(o_2, o_1, c_o, wd_o, far_ao, xn_o)
    o_x2 = cross(o_2)

    near_m = dot_plain(o_1, w_o[:half]) + dot_plain(o_2, w_o[half:])
    near_o = dot_plain(o_1, w_o_o[:half]) + dot_plain(o_2, w_o_o[half:])
    order_y, order_z = order_of(0), order_of(min(1, max(bits - 1, 0)))
    both = lambda own, other: jnp.concatenate([own, other], axis=0)
    c_y = relative(both(c_m, c_t), order_y)
    o = jnp.concatenate([o_1, o_2], axis=1)
    o_t = swap(o)
    qt = jnp.concatenate([qt_1, qt_2], axis=0)
    lse = jnp.concatenate([lse_1, lse_2], axis=0)
    near_m, near_o, far_b = tie(near_m, near_o, far_b)
    far_bo = swap(far_b)
    xn_t = swap(xn_o)
    c_y, qt, lse, far_b, far_bo, o_x1 = tie(c_y, qt, lse, far_b, far_bo, o_x1)
    pick = lambda a, b: (jnp.where(low, a, b), jnp.where(low, b, a))
    far_1, far_2 = pick(far_a, far_b)
    far_1o, far_2o = pick(far_ao, far_bo)
    mid_m, mid_o = dot_plain(o_x1, far_1), dot_plain(o_x1, far_1o)
    mid_m, mid_o, o_t, xn_t, o_x2 = tie(mid_m, mid_o, o_t, xn_t, o_x2)
    hidden_m = x_m + (near_m + (mid_m + dot_plain(o_x2, far_2)))
    hidden_o = x_o + (near_o + (mid_o + dot_plain(o_x2, far_2o)))
    square = jnp.sum(hidden_m * hidden_m, axis=-1, keepdims=True) + jnp.sum(
        hidden_o * hidden_o, axis=-1, keepdims=True
    )
    inv_two = lax.rsqrt(square / MODEL_WIDTH + EPS)
    unit_m, unit_o = hidden_m * inv_two, hidden_o * inv_two
    xn2_m = (unit_m * gains[1]).astype(BF16)
    xn2_o = (unit_o * gains_o[1]).astype(BF16)

    xn2_t = swap(xn2_o)
    tiles = w_gate.shape[1] // 256
    operands = (c_m, c_o, w_gate, wg_o, w_up, wu_o, w_down, wd_o)
    one = hidden_units(0, tiles - tiles // 2, xn2_m, xn2_o, *operands)
    one_t = swap(one)
    one, xn2_m2 = tie(one, xn2_m)
    two = hidden_units(tiles - tiles // 2, tiles // 2, xn2_m2, xn2_o, *operands)
    two, one_t, xn2_t = tie(two, one_t, xn2_t)
    two_t = swap(two)

    all_1 = [both(one[i], one_t[i]) for i in range(3)]
    down_1 = Halving([(c_y, all_1[0])], order_y, flip)
    down_1.begin(two)
    down_1.go()
    down_1.send, xn2_m2 = tie(down_1.send, xn2_m2)
    xn2_all = both(xn2_m2, xn2_t)
    xn2_y, xn2_z = relative(xn2_all, order_y), relative(xn2_all, order_z)
    upper_1 = Halving([(xn2_z, all_1[2])], order_z, flip)
    upper_1.begin()
    upper_1.go()
    upper_1.send, two_late, two_t = tie(upper_1.send, two, two_t)
    part = input_grad(one, two_late, w_gate, w_up, wg_o, wu_o)
    came = cross(part)
    part, two_t = tie(part, two_t)
    all_2 = [both(two[i], two_t[i]) for i in range(3)]
    middle = Halving([(c_y, all_2[0]), (xn2_y, all_1[1])], order_y, flip)
    middle.begin(part)
    middle.go()
    upper_2 = Halving([(xn2_z, all_2[2])], order_z, flip)
    upper_2.begin(middle.send)
    upper_2.go()
    gate_2 = Halving([(xn2_y, all_2[1])], order_y, flip)
    gate_2.begin(upper_2.send)
    down_1.stay(gate_2.send)
    upper_1.stay(down_1.keep)
    part = serve(part, (down_1, upper_1), (upper_1.keep, down_1.keep))
    down_1.add()
    down_1.go()
    upper_1.add()
    upper_1.go()
    middle.stay(part, down_1.send, upper_1.send)
    upper_2.stay(middle.keep)
    gate_2.stay(upper_2.keep)

    came, gate_2.keep, middle.keep, upper_2.keep = tie(came, gate_2.keep, middle.keep, upper_2.keep)
    width = tokens.shape[1]
    d_xn2 = part.astype(F32) + came.astype(F32)
    d_xn2_m, d_xn2_o = d_xn2[:, :width], d_xn2[:, width:]
    e_m, e_o = d_xn2_m * gains[1], d_xn2_o * gains_o[1]
    mean = (
        jnp.sum(e_m * unit_m, axis=-1, keepdims=True) + jnp.sum(e_o * unit_o, axis=-1, keepdims=True)
    ) / MODEL_WIDTH
    gg_mlp_m = jnp.sum(d_xn2_m * unit_m, axis=0)
    gg_mlp_o = jnp.sum(d_xn2_o * unit_o, axis=0)
    d_hid_m = c_m.astype(F32) + inv_two * (e_m - unit_m * mean)
    d_hid_o = c_o.astype(F32) + inv_two * (e_o - unit_o * mean)
    dh_m, dh_o = d_hid_m.astype(BF16), d_hid_o.astype(BF16)
    dh_t = swap(dh_o)
    d_o = (dot_right(dh_m, w_o) + dot_right(dh_o, w_o_o)).astype(BF16)
    d_o, dh_t, gate_2.send = tie(d_o, dh_t, gate_2.send)
    d_o = serve(d_o, (upper_2,))
    gate_2.go()
    upper_2.add()
    d_o, upper_2.send, upper_2.keep, gate_2.send = tie(d_o, upper_2.send, upper_2.keep, gate_2.send)

    d_q, d_k, d_v = attend_back(row_arg, qt, d_o, o, lse, cosine_t, sine_t, start_arg, own_kv, other_kv)
    d_kv = jnp.concatenate([d_k[0], d_k[1], d_v[0], d_v[1]], axis=1)
    d_kv_t = swap(other_rows(d_kv, row))
    d_kv_own = own_rows(d_kv, row)
    d_kv_own = serve(d_kv_own, (down_1,))
    down_1.add()
    d_kv_t, d_kv_own, down_1.send, down_1.keep = tie(d_kv_t, d_kv_own, down_1.send, down_1.keep)
    d_kv = d_kv_own + d_kv_t
    d_key = d_kv[:, :narrow].reshape(OWN, -1, HEAD_SIZE)
    first, second = d_key[..., :HALF], d_key[..., HALF:]
    d_key = jnp.concatenate([first * cosine + second * sine, second * cosine - first * sine], axis=-1)
    d_kv = jnp.concatenate([d_key.reshape(OWN, narrow).astype(BF16), d_kv[:, narrow:].astype(BF16)], axis=1)
    d_qkv = jnp.concatenate([d_q, d_kv], axis=1)
    d_qkv_t = swap(d_qkv)
    last = jnp.concatenate(
        [
            (dot_right(d_q, query_weight) + dot_right(d_kv, wkv)).astype(BF16),
            (dot_right(d_q, wq_o) + dot_right(d_kv, wkv_o)).astype(BF16),
        ],
        axis=1,
    )
    last, d_qkv_t = tie(last, d_qkv_t)
    last_came = cross(last)
    last = serve(last, (middle,))
    middle.add()
    middle.go()
    outer = Halving(
        [
            (relative(both(dh_m, dh_t), order_y), both(o, o_t)),
            (relative(both(xn_m, xn_t), order_y), both(d_qkv, d_qkv_t)),
        ],
        order_y,
        flip,
    )
    outer.begin(last, middle.send, middle.keep)
    outer.send = serve(outer.send, (upper_1,))
    outer.go()
    upper_1.add()
    upper_1.go()
    down_1.send, upper_1.send = tie(down_1.send, upper_1.send)
    down_1.go()
    outer.stay(down_1.send, outer.send)
    one, outer.keep = tie(one, outer.keep)
    cut = one.shape[2]
    mix = jnp.concatenate(
        [
            (dot_plain(one[0], w_down[:cut]) + dot_plain(two[0], w_down[cut:])).astype(BF16),
            (dot_plain(one[0], wd_o[:cut]) + dot_plain(two[0], wd_o[cut:])).astype(BF16),
        ],
        axis=1,
    )
    mix = serve(mix, (down_1, middle, upper_1))
    down_1.add()
    middle.add()
    middle.go()
    upper_2.send, middle.send = tie(upper_2.send, middle.send)
    upper_2.go()

    last_came, mix, middle.keep, middle.send = tie(last_came, mix, middle.keep, middle.send)
    mix_came = cross(mix)
    d_xn = last.astype(F32) + last_came.astype(F32)
    d_xn_m, d_xn_o = d_xn[:, :width], d_xn[:, width:]
    unit_m, unit_o = x_m * inv_one, x_o * inv_one
    e_m, e_o = d_xn_m * gains[0], d_xn_o * gains_o[0]
    mean = (
        jnp.sum(e_m * unit_m, axis=-1, keepdims=True) + jnp.sum(e_o * unit_o, axis=-1, keepdims=True)
    ) / MODEL_WIDTH
    gg_attn_m = jnp.sum(d_xn_m * unit_m, axis=0)
    gg_attn_o = jnp.sum(d_xn_o * unit_o, axis=0)
    d_tok_m = d_hid_m + inv_one * (e_m - unit_m * mean)
    d_tok_o = d_hid_o + inv_one * (e_o - unit_o * mean)
    d_tok_t = swap(d_tok_o)
    gg = jnp.stack([gg_attn_m, gg_mlp_m]) + swap(jnp.stack([gg_attn_o, gg_mlp_o]))
    gg = lax.psum_scatter(gg, "dp", scatter_dimension=1, tiled=True)
    d_tokens = merge_rows(d_tok_m, d_tok_t, row)

    d_tokens = serve(d_tokens, (gate_2,))
    gate_2.add()
    gate_2.go()
    d_tokens, gate_2.send, gate_2.keep = tie(d_tokens, gate_2.send, gate_2.keep)
    gate_2.came = serve(gate_2.came, (middle,))
    middle.add()
    outer.came, middle.total = tie(outer.came, middle.total)
    outer.add()
    outer.go()
    outer.send, mix_came = tie(outer.send, mix_came)

    mixed_all = mix.astype(F32) + mix_came.astype(F32)
    out_m = (hidden_m + mixed_all[:, :width]).astype(BF16)
    out_o = (hidden_o + mixed_all[:, width:]).astype(BF16)
    mixed = merge_rows(out_m, swap(out_o), row)

    cut = one.shape[2]
    down_1, upper_1, middle = down_1.rest(), upper_1.rest(), middle.rest()
    gate_2, upper_2, outer = gate_2.rest(), upper_2.rest(), outer.rest()
    gw_down = jnp.concatenate([down_1.T, middle[:, : w_gate.shape[1] - cut].T], axis=0)
    gw_gate = jnp.concatenate([middle[:, w_gate.shape[1] - cut :], gate_2], axis=1)
    gw_up = jnp.concatenate([upper_1, upper_2], axis=1)
    gw_o, gw_qkv = outer[:, : o.shape[1]].T, outer[:, o.shape[1] :]
    return (
        mixed,
        d_tokens,
        gg[0],
        gw_qkv[:, :wide],
        gw_qkv[:, wide : wide + narrow],
        gw_qkv[:, wide + narrow :],
        gw_o,
        gg[1],
        gw_gate,
        gw_up,
        gw_down,
    )


def solution(mesh):
    count = mesh.shape["dp"]
    placed = (
        P("dp", "row"),
        P("dp"),
        P("dp", "row"),
        P("row"),
        P("row", "col"),
        P("row", "col"),
        P("row", "col"),
        P("col", "row"),
        P("row"),
        P("row", "col"),
        P("row", "col"),
        P("col", "row"),
    )

    def body(*args):
        return shards(count, *args)

    return jax.shard_map(
        body,
        mesh=mesh,
        in_specs=placed,
        out_specs=(
            P("dp", "row"),
            P("dp", "row"),
            P(("row", "dp")),
            P(("row", "dp"), "col"),
            P(("row", "dp"), "col"),
            P(("row", "dp"), "col"),
            P("col", ("row", "dp")),
            P(("row", "dp")),
            P(("row", "dp"), "col"),
            P(("row", "dp"), "col"),
            P("col", ("row", "dp")),
        ),
        check_vma=False,
    )
```

```python
import functools
import math

import jax
import jax.numpy as jnp
from jax import lax
from jax.experimental import pallas as pl
from jax.experimental.pallas import tpu as pltpu
from jax.sharding import PartitionSpec as P

MODEL_WIDTH = 2048
QUERY_HEADS = 32
KEY_VALUE_HEADS = 4
HEAD_SIZE = 64
SEQ = 1024

EPS = 1e-05
THETA = 10000.0
HALF = HEAD_SIZE // 2
CHUNK = SEQ // 4
OWN = SEQ // 2
PAIR = 2 * HEAD_SIZE
SCALE = HEAD_SIZE ** (-0.5)
NEG = -1e30
F32 = jnp.float32
BF16 = jnp.bfloat16


def dot_plain(left, right):
    return jnp.dot(left, right, preferred_element_type=F32)


def dot_right(left, right):
    return lax.dot_general(left, right, (((1,), (1,)), ((), ())), preferred_element_type=F32)


def dot_left(left, right):
    return lax.dot_general(left, right, (((0,), (0,)), ((), ())), preferred_element_type=F32)


def own_rows(value, row):
    a, b, c, d = (value[i * CHUNK : (i + 1) * CHUNK] for i in range(4))
    return jnp.concatenate([jnp.where(row == 0, a, b), jnp.where(row == 0, d, c)], axis=0)


def other_rows(value, row):
    a, b, c, d = (value[i * CHUNK : (i + 1) * CHUNK] for i in range(4))
    return jnp.concatenate([jnp.where(row == 0, b, a), jnp.where(row == 0, c, d)], axis=0)


def merge_rows(own, other, row):
    a, b = own[:CHUNK], own[CHUNK:]
    c, d = other[:CHUNK], other[CHUNK:]
    return jnp.concatenate(
        [
            jnp.where(row == 0, a, c),
            jnp.where(row == 0, c, a),
            jnp.where(row == 0, d, b),
            jnp.where(row == 0, b, d),
        ],
        axis=0,
    )


def chunk_bias(start_ref, bias, row):
    for c in range(2):
        place = jnp.where(row == 0, 3 * c, 1 + c) * CHUNK
        lanes = slice(c * CHUNK, (c + 1) * CHUNK)
        keys = lax.broadcasted_iota(jnp.int32, (SEQ, CHUNK), 0)
        queries = lax.broadcasted_iota(jnp.int32, (SEQ, CHUNK), 1) + place
        allowed = (keys >= start_ref[:, lanes]) & (keys <= queries)
        bias[:, lanes] = jnp.where(allowed, 0.0, NEG)


def place_keys(own_ref, other_ref, row, put):
    @pl.when(row == 0)
    def _():
        for i, (ref, half) in enumerate(((own_ref, 0), (other_ref, 0), (other_ref, 1), (own_ref, 1))):
            put(i, ref[half * CHUNK : (half + 1) * CHUNK, :])

    @pl.when(row == 1)
    def _():
        for i, (ref, half) in enumerate(((other_ref, 0), (own_ref, 0), (own_ref, 1), (other_ref, 1))):
            put(i, ref[half * CHUNK : (half + 1) * CHUNK, :])


def attend_kernel(
    group, row_ref, q_ref, cos_ref, sin_ref, start_ref, own_ref, other_ref, o_ref, lse_ref, qt_ref, bias, keys, values_t
):
    step = pl.program_id(0)
    row = row_ref[0]

    @pl.when(step == 0)
    def _():
        chunk_bias(start_ref, bias, row)

        def put(i, block):
            span = slice(i * CHUNK, (i + 1) * CHUNK)
            lanes = slice(group * HEAD_SIZE, (group + 1) * HEAD_SIZE)
            keys[span, :] = block[:, lanes]
            values_t[:, span] = jnp.transpose(block[:, PAIR:].astype(F32)).astype(BF16)[lanes]

        place_keys(own_ref, other_ref, row, put)

    turned = jnp.transpose(q_ref[...])
    cosine, sine = cos_ref[...], sin_ref[...]
    for h in range(2):
        a = turned[h * HEAD_SIZE : h * HEAD_SIZE + HALF]
        b = turned[h * HEAD_SIZE + HALF : (h + 1) * HEAD_SIZE]
        rot = jnp.concatenate([a * cosine - b * sine, b * cosine + a * sine], axis=0)
        qt_ref[h * HEAD_SIZE : (h + 1) * HEAD_SIZE, :] = (rot * SCALE).astype(BF16)

    def unit(c, blocks):
        lanes = slice(c * CHUNK, (c + 1) * CHUNK)
        count = blocks * CHUNK
        outs, sums = [], []
        for h in range(2):
            query = qt_ref[h * HEAD_SIZE : (h + 1) * HEAD_SIZE, lanes]
            scores = dot_plain(keys[:count, :], query) + bias[:count, lanes]
            top = jnp.max(scores, axis=0, keepdims=True)
            expo = jnp.exp(scores - top)
            total = jnp.sum(expo, axis=0, keepdims=True)
            head = dot_plain(values_t[:, :count], expo.astype(BF16))
            outs.append(head * (1.0 / total))
            sums.append(top + jnp.log(total))
        o_ref[lanes, :] = jnp.transpose(jnp.concatenate(outs, axis=0)).astype(BF16)
        lse_ref[0, :, lanes] = jnp.concatenate(sums, axis=0)

    @pl.when(row == 0)
    def _():
        unit(0, 1)
        unit(1, 4)

    @pl.when(row == 1)
    def _():
        unit(0, 2)
        unit(1, 3)


def attend(group, row, q, cosine, sine, start, own_kv, other_kv):
    pairs = q.shape[1] // (2 * PAIR)
    whole = lambda shape: pl.BlockSpec(shape, lambda i: (0,) * len(shape))
    return pl.pallas_call(
        functools.partial(attend_kernel, group),
        grid=(pairs,),
        in_specs=[
            pl.BlockSpec(memory_space=pltpu.SMEM),
            pl.BlockSpec((OWN, PAIR), lambda i: (0, i + group * pairs)),
            whole((HALF, OWN)),
            whole((HALF, OWN)),
            whole((1, OWN)),
            whole((OWN, 2 * PAIR)),
            whole((OWN, 2 * PAIR)),
        ],
        out_specs=[
            pl.BlockSpec((OWN, PAIR), lambda i: (0, i)),
            pl.BlockSpec((1, 2, OWN), lambda i: (i, 0, 0)),
            pl.BlockSpec((PAIR, OWN), lambda i: (i, 0)),
        ],
        out_shape=[
            jax.ShapeDtypeStruct((OWN, pairs * PAIR), BF16),
            jax.ShapeDtypeStruct((pairs, 2, OWN), F32),
            jax.ShapeDtypeStruct((pairs * PAIR, OWN), BF16),
        ],
        scratch_shapes=[
            pltpu.VMEM((SEQ, OWN), F32),
            pltpu.VMEM((SEQ, HEAD_SIZE), BF16),
            pltpu.VMEM((HEAD_SIZE, SEQ), BF16),
        ],
        compiler_params=pltpu.CompilerParams(vmem_limit_bytes=40 * 1024 * 1024),
        cost_estimate=pl.CostEstimate(flops=1000, bytes_accessed=1000, transcendentals=0),
        name="attend",
    )(row, q, cosine, sine, start, own_kv, other_kv)


def attend_back_kernel(
    row_ref,
    qt_ref,
    do_ref,
    o_ref,
    lse_ref,
    cos_ref,
    sin_ref,
    start_ref,
    own_ref,
    other_ref,
    dq_ref,
    dk_ref,
    dv_ref,
    bias,
    keys,
    keys_t,
    values,
):
    step = pl.program_id(0)
    kv = step // 4
    row = row_ref[0]

    @pl.when(step == 0)
    def _():
        chunk_bias(start_ref, bias, row)

        def put(i, block):
            span = slice(i * CHUNK, (i + 1) * CHUNK)
            for h in range(2):
                keys[h, span, :] = block[:, h * HEAD_SIZE : (h + 1) * HEAD_SIZE]
                values[h, span, :] = block[:, PAIR + h * HEAD_SIZE : PAIR + (h + 1) * HEAD_SIZE]
            turned = jnp.transpose(block[:, :PAIR].astype(F32)).astype(BF16)
            for h in range(2):
                keys_t[h, :, span] = turned[h * HEAD_SIZE : (h + 1) * HEAD_SIZE]

        place_keys(own_ref, other_ref, row, put)

    @pl.when(step % 4 == 0)
    def _():
        dk_ref[...] = jnp.zeros_like(dk_ref)
        dv_ref[...] = jnp.zeros_like(dv_ref)

    grad = do_ref[...].astype(F32)
    grad_t = jnp.transpose(grad)
    mixed_t = jnp.transpose(grad * o_ref[...].astype(F32))
    cosine, sine = cos_ref[...], sin_ref[...]

    def unit(c, blocks):
        lanes = slice(c * CHUNK, (c + 1) * CHUNK)
        count = blocks * CHUNK
        outs = []
        for h in range(2):
            rows = slice(h * HEAD_SIZE, (h + 1) * HEAD_SIZE)
            query = qt_ref[rows, lanes]
            d_head = grad_t[rows, lanes].astype(BF16)
            delta = jnp.sum(mixed_t[rows, lanes], axis=0, keepdims=True)
            scores = dot_plain(keys[kv, :count, :], query) + bias[:count, lanes]
            probs = jnp.exp(scores - lse_ref[0, h : h + 1, lanes])
            dv_ref[0, :count, :] += dot_right(probs.astype(BF16), d_head)
            d_probs = dot_plain(values[kv, :count, :], d_head)
            d_raw = (probs * (d_probs - delta)).astype(BF16)
            d_query = dot_plain(keys_t[kv, :, :count], d_raw) * SCALE
            dk_ref[0, :count, :] += dot_right(d_raw, query)
            a, b = d_query[:HALF], d_query[HALF:]
            co, si = cosine[:, lanes], sine[:, lanes]
            outs.append(a * co + b * si)
            outs.append(b * co - a * si)
        dq_ref[lanes, :] = jnp.transpose(jnp.concatenate(outs, axis=0)).astype(BF16)

    @pl.when(row == 0)
    def _():
        unit(0, 1)
        unit(1, 4)

    @pl.when(row == 1)
    def _():
        unit(0, 2)
        unit(1, 3)


def attend_back(row, qt, d_o, o, lse, cosine, sine, start, own_kv, other_kv):
    heads = qt.shape[0] // HEAD_SIZE
    pairs = heads // 2
    whole = lambda shape: pl.BlockSpec(shape, lambda i: (0,) * len(shape))
    return pl.pallas_call(
        attend_back_kernel,
        grid=(pairs,),
        in_specs=[
            pl.BlockSpec(memory_space=pltpu.SMEM),
            pl.BlockSpec((PAIR, OWN), lambda i: (i, 0)),
            pl.BlockSpec((OWN, PAIR), lambda i: (0, i)),
            pl.BlockSpec((OWN, PAIR), lambda i: (0, i)),
            pl.BlockSpec((1, 2, OWN), lambda i: (i, 0, 0)),
            whole((HALF, OWN)),
            whole((HALF, OWN)),
            whole((1, OWN)),
            whole((OWN, 2 * PAIR)),
            whole((OWN, 2 * PAIR)),
        ],
        out_specs=[
            pl.BlockSpec((OWN, PAIR), lambda i: (0, i)),
            pl.BlockSpec((1, SEQ, HEAD_SIZE), lambda i: (i // 4, 0, 0)),
            pl.BlockSpec((1, SEQ, HEAD_SIZE), lambda i: (i // 4, 0, 0)),
        ],
        out_shape=[
            jax.ShapeDtypeStruct((OWN, heads * HEAD_SIZE), BF16),
            jax.ShapeDtypeStruct((2, SEQ, HEAD_SIZE), F32),
            jax.ShapeDtypeStruct((2, SEQ, HEAD_SIZE), F32),
        ],
        scratch_shapes=[
            pltpu.VMEM((SEQ, OWN), F32),
            pltpu.VMEM((2, SEQ, HEAD_SIZE), BF16),
            pltpu.VMEM((2, HEAD_SIZE, SEQ), BF16),
            pltpu.VMEM((2, SEQ, HEAD_SIZE), BF16),
        ],
        compiler_params=pltpu.CompilerParams(vmem_limit_bytes=40 * 1024 * 1024),
        cost_estimate=pl.CostEstimate(flops=1000, bytes_accessed=1000, transcendentals=0),
        name="attend_back",
    )(row, qt, d_o, o, lse, cosine, sine, start, own_kv, other_kv)


def hidden_units_kernel(
    xm_ref, xo_ref, cm_ref, co_ref, gm_ref, go_ref, um_ref, uo_ref, dm_ref, do_ref, out_ref
):
    gate = dot_plain(xm_ref[...], gm_ref[...]) + dot_plain(xo_ref[...], go_ref[...])
    up = dot_plain(xm_ref[...], um_ref[...]) + dot_plain(xo_ref[...], uo_ref[...])
    d_act = dot_right(cm_ref[...], dm_ref[...]) + dot_right(co_ref[...], do_ref[...])
    sigma = jax.nn.sigmoid(gate)
    swish = gate * sigma
    out_ref[0] = (swish * up).astype(BF16)
    out_ref[1] = (d_act * up * (sigma * (1.0 + gate * (1.0 - sigma)))).astype(BF16)
    out_ref[2] = (d_act * swish).astype(BF16)


def hidden_units(first, tiles, xm, xo, cm, co, gm, go, um, uo, dm, do):
    rows, depth = xm.shape
    tile = 256
    wide = tiles * tile
    full = pl.BlockSpec((rows, depth), lambda i: (0, 0))
    column = pl.BlockSpec((depth, tile), lambda i: (0, i + first))
    line = pl.BlockSpec((tile, depth), lambda i: (i + first, 0))
    out = pl.BlockSpec((3, rows, tile), lambda i: (0, 0, i))
    return pl.pallas_call(
        hidden_units_kernel,
        grid=(tiles,),
        in_specs=[full] * 4 + [column] * 4 + [line] * 2,
        out_specs=out,
        out_shape=jax.ShapeDtypeStruct((3, rows, wide), BF16),
        compiler_params=pltpu.CompilerParams(vmem_limit_bytes=48 * 1024 * 1024),
        cost_estimate=pl.CostEstimate(flops=1000, bytes_accessed=1000, transcendentals=0),
        name="hidden_units",
    )(xm, xo, cm, co, gm, go, um, uo, dm, do)


def input_grad_kernel(a_ref, b_ref, gm_ref, um_ref, go_ref, uo_ref, out_ref):
    cut = a_ref.shape[2]

    def fill(g_ref, u_ref):
        total = dot_right(a_ref[1], g_ref[:, :cut]) + dot_right(b_ref[1], g_ref[:, cut:])
        total += dot_right(a_ref[2], u_ref[:, :cut]) + dot_right(b_ref[2], u_ref[:, cut:])
        out_ref[...] = total.astype(BF16)

    step, half = pl.program_id(0), pl.num_programs(0) // 2
    pl.when(step < half)(lambda: fill(gm_ref, um_ref))
    pl.when(step >= half)(lambda: fill(go_ref, uo_ref))


def input_grad(a, b, gm, um, go, uo):
    rows = a.shape[1]
    depth, wide = gm.shape
    tile = 256
    tiles = depth // tile
    full = lambda value: pl.BlockSpec(value.shape, lambda i: (0, 0, 0))
    line_m = pl.BlockSpec((tile, wide), lambda i: (jnp.minimum(i, tiles - 1), 0))
    line_o = pl.BlockSpec((tile, wide), lambda i: (jnp.maximum(i - tiles, 0), 0))
    return pl.pallas_call(
        input_grad_kernel,
        grid=(2 * tiles,),
        in_specs=[full(a), full(b), line_m, line_m, line_o, line_o],
        out_specs=pl.BlockSpec((rows, tile), lambda i: (0, i)),
        out_shape=jax.ShapeDtypeStruct((rows, 2 * depth), BF16),
        compiler_params=pltpu.CompilerParams(vmem_limit_bytes=48 * 1024 * 1024),
        cost_estimate=pl.CostEstimate(flops=1000, bytes_accessed=1000, transcendentals=0),
        name="input_grad",
    )(a, b, gm, um, go, uo)


def product_kernel(counts, *refs):
    pieces = len(counts)
    lefts, owns, others = (refs[i * pieces : (i + 1) * pieces] for i in range(3))
    send_ref, keep_ref = refs[3 * pieces :]
    step, first = pl.program_id(0), 0
    for left, own, other, count in zip(lefts, owns, others, counts):

        @pl.when((step >= first) & (step < first + count))
        def _(left=left, own=own, other=other):
            tokens, half = own.shape[1], left.shape[0] // 2
            total = dot_plain(left[:, :tokens], own[0]) + dot_plain(left[:, tokens:], other[0])
            send_ref[...] = total[:half].astype(BF16)
            keep_ref[...] = total[half:].astype(BF16)

        first += count


def product(pieces):
    tile = 256
    counts = [own.shape[2] // tile for _, own, _, _ in pieces]
    rows, tokens = pieces[0][0].shape
    owns, others = [], []
    first = 0
    for (_, own, other, index), count in zip(pieces, counts):
        place = lambda i, first=first, count=count: jnp.clip(i - first, 0, count - 1)
        owns.append(pl.BlockSpec((1, own.shape[1], tile), lambda i, index=index, place=place: (index, 0, place(i))))
        others.append(pl.BlockSpec((1, other.shape[1], tile), lambda i, index=index, place=place: (index, 0, place(i))))
        first += count
    return pl.pallas_call(
        functools.partial(product_kernel, counts),
        grid=(first,),
        in_specs=[pl.BlockSpec((rows, tokens), lambda i: (0, 0))] * len(pieces) + owns + others,
        out_specs=[pl.BlockSpec((rows // 2, tile), lambda i: (0, i))] * 2,
        out_shape=[jax.ShapeDtypeStruct((rows // 2, first * tile), BF16)] * 2,
        compiler_params=pltpu.CompilerParams(vmem_limit_bytes=40 * 1024 * 1024),
        cost_estimate=pl.CostEstimate(flops=1000, bytes_accessed=1000, transcendentals=0),
        name="product",
    )(*[p[0] for p in pieces], *[p[1] for p in pieces], *[p[2] for p in pieces])


def sided_kernel(side_ref, own_ref, other_ref, out_ref):
    tokens = own_ref.shape[0]
    out_ref[:, :tokens] = jnp.transpose(own_ref[...])
    out_ref[:, tokens:] = jnp.transpose(other_ref[...])


def sided(own, other, side, count):
    tokens, wide = own.shape
    width = wide // count
    if width % 128:
        blocks = jnp.concatenate([own, other], axis=0).T.reshape(count // 2, 2, width, 2 * tokens)
        near = jnp.where(side == 0, blocks[:, 0], blocks[:, 1])
        far = jnp.where(side == 0, blocks[:, 1], blocks[:, 0])
        return jnp.concatenate([far, near], axis=0).reshape(wide, 2 * tokens)
    column = pl.BlockSpec((tokens, width), lambda i, side: (0, i))
    return pl.pallas_call(
        sided_kernel,
        grid_spec=pltpu.PrefetchScalarGridSpec(
            num_scalar_prefetch=1,
            grid=(count,),
            in_specs=[column, column],
            out_specs=pl.BlockSpec(
                (width, 2 * tokens), lambda i, side: (i // 2 + jnp.where(i % 2 == side[0], count // 2, 0), 0)
            ),
        ),
        out_shape=jax.ShapeDtypeStruct((wide, 2 * tokens), BF16),
        compiler_params=pltpu.CompilerParams(vmem_limit_bytes=40 * 1024 * 1024),
        cost_estimate=pl.CostEstimate(flops=1000, bytes_accessed=1000, transcendentals=0),
        name="sided",
    )(side.astype(jnp.int32).reshape(1), own, other)


class Summed:
    def __init__(self, pieces, flip, count):
        self.pieces, self.flip, self.count = pieces, flip, count

    def begin(self, *deps):
        left, *others = self.pieces[0]
        left, *_ = tie(left, *deps)
        self.send, self.keep = product([(left, *others), *self.pieces[1:]])
        return self.keep

    def go(self, after=None):
        if after is not None:
            self.send, after.came = tie(self.send, after.came)
        self.came = self.flip(self.send)

    def scatter(self, value):
        groups = [list(range(side, self.count, 2)) for side in range(2)]
        return lax.psum_scatter(value, "dp", scatter_dimension=0, axis_index_groups=groups, tiled=True)

    def finish(self):
        total = (self.keep.astype(F32) + self.came.astype(F32)).astype(BF16)
        self.total = self.scatter(total)
        return total


def half_of(value, upper, axis=0):
    size = value.shape[axis] // 2
    return lax.slice_in_dim(value, size if upper else 0, 2 * size if upper else size, axis=axis)


def tie(*values):
    return lax.optimization_barrier(values)


def serve(value, done=(), ready=()):
    out = tie(value, *[h.came for h in done], *ready)
    for h, came in zip(done, out[1:]):
        h.came = came
    return out[0]


def shards(
    count,
    tokens,
    segment_ids,
    cotangent,
    g_attn,
    query_weight,
    key_weight,
    value_weight,
    w_o,
    g_mlp,
    w_gate,
    w_up,
    w_down,
):
    row = lax.axis_index("row")
    side = lax.axis_index("dp") & 1
    low = side == 0

    def swap(value):
        return lax.ppermute(value, "row", [(0, 1), (1, 0)])

    def cross(value):
        return lax.ppermute(value, "col", [(0, 1), (1, 0)])

    def flip(value):
        return lax.ppermute(value, "dp", [(i, i ^ 1) for i in range(count)])

    half = w_o.shape[0] // 2
    far_a = cross(jnp.where(low, w_o[:half], w_o[half:]))
    x_m = own_rows(tokens, row)
    x_o = swap(other_rows(tokens, row))
    wkv = jnp.concatenate([key_weight, value_weight], axis=1)
    wkv_o = swap(wkv)
    wq_o = swap(query_weight)
    gains = jnp.stack([g_attn, g_mlp])
    gains_o = swap(gains)
    x_m, x_o = x_m.astype(F32), x_o.astype(F32)
    square = jnp.sum(x_m * x_m, axis=-1, keepdims=True) + jnp.sum(x_o * x_o, axis=-1, keepdims=True)
    inv_one = lax.rsqrt(square / MODEL_WIDTH + EPS)
    xn_m = (x_m * inv_one * gains[0]).astype(BF16)
    xn_o = (x_o * inv_one * gains_o[0]).astype(BF16)

    start = jnp.sum((segment_ids[None, :] < segment_ids[:, None]).astype(jnp.int32), axis=1)
    index = lax.iota(jnp.int32, SEQ)
    start_own = own_rows(start, row)
    places = own_rows(index, row) - start_own
    freq = jnp.exp(jnp.arange(HALF, dtype=F32) * (-2.0 * math.log(THETA) / HEAD_SIZE))
    turn_t = freq[:, None] * places.astype(F32)[None, :]
    cosine_t, sine_t = jnp.cos(turn_t), jnp.sin(turn_t)
    cosine, sine = cosine_t.T[:, None, :], sine_t.T[:, None, :]

    kv = dot_plain(xn_m, wkv) + dot_plain(xn_o, wkv_o)
    narrow = key_weight.shape[1]
    wide = query_weight.shape[1]
    kp = kv[:, :narrow].reshape(OWN, -1, HEAD_SIZE)
    first, second = kp[..., :HALF], kp[..., HALF:]
    key = jnp.concatenate([first * cosine - second * sine, second * cosine + first * sine], axis=-1)
    own_kv = jnp.concatenate([key.reshape(OWN, narrow), kv[:, narrow:]], axis=1).astype(BF16)
    other_kv = swap(own_kv)
    xn_m, xn_o, own_kv = tie(xn_m, xn_o, own_kv)
    q = dot_plain(xn_m, query_weight) + dot_plain(xn_o, wq_o)

    cotangent, w_gate, w_up, w_down, w_o, xn_o = tie(cotangent, w_gate, w_up, w_down, w_o, xn_o)
    wg_o = swap(w_gate)
    wu_o = swap(w_up)
    w_o_o = swap(w_o)
    c_m = own_rows(cotangent, row)
    c_t = other_rows(cotangent, row)
    q, far_a, other_kv, c_m, c_t = tie(q, far_a, other_kv, c_m, c_t)
    far_b = flip(far_a)
    row_arg = row.astype(jnp.int32).reshape(1)
    start_arg = start_own.reshape(1, OWN)
    o_1, lse_1, qt_1 = attend(0, row_arg, q, cosine_t, sine_t, start_arg, own_kv, other_kv)
    o_1, q, wg_o, wu_o, w_o_o, w_down, c_t, far_a = tie(o_1, q, wg_o, wu_o, w_o_o, w_down, c_t, far_a)
    o_x1 = cross(o_1)
    c_o = swap(c_t)
    wd_o = swap(w_down)
    far_ao = swap(far_a)
    o_2, lse_2, qt_2 = attend(1, row_arg, q, cosine_t, sine_t, start_arg, own_kv, other_kv)
    o_2, o_1, c_o, wd_o, far_ao, xn_o = tie(o_2, o_1, c_o, wd_o, far_ao, xn_o)
    o_x2 = cross(o_2)

    near_m = dot_plain(o_1, w_o[:half]) + dot_plain(o_2, w_o[half:])
    near_o = dot_plain(o_1, w_o_o[:half]) + dot_plain(o_2, w_o_o[half:])
    both = lambda own, other: jnp.concatenate([own, other], axis=0)
    c_y = sided(c_m, c_t, side, count)
    o = jnp.concatenate([o_1, o_2], axis=1)
    o_t = swap(o)
    qt = jnp.concatenate([qt_1, qt_2], axis=0)
    lse = jnp.concatenate([lse_1, lse_2], axis=0)
    near_m, near_o, far_b = tie(near_m, near_o, far_b)
    far_bo = swap(far_b)
    xn_t = swap(xn_o)
    c_y, qt, lse, far_b, far_bo, o_x1 = tie(c_y, qt, lse, far_b, far_bo, o_x1)
    pick = lambda a, b: (jnp.where(low, a, b), jnp.where(low, b, a))
    far_1, far_2 = pick(far_a, far_b)
    far_1o, far_2o = pick(far_ao, far_bo)
    mid_m, mid_o = dot_plain(o_x1, far_1), dot_plain(o_x1, far_1o)
    mid_m, mid_o, o_t, xn_t, o_x2 = tie(mid_m, mid_o, o_t, xn_t, o_x2)
    hidden_m = x_m + (near_m + (mid_m + dot_plain(o_x2, far_2)))
    hidden_o = x_o + (near_o + (mid_o + dot_plain(o_x2, far_2o)))
    square = jnp.sum(hidden_m * hidden_m, axis=-1, keepdims=True) + jnp.sum(
        hidden_o * hidden_o, axis=-1, keepdims=True
    )
    inv_two = lax.rsqrt(square / MODEL_WIDTH + EPS)
    unit_m, unit_o = hidden_m * inv_two, hidden_o * inv_two
    xn2_m = (unit_m * gains[1]).astype(BF16)
    xn2_o = (unit_o * gains_o[1]).astype(BF16)

    xn2_t = swap(xn2_o)
    tiles = w_gate.shape[1] // 256
    operands = (c_m, c_o, w_gate, wg_o, w_up, wu_o, w_down, wd_o)
    one = hidden_units(0, tiles - tiles // 2, xn2_m, xn2_o, *operands)
    one_t = swap(one)
    one, xn2_m2 = tie(one, xn2_m)
    two = hidden_units(tiles - tiles // 2, tiles // 2, xn2_m2, xn2_o, *operands)
    two, one_t, xn2_t = tie(two, one_t, xn2_t)
    two_t = swap(two)

    send_1 = Summed([(c_y, one, one_t, 0)], flip, count)
    send_1.begin(two)
    send_1.go()
    send_1.keep, xn2_m2 = tie(send_1.keep, xn2_m2)
    xn2_y = sided(xn2_m2, xn2_t, side, count)
    first_z = Summed([(xn2_y, one, one_t, 2)], flip, count)
    first_z.begin()
    first_z.send = first_z.scatter(first_z.send)
    first_z.keep, two_late = tie(first_z.keep, two)
    part = input_grad(one, two_late, w_gate, w_up, wg_o, wu_o)
    came = cross(part)
    two_t, part = tie(two_t, part)
    send_2 = Summed([(c_y, two, two_t, 0)], flip, count)
    send_2.begin(part)
    part = serve(part, (send_1,), (send_2.keep,))
    send_2.go(send_1)
    part, first_z.keep, total = tie(part, first_z.keep, send_1.finish())
    first_z.keep = first_z.scatter(first_z.keep)
    send_3 = Summed([(xn2_y, one, one_t, 1)], flip, count)
    send_3.begin(part)
    send_4 = Summed([(xn2_y, two, two_t, 1)], flip, count)
    send_4.begin(send_3.keep)
    send_6 = Summed([(xn2_y, two, two_t, 2)], flip, count)
    send_6.begin(send_4.keep)
    came, first_z.send, part = tie(came, first_z.send, part, send_6.keep)[:3]
    came = serve(came, (send_2,))
    send_3.go(send_2)
    came, _ = tie(came, send_2.finish())

    width = tokens.shape[1]
    d_xn2 = part.astype(F32) + came.astype(F32)
    d_xn2_m, d_xn2_o = d_xn2[:, :width], d_xn2[:, width:]
    e_m, e_o = d_xn2_m * gains[1], d_xn2_o * gains_o[1]
    mean = (
        jnp.sum(e_m * unit_m, axis=-1, keepdims=True) + jnp.sum(e_o * unit_o, axis=-1, keepdims=True)
    ) / MODEL_WIDTH
    gg_mlp_m = jnp.sum(d_xn2_m * unit_m, axis=0)
    gg_mlp_o = jnp.sum(d_xn2_o * unit_o, axis=0)
    d_hid_m = c_m.astype(F32) + inv_two * (e_m - unit_m * mean)
    d_hid_o = c_o.astype(F32) + inv_two * (e_o - unit_o * mean)
    dh_m, dh_o = d_hid_m.astype(BF16), d_hid_o.astype(BF16)
    dh_t = swap(dh_o)
    d_o = (dot_right(dh_m, w_o) + dot_right(dh_o, w_o_o)).astype(BF16)
    d_o, dh_t = tie(d_o, dh_t)

    d_q, d_k, d_v = attend_back(row_arg, qt, d_o, o, lse, cosine_t, sine_t, start_arg, own_kv, other_kv)
    d_q = serve(d_q, (send_3,))
    send_4.go(send_3)
    d_q, d_k, _ = tie(d_q, d_k, send_3.finish())
    d_kv = jnp.concatenate([d_k[0], d_k[1], d_v[0], d_v[1]], axis=1)
    d_kv_t = swap(other_rows(d_kv, row))
    d_kv_own = own_rows(d_kv, row)
    d_kv = d_kv_own + d_kv_t
    d_key = d_kv[:, :narrow].reshape(OWN, -1, HEAD_SIZE)
    first, second = d_key[..., :HALF], d_key[..., HALF:]
    d_key = jnp.concatenate([first * cosine + second * sine, second * cosine - first * sine], axis=-1)
    d_kv = jnp.concatenate([d_key.reshape(OWN, narrow).astype(BF16), d_kv[:, narrow:].astype(BF16)], axis=1)
    d_qkv = jnp.concatenate([d_q, d_kv], axis=1)
    d_qkv_t = swap(d_qkv)
    last = jnp.concatenate(
        [
            (dot_right(d_q, query_weight) + dot_right(d_kv, wkv)).astype(BF16),
            (dot_right(d_q, wq_o) + dot_right(d_kv, wkv_o)).astype(BF16),
        ],
        axis=1,
    )
    last, d_qkv_t = tie(last, d_qkv_t)
    last_came = cross(last)
    last, first_z.keep, send_1.total = tie(last, first_z.keep, send_1.total)
    send_5 = Summed(
        [
            (sided(dh_m, dh_t, side, count), o[None], o_t[None], 0),
            (sided(xn_m, xn_t, side, count), d_qkv[None], d_qkv_t[None], 0),
        ],
        flip,
        count,
    )
    send_5.begin(last)
    one, send_5.keep = tie(one, send_5.keep)
    cut = one.shape[2]
    mix = jnp.concatenate(
        [
            (dot_plain(one[0], w_down[:cut]) + dot_plain(two[0], w_down[cut:])).astype(BF16),
            (dot_plain(one[0], wd_o[:cut]) + dot_plain(two[0], wd_o[cut:])).astype(BF16),
        ],
        axis=1,
    )
    mix = serve(mix, (send_4,))
    send_5.go(send_4)
    mix, send_2.total, _ = tie(mix, send_2.total, send_4.finish())

    last_came, mix, send_3.total = tie(last_came, mix, send_3.total)
    mix_came = cross(mix)
    d_xn = last.astype(F32) + last_came.astype(F32)
    d_xn_m, d_xn_o = d_xn[:, :width], d_xn[:, width:]
    unit_m, unit_o = x_m * inv_one, x_o * inv_one
    e_m, e_o = d_xn_m * gains[0], d_xn_o * gains_o[0]
    mean = (
        jnp.sum(e_m * unit_m, axis=-1, keepdims=True) + jnp.sum(e_o * unit_o, axis=-1, keepdims=True)
    ) / MODEL_WIDTH
    gg_attn_m = jnp.sum(d_xn_m * unit_m, axis=0)
    gg_attn_o = jnp.sum(d_xn_o * unit_o, axis=0)
    d_tok_m = d_hid_m + inv_one * (e_m - unit_m * mean)
    d_tok_o = d_hid_o + inv_one * (e_o - unit_o * mean)
    d_tok_t = swap(d_tok_o)
    gg = jnp.stack([gg_attn_m, gg_mlp_m]) + swap(jnp.stack([gg_attn_o, gg_mlp_o]))
    gg, send_4.total = tie(gg, send_4.total)
    gg = lax.psum_scatter(gg, "dp", scatter_dimension=1, tiled=True)
    d_tokens = merge_rows(d_tok_m, d_tok_t, row)

    d_tokens = serve(d_tokens, (send_5,))
    first_z.go(send_5)
    send_6.go(send_5)
    d_tokens, mix_came, _ = tie(d_tokens, mix_came, send_5.finish())

    mixed_all = mix.astype(F32) + mix_came.astype(F32)
    out_m = (hidden_m + mixed_all[:, :width]).astype(BF16)
    out_o = (hidden_o + mixed_all[:, width:]).astype(BF16)
    mixed = merge_rows(out_m, swap(out_o), row)

    mixed, send_6.came = tie(mixed, send_6.came)
    send_6.finish()
    first_z.total = first_z.keep.astype(F32) + first_z.came.astype(F32)
    got = [h.total.astype(F32) for h in (send_1, send_2, send_3, send_4, first_z, send_6, send_5)]
    gw_down = jnp.concatenate([got[0].T, got[1].T], axis=0)
    gw_gate = jnp.concatenate([got[2], got[3]], axis=1)
    gw_up = jnp.concatenate([got[4], got[5]], axis=1)
    gw_o, gw_qkv = got[6][:, : o.shape[1]].T, got[6][:, o.shape[1] :]
    return (
        mixed,
        d_tokens,
        gg[0],
        gw_qkv[:, :wide],
        gw_qkv[:, wide : wide + narrow],
        gw_qkv[:, wide + narrow :],
        gw_o,
        gg[1],
        gw_gate,
        gw_up,
        gw_down,
    )


def solution(mesh):
    count = mesh.shape["dp"]
    placed = (
        P("dp", "row"),
        P("dp"),
        P("dp", "row"),
        P("row"),
        P("row", "col"),
        P("row", "col"),
        P("row", "col"),
        P("col", "row"),
        P("row"),
        P("row", "col"),
        P("row", "col"),
        P("col", "row"),
    )

    def body(*args):
        return shards(count, *args)

    return jax.shard_map(
        body,
        mesh=mesh,
        in_specs=placed,
        out_specs=(
            P("dp", "row"),
            P("dp", "row"),
            P(("row", "dp")),
            P(("row", "dp"), "col"),
            P(("row", "dp"), "col"),
            P(("row", "dp"), "col"),
            P("col", ("row", "dp")),
            P(("row", "dp")),
            P(("row", "dp"), "col"),
            P(("row", "dp"), "col"),
            P("col", ("row", "dp")),
        ),
        check_vma=False,
    )
```

```python
import functools
import math

import jax
import jax.numpy as jnp
from jax import lax
from jax.experimental import pallas as pl
from jax.experimental.pallas import tpu as pltpu
from jax.sharding import PartitionSpec as P

MODEL_WIDTH = 2048
QUERY_HEADS = 32
KEY_VALUE_HEADS = 4
HEAD_SIZE = 64
SEQ = 1024

EPS = 1e-05
THETA = 10000.0
HALF = HEAD_SIZE // 2
CHUNK = SEQ // 4
OWN = SEQ // 2
PAIR = 2 * HEAD_SIZE
SCALE = HEAD_SIZE ** (-0.5)
NEG = -1e30
F32 = jnp.float32
BF16 = jnp.bfloat16


def dot_plain(left, right):
    return jnp.dot(left, right, preferred_element_type=F32)


def dot_right(left, right):
    return lax.dot_general(left, right, (((1,), (1,)), ((), ())), preferred_element_type=F32)


def dot_left(left, right):
    return lax.dot_general(left, right, (((0,), (0,)), ((), ())), preferred_element_type=F32)


def own_rows(value, row):
    a, b, c, d = (value[i * CHUNK : (i + 1) * CHUNK] for i in range(4))
    return jnp.concatenate([jnp.where(row == 0, a, b), jnp.where(row == 0, d, c)], axis=0)


def other_rows(value, row):
    a, b, c, d = (value[i * CHUNK : (i + 1) * CHUNK] for i in range(4))
    return jnp.concatenate([jnp.where(row == 0, b, a), jnp.where(row == 0, c, d)], axis=0)


def merge_rows(own, other, row):
    a, b = own[:CHUNK], own[CHUNK:]
    c, d = other[:CHUNK], other[CHUNK:]
    return jnp.concatenate(
        [
            jnp.where(row == 0, a, c),
            jnp.where(row == 0, c, a),
            jnp.where(row == 0, d, b),
            jnp.where(row == 0, b, d),
        ],
        axis=0,
    )


def chunk_bias(start_ref, bias, row):
    for c in range(2):
        place = jnp.where(row == 0, 3 * c, 1 + c) * CHUNK
        lanes = slice(c * CHUNK, (c + 1) * CHUNK)
        keys = lax.broadcasted_iota(jnp.int32, (SEQ, CHUNK), 0)
        queries = lax.broadcasted_iota(jnp.int32, (SEQ, CHUNK), 1) + place
        allowed = (keys >= start_ref[:, lanes]) & (keys <= queries)
        bias[:, lanes] = jnp.where(allowed, 0.0, NEG)


def place_keys(own_ref, other_ref, row, put):
    @pl.when(row == 0)
    def _():
        for i, (ref, half) in enumerate(((own_ref, 0), (other_ref, 0), (other_ref, 1), (own_ref, 1))):
            put(i, ref[half * CHUNK : (half + 1) * CHUNK, :])

    @pl.when(row == 1)
    def _():
        for i, (ref, half) in enumerate(((other_ref, 0), (own_ref, 0), (own_ref, 1), (other_ref, 1))):
            put(i, ref[half * CHUNK : (half + 1) * CHUNK, :])


def attend_kernel(
    group, row_ref, q_ref, cos_ref, sin_ref, start_ref, own_ref, other_ref, o_ref, lse_ref, qt_ref, bias, keys, values_t
):
    step = pl.program_id(0)
    row = row_ref[0]

    @pl.when(step == 0)
    def _():
        chunk_bias(start_ref, bias, row)

        def put(i, block):
            span = slice(i * CHUNK, (i + 1) * CHUNK)
            lanes = slice(group * HEAD_SIZE, (group + 1) * HEAD_SIZE)
            keys[span, :] = block[:, lanes]
            values_t[:, span] = jnp.transpose(block[:, PAIR:].astype(F32)).astype(BF16)[lanes]

        place_keys(own_ref, other_ref, row, put)

    turned = jnp.transpose(q_ref[...])
    cosine, sine = cos_ref[...], sin_ref[...]
    for h in range(2):
        a = turned[h * HEAD_SIZE : h * HEAD_SIZE + HALF]
        b = turned[h * HEAD_SIZE + HALF : (h + 1) * HEAD_SIZE]
        rot = jnp.concatenate([a * cosine - b * sine, b * cosine + a * sine], axis=0)
        qt_ref[h * HEAD_SIZE : (h + 1) * HEAD_SIZE, :] = (rot * SCALE).astype(BF16)

    def unit(c, blocks):
        lanes = slice(c * CHUNK, (c + 1) * CHUNK)
        count = blocks * CHUNK
        outs, sums = [], []
        for h in range(2):
            query = qt_ref[h * HEAD_SIZE : (h + 1) * HEAD_SIZE, lanes]
            scores = dot_plain(keys[:count, :], query) + bias[:count, lanes]
            top = jnp.max(scores, axis=0, keepdims=True)
            expo = jnp.exp(scores - top)
            total = jnp.sum(expo, axis=0, keepdims=True)
            head = dot_plain(values_t[:, :count], expo.astype(BF16))
            outs.append(head * (1.0 / total))
            sums.append(top + jnp.log(total))
        o_ref[lanes, :] = jnp.transpose(jnp.concatenate(outs, axis=0)).astype(BF16)
        lse_ref[0, :, lanes] = jnp.concatenate(sums, axis=0)

    @pl.when(row == 0)
    def _():
        unit(0, 1)
        unit(1, 4)

    @pl.when(row == 1)
    def _():
        unit(0, 2)
        unit(1, 3)


def attend(group, row, q, cosine, sine, start, own_kv, other_kv):
    pairs = q.shape[1] // (2 * PAIR)
    whole = lambda shape: pl.BlockSpec(shape, lambda i: (0,) * len(shape))
    return pl.pallas_call(
        functools.partial(attend_kernel, group),
        grid=(pairs,),
        in_specs=[
            pl.BlockSpec(memory_space=pltpu.SMEM),
            pl.BlockSpec((OWN, PAIR), lambda i: (0, i + group * pairs)),
            whole((HALF, OWN)),
            whole((HALF, OWN)),
            whole((1, OWN)),
            whole((OWN, 2 * PAIR)),
            whole((OWN, 2 * PAIR)),
        ],
        out_specs=[
            pl.BlockSpec((OWN, PAIR), lambda i: (0, i)),
            pl.BlockSpec((1, 2, OWN), lambda i: (i, 0, 0)),
            pl.BlockSpec((PAIR, OWN), lambda i: (i, 0)),
        ],
        out_shape=[
            jax.ShapeDtypeStruct((OWN, pairs * PAIR), BF16),
            jax.ShapeDtypeStruct((pairs, 2, OWN), F32),
            jax.ShapeDtypeStruct((pairs * PAIR, OWN), BF16),
        ],
        scratch_shapes=[
            pltpu.VMEM((SEQ, OWN), F32),
            pltpu.VMEM((SEQ, HEAD_SIZE), BF16),
            pltpu.VMEM((HEAD_SIZE, SEQ), BF16),
        ],
        compiler_params=pltpu.CompilerParams(vmem_limit_bytes=40 * 1024 * 1024),
        cost_estimate=pl.CostEstimate(flops=10_000_000_000, bytes_accessed=4_000_000, transcendentals=0),
        name="attend",
    )(row, q, cosine, sine, start, own_kv, other_kv)


def attend_back_kernel(
    row_ref,
    qt_ref,
    do_ref,
    o_ref,
    lse_ref,
    cos_ref,
    sin_ref,
    start_ref,
    own_ref,
    other_ref,
    dq_ref,
    dk_ref,
    dv_ref,
    bias,
    keys,
    keys_t,
    values,
):
    step = pl.program_id(0)
    kv = step // 4
    row = row_ref[0]

    @pl.when(step == 0)
    def _():
        chunk_bias(start_ref, bias, row)

        def put(i, block):
            span = slice(i * CHUNK, (i + 1) * CHUNK)
            for h in range(2):
                keys[h, span, :] = block[:, h * HEAD_SIZE : (h + 1) * HEAD_SIZE]
                values[h, span, :] = block[:, PAIR + h * HEAD_SIZE : PAIR + (h + 1) * HEAD_SIZE]
            turned = jnp.transpose(block[:, :PAIR].astype(F32)).astype(BF16)
            for h in range(2):
                keys_t[h, :, span] = turned[h * HEAD_SIZE : (h + 1) * HEAD_SIZE]

        place_keys(own_ref, other_ref, row, put)

    @pl.when(step % 4 == 0)
    def _():
        dk_ref[...] = jnp.zeros_like(dk_ref)
        dv_ref[...] = jnp.zeros_like(dv_ref)

    grad = do_ref[...].astype(F32)
    grad_t = jnp.transpose(grad)
    mixed_t = jnp.transpose(grad * o_ref[...].astype(F32))
    cosine, sine = cos_ref[...], sin_ref[...]

    def unit(c, blocks):
        lanes = slice(c * CHUNK, (c + 1) * CHUNK)
        count = blocks * CHUNK
        outs = []
        for h in range(2):
            rows = slice(h * HEAD_SIZE, (h + 1) * HEAD_SIZE)
            query = qt_ref[rows, lanes]
            d_head = grad_t[rows, lanes].astype(BF16)
            delta = jnp.sum(mixed_t[rows, lanes], axis=0, keepdims=True)
            scores = dot_plain(keys[kv, :count, :], query) + bias[:count, lanes]
            probs = jnp.exp(scores - lse_ref[0, h : h + 1, lanes])
            dv_ref[0, :count, :] += dot_right(probs.astype(BF16), d_head)
            d_probs = dot_plain(values[kv, :count, :], d_head)
            d_raw = (probs * (d_probs - delta)).astype(BF16)
            d_query = dot_plain(keys_t[kv, :, :count], d_raw) * SCALE
            dk_ref[0, :count, :] += dot_right(d_raw, query)
            a, b = d_query[:HALF], d_query[HALF:]
            co, si = cosine[:, lanes], sine[:, lanes]
            outs.append(a * co + b * si)
            outs.append(b * co - a * si)
        dq_ref[lanes, :] = jnp.transpose(jnp.concatenate(outs, axis=0)).astype(BF16)

    @pl.when(row == 0)
    def _():
        unit(0, 1)
        unit(1, 4)

    @pl.when(row == 1)
    def _():
        unit(0, 2)
        unit(1, 3)


def attend_back(row, qt, d_o, o, lse, cosine, sine, start, own_kv, other_kv):
    heads = qt.shape[0] // HEAD_SIZE
    pairs = heads // 2
    whole = lambda shape: pl.BlockSpec(shape, lambda i: (0,) * len(shape))
    return pl.pallas_call(
        attend_back_kernel,
        grid=(pairs,),
        in_specs=[
            pl.BlockSpec(memory_space=pltpu.SMEM),
            pl.BlockSpec((PAIR, OWN), lambda i: (i, 0)),
            pl.BlockSpec((OWN, PAIR), lambda i: (0, i)),
            pl.BlockSpec((OWN, PAIR), lambda i: (0, i)),
            pl.BlockSpec((1, 2, OWN), lambda i: (i, 0, 0)),
            whole((HALF, OWN)),
            whole((HALF, OWN)),
            whole((1, OWN)),
            whole((OWN, 2 * PAIR)),
            whole((OWN, 2 * PAIR)),
        ],
        out_specs=[
            pl.BlockSpec((OWN, PAIR), lambda i: (0, i)),
            pl.BlockSpec((1, SEQ, HEAD_SIZE), lambda i: (i // 4, 0, 0)),
            pl.BlockSpec((1, SEQ, HEAD_SIZE), lambda i: (i // 4, 0, 0)),
        ],
        out_shape=[
            jax.ShapeDtypeStruct((OWN, heads * HEAD_SIZE), BF16),
            jax.ShapeDtypeStruct((2, SEQ, HEAD_SIZE), F32),
            jax.ShapeDtypeStruct((2, SEQ, HEAD_SIZE), F32),
        ],
        scratch_shapes=[
            pltpu.VMEM((SEQ, OWN), F32),
            pltpu.VMEM((2, SEQ, HEAD_SIZE), BF16),
            pltpu.VMEM((2, HEAD_SIZE, SEQ), BF16),
            pltpu.VMEM((2, SEQ, HEAD_SIZE), BF16),
        ],
        compiler_params=pltpu.CompilerParams(vmem_limit_bytes=40 * 1024 * 1024),
        cost_estimate=pl.CostEstimate(flops=20_000_000_000, bytes_accessed=8_000_000, transcendentals=0),
        name="attend_back",
    )(row, qt, d_o, o, lse, cosine, sine, start, own_kv, other_kv)


def hidden_units_kernel(
    xm_ref, xo_ref, cm_ref, co_ref, gm_ref, go_ref, um_ref, uo_ref, dm_ref, do_ref, out_ref
):
    gate = dot_plain(xm_ref[...], gm_ref[...]) + dot_plain(xo_ref[...], go_ref[...])
    up = dot_plain(xm_ref[...], um_ref[...]) + dot_plain(xo_ref[...], uo_ref[...])
    d_act = dot_right(cm_ref[...], dm_ref[...]) + dot_right(co_ref[...], do_ref[...])
    sigma = jax.nn.sigmoid(gate)
    swish = gate * sigma
    out_ref[0] = (swish * up).astype(BF16)
    out_ref[1] = (d_act * up * (sigma * (1.0 + gate * (1.0 - sigma)))).astype(BF16)
    out_ref[2] = (d_act * swish).astype(BF16)


def hidden_units(first, tiles, xm, xo, cm, co, gm, go, um, uo, dm, do):
    rows, depth = xm.shape
    tile = 256
    wide = tiles * tile
    full = pl.BlockSpec((rows, depth), lambda i: (0, 0))
    column = pl.BlockSpec((depth, tile), lambda i: (0, i + first))
    line = pl.BlockSpec((tile, depth), lambda i: (i + first, 0))
    out = pl.BlockSpec((3, rows, tile), lambda i: (0, 0, i))
    return pl.pallas_call(
        hidden_units_kernel,
        grid=(tiles,),
        in_specs=[full] * 4 + [column] * 4 + [line] * 2,
        out_specs=out,
        out_shape=jax.ShapeDtypeStruct((3, rows, wide), BF16),
        compiler_params=pltpu.CompilerParams(vmem_limit_bytes=48 * 1024 * 1024),
        cost_estimate=pl.CostEstimate(flops=12 * rows * depth * wide, bytes_accessed=12 * depth * wide, transcendentals=0),
        name="hidden_units",
    )(xm, xo, cm, co, gm, go, um, uo, dm, do)


def input_grad_kernel(a_ref, b_ref, gm_ref, um_ref, go_ref, uo_ref, out_ref):
    cut = a_ref.shape[2]

    def fill(g_ref, u_ref):
        total = dot_right(a_ref[1], g_ref[:, :cut]) + dot_right(b_ref[1], g_ref[:, cut:])
        total += dot_right(a_ref[2], u_ref[:, :cut]) + dot_right(b_ref[2], u_ref[:, cut:])
        out_ref[...] = total.astype(BF16)

    step, half = pl.program_id(0), pl.num_programs(0) // 2
    pl.when(step < half)(lambda: fill(gm_ref, um_ref))
    pl.when(step >= half)(lambda: fill(go_ref, uo_ref))


def input_grad(a, b, gm, um, go, uo):
    rows = a.shape[1]
    depth, wide = gm.shape
    tile = 256
    tiles = depth // tile
    full = lambda value: pl.BlockSpec(value.shape, lambda i: (0, 0, 0))
    line_m = pl.BlockSpec((tile, wide), lambda i: (jnp.minimum(i, tiles - 1), 0))
    line_o = pl.BlockSpec((tile, wide), lambda i: (jnp.maximum(i - tiles, 0), 0))
    return pl.pallas_call(
        input_grad_kernel,
        grid=(2 * tiles,),
        in_specs=[full(a), full(b), line_m, line_m, line_o, line_o],
        out_specs=pl.BlockSpec((rows, tile), lambda i: (0, i)),
        out_shape=jax.ShapeDtypeStruct((rows, 2 * depth), BF16),
        compiler_params=pltpu.CompilerParams(vmem_limit_bytes=48 * 1024 * 1024),
        cost_estimate=pl.CostEstimate(flops=8 * rows * depth * wide, bytes_accessed=8 * depth * wide, transcendentals=0),
        name="input_grad",
    )(a, b, gm, um, go, uo)


def product_kernel(counts, *refs):
    pieces = len(counts)
    lefts, owns, others = (refs[i * pieces : (i + 1) * pieces] for i in range(3))
    send_ref, keep_ref = refs[3 * pieces :]
    step, first = pl.program_id(0), 0
    for left, own, other, count in zip(lefts, owns, others, counts):

        @pl.when((step >= first) & (step < first + count))
        def _(left=left, own=own, other=other):
            tokens, half = own.shape[1], left.shape[0] // 2
            total = dot_plain(left[:, :tokens], own[0]) + dot_plain(left[:, tokens:], other[0])
            send_ref[...] = total[:half].astype(BF16)
            keep_ref[...] = total[half:].astype(BF16)

        first += count


def product(pieces):
    tile = 256
    counts = [own.shape[2] // tile for _, own, _, _ in pieces]
    rows, tokens = pieces[0][0].shape
    owns, others = [], []
    first = 0
    for (_, own, other, index), count in zip(pieces, counts):
        place = lambda i, first=first, count=count: jnp.clip(i - first, 0, count - 1)
        owns.append(pl.BlockSpec((1, own.shape[1], tile), lambda i, index=index, place=place: (index, 0, place(i))))
        others.append(pl.BlockSpec((1, other.shape[1], tile), lambda i, index=index, place=place: (index, 0, place(i))))
        first += count
    return pl.pallas_call(
        functools.partial(product_kernel, counts),
        grid=(first,),
        in_specs=[pl.BlockSpec((rows, tokens), lambda i: (0, 0))] * len(pieces) + owns + others,
        out_specs=[pl.BlockSpec((rows // 2, tile), lambda i: (0, i))] * 2,
        out_shape=[jax.ShapeDtypeStruct((rows // 2, first * tile), BF16)] * 2,
        compiler_params=pltpu.CompilerParams(vmem_limit_bytes=40 * 1024 * 1024),
        cost_estimate=pl.CostEstimate(flops=4 * rows * tokens * first * tile, bytes_accessed=6 * rows * first * tile, transcendentals=0),
        name="product",
    )(*[p[0] for p in pieces], *[p[1] for p in pieces], *[p[2] for p in pieces])


def sided_kernel(side_ref, own_ref, other_ref, out_ref):
    tokens = own_ref.shape[0]
    out_ref[:, :tokens] = jnp.transpose(own_ref[...])
    out_ref[:, tokens:] = jnp.transpose(other_ref[...])


def sided(own, other, side, count):
    tokens, wide = own.shape
    width = wide // count
    if width % 128:
        blocks = jnp.concatenate([own, other], axis=0).T.reshape(count // 2, 2, width, 2 * tokens)
        near = jnp.where(side == 0, blocks[:, 0], blocks[:, 1])
        far = jnp.where(side == 0, blocks[:, 1], blocks[:, 0])
        return jnp.concatenate([far, near], axis=0).reshape(wide, 2 * tokens)
    column = pl.BlockSpec((tokens, width), lambda i, side: (0, i))
    return pl.pallas_call(
        sided_kernel,
        grid_spec=pltpu.PrefetchScalarGridSpec(
            num_scalar_prefetch=1,
            grid=(count,),
            in_specs=[column, column],
            out_specs=pl.BlockSpec(
                (width, 2 * tokens), lambda i, side: (i // 2 + jnp.where(i % 2 == side[0], count // 2, 0), 0)
            ),
        ),
        out_shape=jax.ShapeDtypeStruct((wide, 2 * tokens), BF16),
        compiler_params=pltpu.CompilerParams(vmem_limit_bytes=40 * 1024 * 1024),
        cost_estimate=pl.CostEstimate(flops=1000, bytes_accessed=8 * tokens * wide, transcendentals=0),
        name="sided",
    )(side.astype(jnp.int32).reshape(1), own, other)


class Summed:
    def __init__(self, pieces, flip, count):
        self.pieces, self.flip, self.count = pieces, flip, count

    def begin(self, *deps):
        left, *others = self.pieces[0]
        left, *_ = tie(left, *deps)
        self.send, self.keep = product([(left, *others), *self.pieces[1:]])
        return self.keep

    def go(self, after=None):
        if after is not None:
            self.send, after.came = tie(self.send, after.came)
        self.came = self.flip(self.send)

    def scatter(self, value):
        groups = [list(range(side, self.count, 2)) for side in range(2)]
        return lax.psum_scatter(value, "dp", scatter_dimension=0, axis_index_groups=groups, tiled=True)

    def finish(self):
        total = (self.keep.astype(F32) + self.came.astype(F32)).astype(BF16)
        self.total = self.scatter(total)
        return total


def half_of(value, upper, axis=0):
    size = value.shape[axis] // 2
    return lax.slice_in_dim(value, size if upper else 0, 2 * size if upper else size, axis=axis)


def tie(*values):
    return lax.optimization_barrier(values)


def serve(value, done=(), ready=()):
    out = tie(value, *[h.came for h in done], *ready)
    for h, came in zip(done, out[1:]):
        h.came = came
    return out[0]


def shards(
    count,
    tokens,
    segment_ids,
    cotangent,
    g_attn,
    query_weight,
    key_weight,
    value_weight,
    w_o,
    g_mlp,
    w_gate,
    w_up,
    w_down,
):
    row = lax.axis_index("row")
    side = lax.axis_index("dp") & 1
    low = side == 0

    def swap(value):
        return lax.ppermute(value, "row", [(0, 1), (1, 0)])

    def cross(value):
        return lax.ppermute(value, "col", [(0, 1), (1, 0)])

    def flip(value):
        return lax.ppermute(value, "dp", [(i, i ^ 1) for i in range(count)])

    half = w_o.shape[0] // 2
    far_a = cross(jnp.where(low, w_o[:half], w_o[half:]))
    x_m = own_rows(tokens, row)
    x_o = swap(other_rows(tokens, row))
    wkv = jnp.concatenate([key_weight, value_weight], axis=1)
    wkv_o = swap(wkv)
    wq_o = swap(query_weight)
    gains = jnp.stack([g_attn, g_mlp])
    gains_o = swap(gains)
    x_o, wkv_o, wq_o, gains_o = tie(x_o, wkv_o, wq_o, gains_o)
    x_m, x_o = x_m.astype(F32), x_o.astype(F32)
    square = jnp.sum(x_m * x_m, axis=-1, keepdims=True) + jnp.sum(x_o * x_o, axis=-1, keepdims=True)
    inv_one = lax.rsqrt(square / MODEL_WIDTH + EPS)
    xn_m = (x_m * inv_one * gains[0]).astype(BF16)
    xn_o = (x_o * inv_one * gains_o[0]).astype(BF16)

    start = jnp.sum((segment_ids[None, :] < segment_ids[:, None]).astype(jnp.int32), axis=1)
    index = lax.iota(jnp.int32, SEQ)
    start_own = own_rows(start, row)
    places = own_rows(index, row) - start_own
    freq = jnp.exp(jnp.arange(HALF, dtype=F32) * (-2.0 * math.log(THETA) / HEAD_SIZE))
    turn_t = freq[:, None] * places.astype(F32)[None, :]
    cosine_t, sine_t = jnp.cos(turn_t), jnp.sin(turn_t)
    cosine, sine = cosine_t.T[:, None, :], sine_t.T[:, None, :]

    kv = dot_plain(xn_m, wkv) + dot_plain(xn_o, wkv_o)
    narrow = key_weight.shape[1]
    wide = query_weight.shape[1]
    kp = kv[:, :narrow].reshape(OWN, -1, HEAD_SIZE)
    first, second = kp[..., :HALF], kp[..., HALF:]
    key = jnp.concatenate([first * cosine - second * sine, second * cosine + first * sine], axis=-1)
    own_kv = jnp.concatenate([key.reshape(OWN, narrow), kv[:, narrow:]], axis=1).astype(BF16)
    other_kv = swap(own_kv)
    xn_m, xn_o, own_kv = tie(xn_m, xn_o, own_kv)
    q = dot_plain(xn_m, query_weight) + dot_plain(xn_o, wq_o)

    cotangent, w_gate, w_up, w_down, w_o, xn_o = tie(cotangent, w_gate, w_up, w_down, w_o, xn_o)
    wg_o = swap(w_gate)
    wu_o = swap(w_up)
    w_o_o = swap(w_o)
    c_m = own_rows(cotangent, row)
    c_t = other_rows(cotangent, row)
    q, far_a, other_kv, c_m, c_t = tie(q, far_a, other_kv, c_m, c_t)
    far_b = flip(far_a)
    row_arg = row.astype(jnp.int32).reshape(1)
    start_arg = start_own.reshape(1, OWN)
    o_1, lse_1, qt_1 = attend(0, row_arg, q, cosine_t, sine_t, start_arg, own_kv, other_kv)
    o_1, q, wg_o, wu_o, w_o_o, w_down, c_t, far_a = tie(o_1, q, wg_o, wu_o, w_o_o, w_down, c_t, far_a)
    o_x1 = cross(o_1)
    c_o = swap(c_t)
    wd_o = swap(w_down)
    far_ao = swap(far_a)
    o_2, lse_2, qt_2 = attend(1, row_arg, q, cosine_t, sine_t, start_arg, own_kv, other_kv)
    o_2, o_1, c_o, wd_o, far_ao, xn_o = tie(o_2, o_1, c_o, wd_o, far_ao, xn_o)
    o_x2 = cross(o_2)

    near_m = dot_plain(o_1, w_o[:half]) + dot_plain(o_2, w_o[half:])
    near_o = dot_plain(o_1, w_o_o[:half]) + dot_plain(o_2, w_o_o[half:])
    both = lambda own, other: jnp.concatenate([own, other], axis=0)
    c_y = sided(c_m, c_t, side, count)
    o = jnp.concatenate([o_1, o_2], axis=1)
    o_t = swap(o)
    qt = jnp.concatenate([qt_1, qt_2], axis=0)
    lse = jnp.concatenate([lse_1, lse_2], axis=0)
    near_m, near_o, far_b = tie(near_m, near_o, far_b)
    far_bo = swap(far_b)
    xn_t = swap(xn_o)
    c_y, qt, lse, far_b, far_bo, o_x1 = tie(c_y, qt, lse, far_b, far_bo, o_x1)
    pick = lambda a, b: (jnp.where(low, a, b), jnp.where(low, b, a))
    far_1, far_2 = pick(far_a, far_b)
    far_1o, far_2o = pick(far_ao, far_bo)
    mid_m, mid_o = dot_plain(o_x1, far_1), dot_plain(o_x1, far_1o)
    mid_m, mid_o, o_t, xn_t, o_x2 = tie(mid_m, mid_o, o_t, xn_t, o_x2)
    hidden_m = x_m + (near_m + (mid_m + dot_plain(o_x2, far_2)))
    hidden_o = x_o + (near_o + (mid_o + dot_plain(o_x2, far_2o)))
    square = jnp.sum(hidden_m * hidden_m, axis=-1, keepdims=True) + jnp.sum(
        hidden_o * hidden_o, axis=-1, keepdims=True
    )
    inv_two = lax.rsqrt(square / MODEL_WIDTH + EPS)
    unit_m, unit_o = hidden_m * inv_two, hidden_o * inv_two
    xn2_m = (unit_m * gains[1]).astype(BF16)
    xn2_o = (unit_o * gains_o[1]).astype(BF16)

    xn2_t = swap(xn2_o)
    tiles = w_gate.shape[1] // 256
    operands = (c_m, c_o, w_gate, wg_o, w_up, wu_o, w_down, wd_o)
    one = hidden_units(0, tiles - tiles // 2, xn2_m, xn2_o, *operands)
    one_t = swap(one)
    one, xn2_m2 = tie(one, xn2_m)
    two = hidden_units(tiles - tiles // 2, tiles // 2, xn2_m2, xn2_o, *operands)
    two, one_t, xn2_t = tie(two, one_t, xn2_t)
    two_t = swap(two)

    two, xn2_m2 = tie(two, xn2_m2)
    xn2_y = sided(xn2_m2, xn2_t, side, count)
    first_z = Summed([(xn2_y, one, one_t, 2)], flip, count)
    first_z.begin()
    first_z.send = first_z.scatter(first_z.send)
    first_z.keep, two_t = tie(first_z.keep, two_t)
    send_1 = Summed([(c_y, one, one_t, 0), (c_y, two, two_t, 0)], flip, count)
    send_1.begin(first_z.keep)
    send_1.go()
    send_1.keep, two_late, first_z.keep = tie(send_1.keep, two, first_z.keep)
    first_z.keep = first_z.scatter(first_z.keep)
    part = input_grad(one, two_late, w_gate, w_up, wg_o, wu_o)
    came = cross(part)
    send_2 = Summed([(xn2_y, one, one_t, 1)], flip, count)
    send_2.begin(part)
    send_3 = Summed([(xn2_y, two, two_t, 1), (xn2_y, two, two_t, 2)], flip, count)
    send_3.begin(send_2.keep)
    came, first_z.send, part = tie(came, first_z.send, part, send_3.keep)[:3]
    came = serve(came, (send_1,))
    send_2.go(send_1)
    came, _ = tie(came, send_1.finish())

    width = tokens.shape[1]
    d_xn2 = part.astype(F32) + came.astype(F32)
    d_xn2_m, d_xn2_o = d_xn2[:, :width], d_xn2[:, width:]
    e_m, e_o = d_xn2_m * gains[1], d_xn2_o * gains_o[1]
    mean = (
        jnp.sum(e_m * unit_m, axis=-1, keepdims=True) + jnp.sum(e_o * unit_o, axis=-1, keepdims=True)
    ) / MODEL_WIDTH
    gg_mlp_m = jnp.sum(d_xn2_m * unit_m, axis=0)
    gg_mlp_o = jnp.sum(d_xn2_o * unit_o, axis=0)
    d_hid_m = c_m.astype(F32) + inv_two * (e_m - unit_m * mean)
    d_hid_o = c_o.astype(F32) + inv_two * (e_o - unit_o * mean)
    dh_m, dh_o = d_hid_m.astype(BF16), d_hid_o.astype(BF16)
    dh_t = swap(dh_o)
    d_o = (dot_right(dh_m, w_o) + dot_right(dh_o, w_o_o)).astype(BF16)
    d_o, dh_t, first_z.keep = tie(d_o, dh_t, first_z.keep)
    d_o = serve(d_o, (send_2,))
    send_3.go(send_2)
    d_o, _ = tie(d_o, send_2.finish())

    d_q, d_k, d_v = attend_back(row_arg, qt, d_o, o, lse, cosine_t, sine_t, start_arg, own_kv, other_kv)
    d_kv = jnp.concatenate([d_k[0], d_k[1], d_v[0], d_v[1]], axis=1)
    d_kv_t = swap(other_rows(d_kv, row))
    d_kv_own = own_rows(d_kv, row)
    d_kv = d_kv_own + d_kv_t
    d_key = d_kv[:, :narrow].reshape(OWN, -1, HEAD_SIZE)
    first, second = d_key[..., :HALF], d_key[..., HALF:]
    d_key = jnp.concatenate([first * cosine + second * sine, second * cosine - first * sine], axis=-1)
    d_kv = jnp.concatenate([d_key.reshape(OWN, narrow).astype(BF16), d_kv[:, narrow:].astype(BF16)], axis=1)
    d_qkv = jnp.concatenate([d_q, d_kv], axis=1)
    d_qkv_t = swap(d_qkv)
    last = jnp.concatenate(
        [
            (dot_right(d_q, query_weight) + dot_right(d_kv, wkv)).astype(BF16),
            (dot_right(d_q, wq_o) + dot_right(d_kv, wkv_o)).astype(BF16),
        ],
        axis=1,
    )
    last, d_qkv_t = tie(last, d_qkv_t)
    last_came = cross(last)
    last, send_1.total = tie(last, send_1.total)
    send_5 = Summed(
        [
            (sided(dh_m, dh_t, side, count), o[None], o_t[None], 0),
            (sided(xn_m, xn_t, side, count), d_qkv[None], d_qkv_t[None], 0),
        ],
        flip,
        count,
    )
    send_5.begin(last)
    one, send_5.keep = tie(one, send_5.keep)
    one = serve(one, (send_3,))
    send_5.go(send_3)
    first_z.go(send_3)
    one, _ = tie(one, send_3.finish())
    cut = one.shape[2]
    mix = jnp.concatenate(
        [
            (dot_plain(one[0], w_down[:cut]) + dot_plain(two[0], w_down[cut:])).astype(BF16),
            (dot_plain(one[0], wd_o[:cut]) + dot_plain(two[0], wd_o[cut:])).astype(BF16),
        ],
        axis=1,
    )

    last_came, mix, send_2.total = tie(last_came, mix, send_2.total)
    last_came, first_z.came = tie(last_came, first_z.came)
    last_came = serve(last_came, (send_5,))
    last_came, mix, _ = tie(last_came, mix, send_5.finish())
    mix_came = cross(mix)
    d_xn = last.astype(F32) + last_came.astype(F32)
    d_xn_m, d_xn_o = d_xn[:, :width], d_xn[:, width:]
    unit_m, unit_o = x_m * inv_one, x_o * inv_one
    e_m, e_o = d_xn_m * gains[0], d_xn_o * gains_o[0]
    mean = (
        jnp.sum(e_m * unit_m, axis=-1, keepdims=True) + jnp.sum(e_o * unit_o, axis=-1, keepdims=True)
    ) / MODEL_WIDTH
    gg_attn_m = jnp.sum(d_xn_m * unit_m, axis=0)
    gg_attn_o = jnp.sum(d_xn_o * unit_o, axis=0)
    d_tok_m = d_hid_m + inv_one * (e_m - unit_m * mean)
    d_tok_o = d_hid_o + inv_one * (e_o - unit_o * mean)
    d_tok_t = swap(d_tok_o)
    gg = jnp.stack([gg_attn_m, gg_mlp_m]) + swap(jnp.stack([gg_attn_o, gg_mlp_o]))
    for bit in range(count.bit_length() - 1):
        gg = gg + lax.ppermute(gg, "dp", [(i, i ^ (1 << bit)) for i in range(count)])
    gg = lax.dynamic_slice_in_dim(gg, lax.axis_index("dp") * (width // count), width // count, axis=1)
    d_tokens = merge_rows(d_tok_m, d_tok_t, row)

    mixed_all = mix.astype(F32) + mix_came.astype(F32)
    out_m = (hidden_m + mixed_all[:, :width]).astype(BF16)
    out_o = (hidden_o + mixed_all[:, width:]).astype(BF16)
    mixed = merge_rows(out_m, swap(out_o), row)

    first_z.total = first_z.keep.astype(F32) + first_z.came.astype(F32)
    got = [h.total.astype(F32) for h in (send_1, send_2, send_3, first_z, send_5)]
    rest = two.shape[2]
    gw_down = got[0].T
    gw_gate = jnp.concatenate([got[1], got[2][:, :rest]], axis=1)
    gw_up = jnp.concatenate([got[3], got[2][:, rest:]], axis=1)
    gw_o, gw_qkv = got[4][:, : o.shape[1]].T, got[4][:, o.shape[1] :]
    return (
        mixed,
        d_tokens,
        gg[0],
        gw_qkv[:, :wide],
        gw_qkv[:, wide : wide + narrow],
        gw_qkv[:, wide + narrow :],
        gw_o,
        gg[1],
        gw_gate,
        gw_up,
        gw_down,
    )


def solution(mesh):
    count = mesh.shape["dp"]
    placed = (
        P("dp", "row"),
        P("dp"),
        P("dp", "row"),
        P("row"),
        P("row", "col"),
        P("row", "col"),
        P("row", "col"),
        P("col", "row"),
        P("row"),
        P("row", "col"),
        P("row", "col"),
        P("col", "row"),
    )

    def body(*args):
        return shards(count, *args)

    return jax.shard_map(
        body,
        mesh=mesh,
        in_specs=placed,
        out_specs=(
            P("dp", "row"),
            P("dp", "row"),
            P(("row", "dp")),
            P(("row", "dp"), "col"),
            P(("row", "dp"), "col"),
            P(("row", "dp"), "col"),
            P("col", ("row", "dp")),
            P(("row", "dp")),
            P(("row", "dp"), "col"),
            P(("row", "dp"), "col"),
            P("col", ("row", "dp")),
        ),
        check_vma=False,
    )
```

```python
import functools
import math

import jax
import jax.numpy as jnp
from jax import lax
from jax.experimental import pallas as pl
from jax.experimental.pallas import tpu as pltpu
from jax.sharding import PartitionSpec as P

MODEL_WIDTH = 2048
QUERY_HEADS = 32
KEY_VALUE_HEADS = 4
HEAD_SIZE = 64
SEQ = 1024

EPS = 1e-05
THETA = 10000.0
HALF = HEAD_SIZE // 2
CHUNK = SEQ // 4
OWN = SEQ // 2
PAIR = 2 * HEAD_SIZE
SCALE = HEAD_SIZE ** (-0.5)
NEG = -1e30
F32 = jnp.float32
BF16 = jnp.bfloat16


def dot_plain(left, right):
    return jnp.dot(left, right, preferred_element_type=F32)


def dot_right(left, right):
    return lax.dot_general(left, right, (((1,), (1,)), ((), ())), preferred_element_type=F32)


def dot_left(left, right):
    return lax.dot_general(left, right, (((0,), (0,)), ((), ())), preferred_element_type=F32)


def own_rows(value, row):
    a, b, c, d = (value[i * CHUNK : (i + 1) * CHUNK] for i in range(4))
    return jnp.concatenate([jnp.where(row == 0, a, b), jnp.where(row == 0, d, c)], axis=0)


def other_rows(value, row):
    a, b, c, d = (value[i * CHUNK : (i + 1) * CHUNK] for i in range(4))
    return jnp.concatenate([jnp.where(row == 0, b, a), jnp.where(row == 0, c, d)], axis=0)


def merge_rows(own, other, row):
    a, b = own[:CHUNK], own[CHUNK:]
    c, d = other[:CHUNK], other[CHUNK:]
    return jnp.concatenate(
        [
            jnp.where(row == 0, a, c),
            jnp.where(row == 0, c, a),
            jnp.where(row == 0, d, b),
            jnp.where(row == 0, b, d),
        ],
        axis=0,
    )


def chunk_bias(start_ref, bias, row):
    for c in range(2):
        place = jnp.where(row == 0, 3 * c, 1 + c) * CHUNK
        lanes = slice(c * CHUNK, (c + 1) * CHUNK)
        keys = lax.broadcasted_iota(jnp.int32, (SEQ, CHUNK), 0)
        queries = lax.broadcasted_iota(jnp.int32, (SEQ, CHUNK), 1) + place
        allowed = (keys >= start_ref[:, lanes]) & (keys <= queries)
        bias[:, lanes] = jnp.where(allowed, 0.0, NEG)


def place_keys(own_ref, other_ref, row, put):
    @pl.when(row == 0)
    def _():
        for i, (ref, half) in enumerate(((own_ref, 0), (other_ref, 0), (other_ref, 1), (own_ref, 1))):
            put(i, ref[half * CHUNK : (half + 1) * CHUNK, :])

    @pl.when(row == 1)
    def _():
        for i, (ref, half) in enumerate(((other_ref, 0), (own_ref, 0), (own_ref, 1), (other_ref, 1))):
            put(i, ref[half * CHUNK : (half + 1) * CHUNK, :])


def attend_kernel(
    row_ref, q_ref, cos_ref, sin_ref, start_ref, own_ref, other_ref, o_ref, lse_ref, qt_ref, bias, keys, values_t
):
    step = pl.program_id(0)
    kv = step // 4
    row = row_ref[0]

    @pl.when(step == 0)
    def _():
        chunk_bias(start_ref, bias, row)

        def put(i, block):
            span = slice(i * CHUNK, (i + 1) * CHUNK)
            for h in range(2):
                keys[h, span, :] = block[:, h * HEAD_SIZE : (h + 1) * HEAD_SIZE]
            turned = jnp.transpose(block[:, PAIR:].astype(F32)).astype(BF16)
            for h in range(2):
                values_t[h, :, span] = turned[h * HEAD_SIZE : (h + 1) * HEAD_SIZE]

        place_keys(own_ref, other_ref, row, put)

    turned = jnp.transpose(q_ref[...])
    cosine, sine = cos_ref[...], sin_ref[...]
    for h in range(2):
        a = turned[h * HEAD_SIZE : h * HEAD_SIZE + HALF]
        b = turned[h * HEAD_SIZE + HALF : (h + 1) * HEAD_SIZE]
        rot = jnp.concatenate([a * cosine - b * sine, b * cosine + a * sine], axis=0)
        qt_ref[h * HEAD_SIZE : (h + 1) * HEAD_SIZE, :] = (rot * SCALE).astype(BF16)

    def unit(c, blocks):
        lanes = slice(c * CHUNK, (c + 1) * CHUNK)
        count = blocks * CHUNK
        outs, sums = [], []
        for h in range(2):
            query = qt_ref[h * HEAD_SIZE : (h + 1) * HEAD_SIZE, lanes]
            scores = dot_plain(keys[kv, :count, :], query) + bias[:count, lanes]
            top = jnp.max(scores, axis=0, keepdims=True)
            expo = jnp.exp(scores - top)
            total = jnp.sum(expo, axis=0, keepdims=True)
            head = dot_plain(values_t[kv, :, :count], expo.astype(BF16))
            outs.append(head * (1.0 / total))
            sums.append(top + jnp.log(total))
        o_ref[lanes, :] = jnp.transpose(jnp.concatenate(outs, axis=0)).astype(BF16)
        lse_ref[0, :, lanes] = jnp.concatenate(sums, axis=0)

    @pl.when(row == 0)
    def _():
        unit(0, 1)
        unit(1, 4)

    @pl.when(row == 1)
    def _():
        unit(0, 2)
        unit(1, 3)


def attend(row, q, cosine, sine, start, own_kv, other_kv):
    heads = q.shape[1] // HEAD_SIZE
    pairs = heads // 2
    whole = lambda shape: pl.BlockSpec(shape, lambda i: (0,) * len(shape))
    return pl.pallas_call(
        attend_kernel,
        grid=(pairs,),
        in_specs=[
            pl.BlockSpec(memory_space=pltpu.SMEM),
            pl.BlockSpec((OWN, PAIR), lambda i: (0, i)),
            whole((HALF, OWN)),
            whole((HALF, OWN)),
            whole((1, OWN)),
            whole((OWN, 2 * PAIR)),
            whole((OWN, 2 * PAIR)),
        ],
        out_specs=[
            pl.BlockSpec((OWN, PAIR), lambda i: (0, i)),
            pl.BlockSpec((1, 2, OWN), lambda i: (i, 0, 0)),
            pl.BlockSpec((PAIR, OWN), lambda i: (i, 0)),
        ],
        out_shape=[
            jax.ShapeDtypeStruct((OWN, heads * HEAD_SIZE), BF16),
            jax.ShapeDtypeStruct((pairs, 2, OWN), F32),
            jax.ShapeDtypeStruct((heads * HEAD_SIZE, OWN), BF16),
        ],
        scratch_shapes=[
            pltpu.VMEM((SEQ, OWN), F32),
            pltpu.VMEM((2, SEQ, HEAD_SIZE), BF16),
            pltpu.VMEM((2, HEAD_SIZE, SEQ), BF16),
        ],
        compiler_params=pltpu.CompilerParams(vmem_limit_bytes=60 * 1024 * 1024),
        cost_estimate=pl.CostEstimate(flops=20_000_000_000, bytes_accessed=8_000_000, transcendentals=0),
        name="attend",
    )(row, q, cosine, sine, start, own_kv, other_kv)


def attend_back_kernel(
    row_ref,
    qt_ref,
    do_ref,
    o_ref,
    lse_ref,
    cos_ref,
    sin_ref,
    start_ref,
    own_ref,
    other_ref,
    dq_ref,
    dk_ref,
    dv_ref,
    bias,
    keys,
    keys_t,
    values,
):
    step = pl.program_id(0)
    kv = step // 4
    row = row_ref[0]

    @pl.when(step == 0)
    def _():
        chunk_bias(start_ref, bias, row)

        def put(i, block):
            span = slice(i * CHUNK, (i + 1) * CHUNK)
            for h in range(2):
                keys[h, span, :] = block[:, h * HEAD_SIZE : (h + 1) * HEAD_SIZE]
                values[h, span, :] = block[:, PAIR + h * HEAD_SIZE : PAIR + (h + 1) * HEAD_SIZE]
            turned = jnp.transpose(block[:, :PAIR].astype(F32)).astype(BF16)
            for h in range(2):
                keys_t[h, :, span] = turned[h * HEAD_SIZE : (h + 1) * HEAD_SIZE]

        place_keys(own_ref, other_ref, row, put)

    @pl.when(step % 4 == 0)
    def _():
        dk_ref[...] = jnp.zeros_like(dk_ref)
        dv_ref[...] = jnp.zeros_like(dv_ref)

    grad = do_ref[...].astype(F32)
    grad_t = jnp.transpose(grad)
    mixed_t = jnp.transpose(grad * o_ref[...].astype(F32))
    cosine, sine = cos_ref[...], sin_ref[...]

    def unit(c, blocks):
        lanes = slice(c * CHUNK, (c + 1) * CHUNK)
        count = blocks * CHUNK
        outs = []
        for h in range(2):
            rows = slice(h * HEAD_SIZE, (h + 1) * HEAD_SIZE)
            query = qt_ref[rows, lanes]
            d_head = grad_t[rows, lanes].astype(BF16)
            delta = jnp.sum(mixed_t[rows, lanes], axis=0, keepdims=True)
            scores = dot_plain(keys[kv, :count, :], query) + bias[:count, lanes]
            probs = jnp.exp(scores - lse_ref[0, h : h + 1, lanes])
            dv_ref[0, :count, :] += dot_right(probs.astype(BF16), d_head)
            d_probs = dot_plain(values[kv, :count, :], d_head)
            d_raw = (probs * (d_probs - delta)).astype(BF16)
            d_query = dot_plain(keys_t[kv, :, :count], d_raw) * SCALE
            dk_ref[0, :count, :] += dot_right(d_raw, query)
            a, b = d_query[:HALF], d_query[HALF:]
            co, si = cosine[:, lanes], sine[:, lanes]
            outs.append(a * co + b * si)
            outs.append(b * co - a * si)
        dq_ref[lanes, :] = jnp.transpose(jnp.concatenate(outs, axis=0)).astype(BF16)

    @pl.when(row == 0)
    def _():
        unit(0, 1)
        unit(1, 4)

    @pl.when(row == 1)
    def _():
        unit(0, 2)
        unit(1, 3)


def attend_back(row, qt, d_o, o, lse, cosine, sine, start, own_kv, other_kv):
    heads = qt.shape[0] // HEAD_SIZE
    pairs = heads // 2
    whole = lambda shape: pl.BlockSpec(shape, lambda i: (0,) * len(shape))
    return pl.pallas_call(
        attend_back_kernel,
        grid=(pairs,),
        in_specs=[
            pl.BlockSpec(memory_space=pltpu.SMEM),
            pl.BlockSpec((PAIR, OWN), lambda i: (i, 0)),
            pl.BlockSpec((OWN, PAIR), lambda i: (0, i)),
            pl.BlockSpec((OWN, PAIR), lambda i: (0, i)),
            pl.BlockSpec((1, 2, OWN), lambda i: (i, 0, 0)),
            whole((HALF, OWN)),
            whole((HALF, OWN)),
            whole((1, OWN)),
            whole((OWN, 2 * PAIR)),
            whole((OWN, 2 * PAIR)),
        ],
        out_specs=[
            pl.BlockSpec((OWN, PAIR), lambda i: (0, i)),
            pl.BlockSpec((1, SEQ, HEAD_SIZE), lambda i: (i // 4, 0, 0)),
            pl.BlockSpec((1, SEQ, HEAD_SIZE), lambda i: (i // 4, 0, 0)),
        ],
        out_shape=[
            jax.ShapeDtypeStruct((OWN, heads * HEAD_SIZE), BF16),
            jax.ShapeDtypeStruct((2, SEQ, HEAD_SIZE), F32),
            jax.ShapeDtypeStruct((2, SEQ, HEAD_SIZE), F32),
        ],
        scratch_shapes=[
            pltpu.VMEM((SEQ, OWN), F32),
            pltpu.VMEM((2, SEQ, HEAD_SIZE), BF16),
            pltpu.VMEM((2, HEAD_SIZE, SEQ), BF16),
            pltpu.VMEM((2, SEQ, HEAD_SIZE), BF16),
        ],
        compiler_params=pltpu.CompilerParams(vmem_limit_bytes=60 * 1024 * 1024),
        cost_estimate=pl.CostEstimate(flops=1000, bytes_accessed=1000, transcendentals=0),
        name="attend_back",
    )(row, qt, d_o, o, lse, cosine, sine, start, own_kv, other_kv)


def hidden_units_kernel(
    xm_ref, xo_ref, cm_ref, co_ref, gm_ref, go_ref, um_ref, uo_ref, dm_ref, do_ref, out_ref
):
    gate = dot_plain(xm_ref[...], gm_ref[...]) + dot_plain(xo_ref[...], go_ref[...])
    up = dot_plain(xm_ref[...], um_ref[...]) + dot_plain(xo_ref[...], uo_ref[...])
    d_act = dot_right(cm_ref[...], dm_ref[...]) + dot_right(co_ref[...], do_ref[...])
    sigma = jax.nn.sigmoid(gate)
    swish = gate * sigma
    out_ref[0] = (swish * up).astype(BF16)
    out_ref[1] = (d_act * up * (sigma * (1.0 + gate * (1.0 - sigma)))).astype(BF16)
    out_ref[2] = (d_act * swish).astype(BF16)


def hidden_units(first, tiles, xm, xo, cm, co, gm, go, um, uo, dm, do):
    rows, depth = xm.shape
    tile = 256
    wide = tiles * tile
    full = pl.BlockSpec((rows, depth), lambda i: (0, 0))
    column = pl.BlockSpec((depth, tile), lambda i: (0, i + first))
    line = pl.BlockSpec((tile, depth), lambda i: (i + first, 0))
    out = pl.BlockSpec((3, rows, tile), lambda i: (0, 0, i))
    return pl.pallas_call(
        hidden_units_kernel,
        grid=(tiles,),
        in_specs=[full] * 4 + [column] * 4 + [line] * 2,
        out_specs=out,
        out_shape=jax.ShapeDtypeStruct((3, rows, wide), BF16),
        compiler_params=pltpu.CompilerParams(vmem_limit_bytes=60 * 1024 * 1024),
        cost_estimate=pl.CostEstimate(flops=12 * rows * depth * wide, bytes_accessed=12 * depth * wide, transcendentals=0),
        name="hidden_units",
    )(xm, xo, cm, co, gm, go, um, uo, dm, do)


def input_grad_kernel(a_ref, b_ref, gm_ref, um_ref, go_ref, uo_ref, out_ref):
    cut = a_ref.shape[2]

    def fill(g_ref, u_ref):
        total = dot_right(a_ref[1], g_ref[:, :cut]) + dot_right(b_ref[1], g_ref[:, cut:])
        total += dot_right(a_ref[2], u_ref[:, :cut]) + dot_right(b_ref[2], u_ref[:, cut:])
        out_ref[...] = total.astype(BF16)

    step, half = pl.program_id(0), pl.num_programs(0) // 2
    pl.when(step < half)(lambda: fill(gm_ref, um_ref))
    pl.when(step >= half)(lambda: fill(go_ref, uo_ref))


def input_grad(a, b, gm, um, go, uo):
    rows = a.shape[1]
    depth, wide = gm.shape
    tile = 256
    tiles = depth // tile
    full = lambda value: pl.BlockSpec(value.shape, lambda i: (0, 0, 0))
    line_m = pl.BlockSpec((tile, wide), lambda i: (jnp.minimum(i, tiles - 1), 0))
    line_o = pl.BlockSpec((tile, wide), lambda i: (jnp.maximum(i - tiles, 0), 0))
    return pl.pallas_call(
        input_grad_kernel,
        grid=(2 * tiles,),
        in_specs=[full(a), full(b), line_m, line_m, line_o, line_o],
        out_specs=pl.BlockSpec((rows, tile), lambda i: (0, i)),
        out_shape=jax.ShapeDtypeStruct((rows, 2 * depth), BF16),
        compiler_params=pltpu.CompilerParams(vmem_limit_bytes=60 * 1024 * 1024),
        cost_estimate=pl.CostEstimate(flops=8 * rows * depth * wide, bytes_accessed=8 * depth * wide, transcendentals=0),
        name="input_grad",
    )(a, b, gm, um, go, uo)


def product_kernel(counts, *refs):
    pieces = len(counts)
    lefts, owns, others = (refs[i * pieces : (i + 1) * pieces] for i in range(3))
    send_ref, keep_ref = refs[3 * pieces :]
    step, first = pl.program_id(0), 0
    for left, own, other, count in zip(lefts, owns, others, counts):

        @pl.when((step >= first) & (step < first + count))
        def _(left=left, own=own, other=other):
            tokens, half = own.shape[1], left.shape[0] // 2
            total = dot_plain(left[:, :tokens], own[0]) + dot_plain(left[:, tokens:], other[0])
            send_ref[...] = total[:half].astype(BF16)
            keep_ref[...] = total[half:].astype(BF16)

        first += count


def product(pieces):
    tile = 256
    counts = [own.shape[2] // tile for _, own, _, _ in pieces]
    rows, tokens = pieces[0][0].shape
    owns, others = [], []
    first = 0
    for (_, own, other, index), count in zip(pieces, counts):
        place = lambda i, first=first, count=count: jnp.clip(i - first, 0, count - 1)
        owns.append(pl.BlockSpec((1, own.shape[1], tile), lambda i, index=index, place=place: (index, 0, place(i))))
        others.append(pl.BlockSpec((1, other.shape[1], tile), lambda i, index=index, place=place: (index, 0, place(i))))
        first += count
    return pl.pallas_call(
        functools.partial(product_kernel, counts),
        grid=(first,),
        in_specs=[pl.BlockSpec((rows, tokens), lambda i: (0, 0))] * len(pieces) + owns + others,
        out_specs=[pl.BlockSpec((rows // 2, tile), lambda i: (0, i))] * 2,
        out_shape=[jax.ShapeDtypeStruct((rows // 2, first * tile), BF16)] * 2,
        compiler_params=pltpu.CompilerParams(vmem_limit_bytes=60 * 1024 * 1024),
        cost_estimate=pl.CostEstimate(flops=4 * rows * tokens * first * tile, bytes_accessed=6 * rows * first * tile, transcendentals=0),
        name="product",
    )(*[p[0] for p in pieces], *[p[1] for p in pieces], *[p[2] for p in pieces])


def blend_kernel(sizes, halves, counts, transposed, *refs):
    total_a = sum(len(g) for g in sizes)
    a_refs, w_refs, out_ref = refs[:total_a], refs[total_a:-1], refs[-1]
    step, first = pl.program_id(0), 0
    for half in range(halves):

        @pl.when((step >= first) & (step < first + counts[half]))
        def _(half=half):
            total, at = None, 0
            for g, group in enumerate(sizes):
                w, low = w_refs[half * len(sizes) + g], 0
                for size in group:
                    if transposed:
                        part = dot_right(a_refs[at][0], w[:, low : low + size])
                    else:
                        part = dot_plain(a_refs[at][0], w[low : low + size, :])
                    total = part if total is None else total + part
                    low, at = low + size, at + 1
            out_ref[...] = total.astype(out_ref.dtype)

        first += counts[half]


def blend(groups, weights, transposed, dtype, flops=1000):
    tile = 256
    arrays = [v if v.ndim == 3 else v[None] for g in groups for v in g]
    sizes = [[v.shape[-1] for v in g] for g in groups]
    rows = arrays[0].shape[1]
    counts = [ws[0].shape[0 if transposed else 1] // tile for ws in weights]
    specs = [pl.BlockSpec((1, rows, v.shape[2]), lambda i: (0, 0, 0)) for v in arrays]
    first = 0
    for ws, count in zip(weights, counts):
        for w in ws:
            place = lambda i, first=first, count=count: jnp.clip(i - first, 0, count - 1)
            if transposed:
                specs.append(pl.BlockSpec((tile, w.shape[1]), lambda i, place=place: (place(i), 0)))
            else:
                specs.append(pl.BlockSpec((w.shape[0], tile), lambda i, place=place: (0, place(i))))
        first += count
    return pl.pallas_call(
        functools.partial(blend_kernel, sizes, len(weights), counts, transposed),
        grid=(first,),
        in_specs=specs,
        out_specs=pl.BlockSpec((rows, tile), lambda i: (0, i)),
        out_shape=jax.ShapeDtypeStruct((rows, first * tile), dtype),
        compiler_params=pltpu.CompilerParams(vmem_limit_bytes=60 * 1024 * 1024),
        cost_estimate=pl.CostEstimate(flops=flops, bytes_accessed=1000, transcendentals=0),
        name="blend",
    )(*arrays, *[w for ws in weights for w in ws])


def sided_kernel(side_ref, own_ref, other_ref, out_ref):
    tokens = own_ref.shape[0]
    out_ref[:, :tokens] = jnp.transpose(own_ref[...])
    out_ref[:, tokens:] = jnp.transpose(other_ref[...])


def sided(own, other, side, count):
    tokens, wide = own.shape
    width = wide // count
    if width % 128:
        blocks = jnp.concatenate([own, other], axis=0).T.reshape(count // 2, 2, width, 2 * tokens)
        near = jnp.where(side == 0, blocks[:, 0], blocks[:, 1])
        far = jnp.where(side == 0, blocks[:, 1], blocks[:, 0])
        return jnp.concatenate([far, near], axis=0).reshape(wide, 2 * tokens)
    column = pl.BlockSpec((tokens, width), lambda i, side: (0, i))
    return pl.pallas_call(
        sided_kernel,
        grid_spec=pltpu.PrefetchScalarGridSpec(
            num_scalar_prefetch=1,
            grid=(count,),
            in_specs=[column, column],
            out_specs=pl.BlockSpec(
                (width, 2 * tokens), lambda i, side: (i // 2 + jnp.where(i % 2 == side[0], count // 2, 0), 0)
            ),
        ),
        out_shape=jax.ShapeDtypeStruct((wide, 2 * tokens), BF16),
        compiler_params=pltpu.CompilerParams(vmem_limit_bytes=60 * 1024 * 1024),
        cost_estimate=pl.CostEstimate(flops=1000, bytes_accessed=1000, transcendentals=0),
        name="sided",
    )(side.astype(jnp.int32).reshape(1), own, other)


class Summed:
    def __init__(self, pieces, flip, count):
        self.pieces, self.flip, self.count = pieces, flip, count

    def begin(self, *deps):
        left, *others = self.pieces[0]
        left, *_ = tie(left, *deps)
        self.send, self.keep = product([(left, *others), *self.pieces[1:]])
        return self.keep

    def go(self, after=None):
        if after is not None:
            self.send, after.came = tie(self.send, after.came)
        self.came = self.flip(self.send)

    def scatter(self, value):
        groups = [list(range(side, self.count, 2)) for side in range(2)]
        return lax.psum_scatter(value, "dp", scatter_dimension=0, axis_index_groups=groups, tiled=True)

    def finish(self):
        total = (self.keep.astype(F32) + self.came.astype(F32)).astype(BF16)
        self.total = self.scatter(total)
        return total


def half_of(value, upper, axis=0):
    size = value.shape[axis] // 2
    return lax.slice_in_dim(value, size if upper else 0, 2 * size if upper else size, axis=axis)


def tie(*values):
    return lax.optimization_barrier(values)


def serve(value, done=(), ready=()):
    out = tie(value, *[h.came for h in done], *ready)
    for h, came in zip(done, out[1:]):
        h.came = came
    return out[0]


def shards(
    count,
    tokens,
    segment_ids,
    cotangent,
    g_attn,
    query_weight,
    key_weight,
    value_weight,
    w_o,
    g_mlp,
    w_gate,
    w_up,
    w_down,
):
    row = lax.axis_index("row")
    side = lax.axis_index("dp") & 1
    low = side == 0

    def swap(value):
        return lax.ppermute(value, "row", [(0, 1), (1, 0)])

    def cross(value):
        return lax.ppermute(value, "col", [(0, 1), (1, 0)])

    def flip(value):
        return lax.ppermute(value, "dp", [(i, i ^ 1) for i in range(count)])

    part_rows = w_o.shape[0] // 4
    far_0 = cross(w_o[:part_rows])
    x_m = own_rows(tokens, row)
    x_o = swap(other_rows(tokens, row))
    wkv = jnp.concatenate([key_weight, value_weight], axis=1)
    wkv_o = swap(wkv)
    wq_o = swap(query_weight)
    gains = jnp.stack([g_attn, g_mlp])
    gains_o = swap(gains)
    x_o, wkv_o, wq_o, gains_o, far_0, w_o = tie(x_o, wkv_o, wq_o, gains_o, far_0, w_o)
    far_1 = cross(w_o[part_rows : 2 * part_rows])
    x_m, x_o = x_m.astype(F32), x_o.astype(F32)
    square = jnp.sum(x_m * x_m, axis=-1, keepdims=True) + jnp.sum(x_o * x_o, axis=-1, keepdims=True)
    inv_one = lax.rsqrt(square / MODEL_WIDTH + EPS)
    xn_m = (x_m * inv_one * gains[0]).astype(BF16)
    xn_o = (x_o * inv_one * gains_o[0]).astype(BF16)

    start = jnp.sum((segment_ids[None, :] < segment_ids[:, None]).astype(jnp.int32), axis=1)
    index = lax.iota(jnp.int32, SEQ)
    start_own = own_rows(start, row)
    places = own_rows(index, row) - start_own
    freq = jnp.exp(jnp.arange(HALF, dtype=F32) * (-2.0 * math.log(THETA) / HEAD_SIZE))
    turn_t = freq[:, None] * places.astype(F32)[None, :]
    cosine_t, sine_t = jnp.cos(turn_t), jnp.sin(turn_t)
    cosine, sine = cosine_t.T[:, None, :], sine_t.T[:, None, :]

    kv = dot_plain(xn_m, wkv) + dot_plain(xn_o, wkv_o)
    narrow = key_weight.shape[1]
    wide = query_weight.shape[1]
    kp = kv[:, :narrow].reshape(OWN, -1, HEAD_SIZE)
    first, second = kp[..., :HALF], kp[..., HALF:]
    key = jnp.concatenate([first * cosine - second * sine, second * cosine + first * sine], axis=-1)
    own_kv = jnp.concatenate([key.reshape(OWN, narrow), kv[:, narrow:]], axis=1).astype(BF16)
    other_kv = swap(own_kv)
    xn_m, xn_o, own_kv = tie(xn_m, xn_o, own_kv)
    q = dot_plain(xn_m, query_weight) + dot_plain(xn_o, wq_o)

    cotangent, w_gate, w_up, w_down, w_o, xn_o = tie(cotangent, w_gate, w_up, w_down, w_o, xn_o)
    wg_o = swap(w_gate)
    wu_o = swap(w_up)
    row_arg = row.astype(jnp.int32).reshape(1)
    start_arg = start_own.reshape(1, OWN)
    q, other_kv, far_1, w_o = tie(q, other_kv, far_1, w_o)
    far_2 = cross(w_o[2 * part_rows :])
    o, lse, qt = attend(row_arg, q, cosine_t, sine_t, start_arg, own_kv, other_kv)
    o, far_2, w_o, w_down, cotangent, wg_o, wu_o = tie(o, far_2, w_o, w_down, cotangent, wg_o, wu_o)
    w_o_o = swap(w_o)
    far = jnp.concatenate([far_0, far_1, far_2], axis=0)
    o_x = cross(o)

    c_m = own_rows(cotangent, row)
    c_t = other_rows(cotangent, row)
    c_o = swap(c_t)
    far_o = swap(far)
    wd_o = swap(w_down)
    near = blend([[o]], [[w_o], [w_o_o]], False, F32)
    both = lambda own, other: jnp.concatenate([own, other], axis=0)
    c_y = sided(c_m, c_t, side, count)
    near, c_y, c_o, far_o, o_x, wd_o = tie(near, c_y, c_o, far_o, o_x, wd_o)
    width = tokens.shape[1]
    total = near + blend([[o_x]], [[far], [far_o]], False, F32)
    hidden_m, hidden_o = x_m + total[:, :width], x_o + total[:, width:]
    square = jnp.sum(hidden_m * hidden_m, axis=-1, keepdims=True) + jnp.sum(
        hidden_o * hidden_o, axis=-1, keepdims=True
    )
    inv_two = lax.rsqrt(square / MODEL_WIDTH + EPS)
    unit_m, unit_o = hidden_m * inv_two, hidden_o * inv_two
    xn2_m = (unit_m * gains[1]).astype(BF16)
    xn2_o = (unit_o * gains_o[1]).astype(BF16)

    xn2_t = swap(xn2_o)
    tiles = w_gate.shape[1] // 256
    operands = (c_m, c_o, w_gate, wg_o, w_up, wu_o, w_down, wd_o)
    one = hidden_units(0, tiles - tiles // 2, xn2_m, xn2_o, *operands)
    one_t = swap(one)
    one, xn2_m2, o_late, xn_o = tie(one, xn2_m, o, xn_o)
    o_t, xn_t = swap(o_late), swap(xn_o)
    two = hidden_units(tiles - tiles // 2, tiles // 2, xn2_m2, xn2_o, *operands)
    two, one_t, xn2_t, o_t, xn_t = tie(two, one_t, xn2_t, o_t, xn_t)
    two_t = swap(two)

    two, xn2_m2 = tie(two, xn2_m2)
    xn2_y = sided(xn2_m2, xn2_t, side, count)
    first_z = Summed([(xn2_y, one, one_t, 2)], flip, count)
    first_z.begin()
    first_z.send = first_z.scatter(first_z.send)
    first_z.keep, two_t = tie(first_z.keep, two_t)
    send_1 = Summed([(c_y, one, one_t, 0), (c_y, two, two_t, 0)], flip, count)
    send_1.begin(first_z.keep)
    send_1.go()
    send_1.keep, two_late, first_z.keep = tie(send_1.keep, two, first_z.keep)
    first_z.keep = first_z.scatter(first_z.keep)
    part = input_grad(one, two_late, w_gate, w_up, wg_o, wu_o)
    came = cross(part)
    send_2 = Summed([(xn2_y, one, one_t, 1)], flip, count)
    send_2.begin(part)
    send_3 = Summed([(xn2_y, two, two_t, 1)], flip, count)
    send_3.begin(send_2.keep)
    send_4 = Summed([(xn2_y, two, two_t, 2)], flip, count)
    send_4.begin(send_3.keep)
    came, first_z.send, part = tie(came, first_z.send, part, send_4.keep)[:3]
    came = serve(came, (send_1,))
    send_2.go(send_1)
    came, _ = tie(came, send_1.finish())

    width = tokens.shape[1]
    d_xn2 = part.astype(F32) + came.astype(F32)
    d_xn2_m, d_xn2_o = d_xn2[:, :width], d_xn2[:, width:]
    e_m, e_o = d_xn2_m * gains[1], d_xn2_o * gains_o[1]
    mean = (
        jnp.sum(e_m * unit_m, axis=-1, keepdims=True) + jnp.sum(e_o * unit_o, axis=-1, keepdims=True)
    ) / MODEL_WIDTH
    gg_mlp_m = jnp.sum(d_xn2_m * unit_m, axis=0)
    gg_mlp_o = jnp.sum(d_xn2_o * unit_o, axis=0)
    d_hid_m = c_m.astype(F32) + inv_two * (e_m - unit_m * mean)
    d_hid_o = c_o.astype(F32) + inv_two * (e_o - unit_o * mean)
    dh_m, dh_o = d_hid_m.astype(BF16), d_hid_o.astype(BF16)
    dh_t = swap(dh_o)
    d_o = blend([[dh_m], [dh_o]], [[w_o, w_o_o]], True, BF16)
    dh_y, xn_y = sided(dh_m, dh_t, side, count), sided(xn_m, xn_t, side, count)
    d_o, dh_y, xn_y, first_z.keep = tie(d_o, dh_y, xn_y, first_z.keep)
    d_o = serve(d_o, (send_2,))
    send_3.go(send_2)
    d_o, _ = tie(d_o, send_2.finish())

    d_q, d_k, d_v = attend_back(row_arg, qt, d_o, o, lse, cosine_t, sine_t, start_arg, own_kv, other_kv)
    d_q = serve(d_q, (send_3,))
    send_4.go(send_3)
    d_q, d_k, _ = tie(d_q, d_k, send_3.finish())
    d_kv = jnp.concatenate([d_k[0], d_k[1], d_v[0], d_v[1]], axis=1)
    d_kv_t = swap(other_rows(d_kv, row))
    d_kv_own = own_rows(d_kv, row)
    d_kv = d_kv_own + d_kv_t
    d_key = d_kv[:, :narrow].reshape(OWN, -1, HEAD_SIZE)
    first, second = d_key[..., :HALF], d_key[..., HALF:]
    d_key = jnp.concatenate([first * cosine + second * sine, second * cosine - first * sine], axis=-1)
    d_kv = jnp.concatenate([d_key.reshape(OWN, narrow).astype(BF16), d_kv[:, narrow:].astype(BF16)], axis=1)
    d_qkv = jnp.concatenate([d_q, d_kv], axis=1)
    d_qkv_t = swap(d_qkv)
    last = blend([[d_q], [d_kv]], [[query_weight, wkv], [wq_o, wkv_o]], True, BF16)
    last, d_qkv_t = tie(last, d_qkv_t)
    last_came = cross(last)
    last, send_1.total = tie(last, send_1.total)
    last = serve(last, (send_4,))
    last, _ = tie(last, send_4.finish())
    send_5 = Summed(
        [
            (dh_y, o[None], o_t[None], 0),
            (xn_y, d_qkv[None], d_qkv_t[None], 0),
        ],
        flip,
        count,
    )
    send_5.begin(last)
    one, send_5.keep = tie(one, send_5.keep)
    one, send_2.total = tie(one, send_2.total)
    send_5.go()
    first_z.go()
    mix = blend([[one, two]], [[w_down], [wd_o]], False, BF16)

    last_came, mix, send_3.total = tie(last_came, mix, send_3.total)
    mix_came = cross(mix)
    last_came = serve(last_came, (send_5,))
    last_came, _ = tie(last_came, send_5.finish())
    d_xn = last.astype(F32) + last_came.astype(F32)
    d_xn_m, d_xn_o = d_xn[:, :width], d_xn[:, width:]
    unit_m, unit_o = x_m * inv_one, x_o * inv_one
    e_m, e_o = d_xn_m * gains[0], d_xn_o * gains_o[0]
    mean = (
        jnp.sum(e_m * unit_m, axis=-1, keepdims=True) + jnp.sum(e_o * unit_o, axis=-1, keepdims=True)
    ) / MODEL_WIDTH
    gg_attn_m = jnp.sum(d_xn_m * unit_m, axis=0)
    gg_attn_o = jnp.sum(d_xn_o * unit_o, axis=0)
    d_tok_m = d_hid_m + inv_one * (e_m - unit_m * mean)
    d_tok_o = d_hid_o + inv_one * (e_o - unit_o * mean)
    d_tok_t = swap(d_tok_o)
    gg = jnp.stack([gg_attn_m, gg_mlp_m]) + swap(jnp.stack([gg_attn_o, gg_mlp_o]))
    for bit in range(count.bit_length() - 1):
        gg = gg + lax.ppermute(gg, "dp", [(i, i ^ (1 << bit)) for i in range(count)])
    gg = lax.dynamic_slice_in_dim(gg, lax.axis_index("dp") * (width // count), width // count, axis=1)
    d_tok_t, send_5.total = tie(d_tok_t, send_5.total)
    d_tokens = merge_rows(d_tok_m, d_tok_t, row)

    mixed_all = mix.astype(F32) + mix_came.astype(F32)
    out_m = (hidden_m + mixed_all[:, :width]).astype(BF16)
    out_o = (hidden_o + mixed_all[:, width:]).astype(BF16)
    mixed = merge_rows(out_m, swap(out_o), row)

    first_z.total = first_z.keep.astype(F32) + first_z.came.astype(F32)
    got = [h.total.astype(F32) for h in (send_1, send_2, send_3, first_z, send_4, send_5)]
    gw_down = got[0].T
    gw_gate = jnp.concatenate([got[1], got[2]], axis=1)
    gw_up = jnp.concatenate([got[3], got[4]], axis=1)
    gw_o, gw_qkv = got[5][:, : o.shape[1]].T, got[5][:, o.shape[1] :]
    return (
        mixed,
        d_tokens,
        gg[0],
        gw_qkv[:, :wide],
        gw_qkv[:, wide : wide + narrow],
        gw_qkv[:, wide + narrow :],
        gw_o,
        gg[1],
        gw_gate,
        gw_up,
        gw_down,
    )


def solution(mesh):
    count = mesh.shape["dp"]
    placed = (
        P("dp", "row"),
        P("dp"),
        P("dp", "row"),
        P("row"),
        P("row", "col"),
        P("row", "col"),
        P("row", "col"),
        P("col", "row"),
        P("row"),
        P("row", "col"),
        P("row", "col"),
        P("col", "row"),
    )

    def body(*args):
        return shards(count, *args)

    return jax.shard_map(
        body,
        mesh=mesh,
        in_specs=placed,
        out_specs=(
            P("dp", "row"),
            P("dp", "row"),
            P(("row", "dp")),
            P(("row", "dp"), "col"),
            P(("row", "dp"), "col"),
            P(("row", "dp"), "col"),
            P("col", ("row", "dp")),
            P(("row", "dp")),
            P(("row", "dp"), "col"),
            P(("row", "dp"), "col"),
            P("col", ("row", "dp")),
        ),
        check_vma=False,
    )
```

```python
import functools
import math

import jax
import jax.numpy as jnp
from jax import lax
from jax.experimental import pallas as pl
from jax.experimental.pallas import tpu as pltpu
from jax.sharding import PartitionSpec as P

MODEL_WIDTH = 2048
QUERY_HEADS = 32
KEY_VALUE_HEADS = 4
HEAD_SIZE = 64
SEQ = 1024

EPS = 1e-05
THETA = 10000.0
HALF = HEAD_SIZE // 2
CHUNK = SEQ // 4
OWN = SEQ // 2
PAIR = 2 * HEAD_SIZE
SCALE = HEAD_SIZE ** (-0.5)
NEG = -1e30
F32 = jnp.float32
BF16 = jnp.bfloat16


def dot_plain(left, right):
    return jnp.dot(left, right, preferred_element_type=F32)


def dot_right(left, right):
    return lax.dot_general(left, right, (((1,), (1,)), ((), ())), preferred_element_type=F32)


def dot_left(left, right):
    return lax.dot_general(left, right, (((0,), (0,)), ((), ())), preferred_element_type=F32)


def own_rows(value, row):
    a, b, c, d = (value[i * CHUNK : (i + 1) * CHUNK] for i in range(4))
    return jnp.concatenate([jnp.where(row == 0, a, b), jnp.where(row == 0, d, c)], axis=0)


def other_rows(value, row):
    a, b, c, d = (value[i * CHUNK : (i + 1) * CHUNK] for i in range(4))
    return jnp.concatenate([jnp.where(row == 0, b, a), jnp.where(row == 0, c, d)], axis=0)


def merge_rows(own, other, row):
    a, b = own[:CHUNK], own[CHUNK:]
    c, d = other[:CHUNK], other[CHUNK:]
    return jnp.concatenate(
        [
            jnp.where(row == 0, a, c),
            jnp.where(row == 0, c, a),
            jnp.where(row == 0, d, b),
            jnp.where(row == 0, b, d),
        ],
        axis=0,
    )


def chunk_bias(start_ref, bias, row):
    for c in range(2):
        place = jnp.where(row == 0, 3 * c, 1 + c) * CHUNK
        lanes = slice(c * CHUNK, (c + 1) * CHUNK)
        keys = lax.broadcasted_iota(jnp.int32, (SEQ, CHUNK), 0)
        queries = lax.broadcasted_iota(jnp.int32, (SEQ, CHUNK), 1) + place
        allowed = (keys >= start_ref[:, lanes]) & (keys <= queries)
        bias[:, lanes] = jnp.where(allowed, 0.0, NEG)


def place_keys(own_ref, other_ref, row, put):
    @pl.when(row == 0)
    def _():
        for i, (ref, half) in enumerate(((own_ref, 0), (other_ref, 0), (other_ref, 1), (own_ref, 1))):
            put(i, ref[half * CHUNK : (half + 1) * CHUNK, :])

    @pl.when(row == 1)
    def _():
        for i, (ref, half) in enumerate(((other_ref, 0), (own_ref, 0), (own_ref, 1), (other_ref, 1))):
            put(i, ref[half * CHUNK : (half + 1) * CHUNK, :])


def attend_kernel(
    row_ref, q_ref, cos_ref, sin_ref, start_ref, own_ref, other_ref, o_ref, lse_ref, qt_ref, bias, keys, values_t
):
    step = pl.program_id(0)
    kv = step // 4
    row = row_ref[0]

    @pl.when(step == 0)
    def _():
        chunk_bias(start_ref, bias, row)

        def put(i, block):
            span = slice(i * CHUNK, (i + 1) * CHUNK)
            for h in range(2):
                keys[h, span, :] = block[:, h * HEAD_SIZE : (h + 1) * HEAD_SIZE]
            turned = jnp.transpose(block[:, PAIR:].astype(F32)).astype(BF16)
            for h in range(2):
                values_t[h, :, span] = turned[h * HEAD_SIZE : (h + 1) * HEAD_SIZE]

        place_keys(own_ref, other_ref, row, put)

    turned = jnp.transpose(q_ref[...])
    cosine, sine = cos_ref[...], sin_ref[...]
    for h in range(2):
        a = turned[h * HEAD_SIZE : h * HEAD_SIZE + HALF]
        b = turned[h * HEAD_SIZE + HALF : (h + 1) * HEAD_SIZE]
        rot = jnp.concatenate([a * cosine - b * sine, b * cosine + a * sine], axis=0)
        qt_ref[h * HEAD_SIZE : (h + 1) * HEAD_SIZE, :] = (rot * SCALE).astype(BF16)

    def unit(c, blocks):
        lanes = slice(c * CHUNK, (c + 1) * CHUNK)
        count = blocks * CHUNK
        outs, sums = [], []
        for h in range(2):
            query = qt_ref[h * HEAD_SIZE : (h + 1) * HEAD_SIZE, lanes]
            scores = dot_plain(keys[kv, :count, :], query) + bias[:count, lanes]
            top = jnp.max(scores, axis=0, keepdims=True)
            expo = jnp.exp(scores - top)
            total = jnp.sum(expo, axis=0, keepdims=True)
            head = dot_plain(values_t[kv, :, :count], expo.astype(BF16))
            outs.append(head * (1.0 / total))
            sums.append(top + jnp.log(total))
        o_ref[lanes, :] = jnp.transpose(jnp.concatenate(outs, axis=0)).astype(BF16)
        lse_ref[0, :, lanes] = jnp.concatenate(sums, axis=0)

    @pl.when(row == 0)
    def _():
        unit(0, 1)
        unit(1, 4)

    @pl.when(row == 1)
    def _():
        unit(0, 2)
        unit(1, 3)


def attend(row, q, cosine, sine, start, own_kv, other_kv):
    heads = q.shape[1] // HEAD_SIZE
    pairs = heads // 2
    whole = lambda shape: pl.BlockSpec(shape, lambda i: (0,) * len(shape))
    return pl.pallas_call(
        attend_kernel,
        grid=(pairs,),
        in_specs=[
            pl.BlockSpec(memory_space=pltpu.SMEM),
            pl.BlockSpec((OWN, PAIR), lambda i: (0, i)),
            whole((HALF, OWN)),
            whole((HALF, OWN)),
            whole((1, OWN)),
            whole((OWN, 2 * PAIR)),
            whole((OWN, 2 * PAIR)),
        ],
        out_specs=[
            pl.BlockSpec((OWN, PAIR), lambda i: (0, i)),
            pl.BlockSpec((1, 2, OWN), lambda i: (i, 0, 0)),
            pl.BlockSpec((PAIR, OWN), lambda i: (i, 0)),
        ],
        out_shape=[
            jax.ShapeDtypeStruct((OWN, heads * HEAD_SIZE), BF16),
            jax.ShapeDtypeStruct((pairs, 2, OWN), F32),
            jax.ShapeDtypeStruct((heads * HEAD_SIZE, OWN), BF16),
        ],
        scratch_shapes=[
            pltpu.VMEM((SEQ, OWN), F32),
            pltpu.VMEM((2, SEQ, HEAD_SIZE), BF16),
            pltpu.VMEM((2, HEAD_SIZE, SEQ), BF16),
        ],
        compiler_params=pltpu.CompilerParams(vmem_limit_bytes=60 * 1024 * 1024),
        cost_estimate=pl.CostEstimate(flops=20_000_000_000, bytes_accessed=8_000_000, transcendentals=0),
        name="attend",
    )(row, q, cosine, sine, start, own_kv, other_kv)


def attend_back_kernel(
    row_ref,
    qt_ref,
    do_ref,
    o_ref,
    lse_ref,
    cos_ref,
    sin_ref,
    start_ref,
    own_ref,
    other_ref,
    dq_ref,
    dk_ref,
    dv_ref,
    bias,
    keys,
    keys_t,
    values,
):
    step = pl.program_id(0)
    kv = step // 4
    row = row_ref[0]

    @pl.when(step == 0)
    def _():
        chunk_bias(start_ref, bias, row)

        def put(i, block):
            span = slice(i * CHUNK, (i + 1) * CHUNK)
            for h in range(2):
                keys[h, span, :] = block[:, h * HEAD_SIZE : (h + 1) * HEAD_SIZE]
                values[h, span, :] = block[:, PAIR + h * HEAD_SIZE : PAIR + (h + 1) * HEAD_SIZE]
            turned = jnp.transpose(block[:, :PAIR].astype(F32)).astype(BF16)
            for h in range(2):
                keys_t[h, :, span] = turned[h * HEAD_SIZE : (h + 1) * HEAD_SIZE]

        place_keys(own_ref, other_ref, row, put)

    @pl.when(step % 4 == 0)
    def _():
        dk_ref[...] = jnp.zeros_like(dk_ref)
        dv_ref[...] = jnp.zeros_like(dv_ref)

    grad = do_ref[...].astype(F32)
    grad_t = jnp.transpose(grad)
    mixed_t = jnp.transpose(grad * o_ref[...].astype(F32))
    cosine, sine = cos_ref[...], sin_ref[...]

    def unit(c, blocks):
        lanes = slice(c * CHUNK, (c + 1) * CHUNK)
        count = blocks * CHUNK
        outs = []
        for h in range(2):
            rows = slice(h * HEAD_SIZE, (h + 1) * HEAD_SIZE)
            query = qt_ref[rows, lanes]
            d_head = grad_t[rows, lanes].astype(BF16)
            delta = jnp.sum(mixed_t[rows, lanes], axis=0, keepdims=True)
            scores = dot_plain(keys[kv, :count, :], query) + bias[:count, lanes]
            probs = jnp.exp(scores - lse_ref[0, h : h + 1, lanes])
            dv_ref[0, :count, :] += dot_right(probs.astype(BF16), d_head)
            d_probs = dot_plain(values[kv, :count, :], d_head)
            d_raw = (probs * (d_probs - delta)).astype(BF16)
            d_query = dot_plain(keys_t[kv, :, :count], d_raw) * SCALE
            dk_ref[0, :count, :] += dot_right(d_raw, query)
            a, b = d_query[:HALF], d_query[HALF:]
            co, si = cosine[:, lanes], sine[:, lanes]
            outs.append(a * co + b * si)
            outs.append(b * co - a * si)
        dq_ref[lanes, :] = jnp.transpose(jnp.concatenate(outs, axis=0)).astype(BF16)

    @pl.when(row == 0)
    def _():
        unit(0, 1)
        unit(1, 4)

    @pl.when(row == 1)
    def _():
        unit(0, 2)
        unit(1, 3)


def attend_back(row, qt, d_o, o, lse, cosine, sine, start, own_kv, other_kv):
    heads = qt.shape[0] // HEAD_SIZE
    pairs = heads // 2
    whole = lambda shape: pl.BlockSpec(shape, lambda i: (0,) * len(shape))
    return pl.pallas_call(
        attend_back_kernel,
        grid=(pairs,),
        in_specs=[
            pl.BlockSpec(memory_space=pltpu.SMEM),
            pl.BlockSpec((PAIR, OWN), lambda i: (i, 0)),
            pl.BlockSpec((OWN, PAIR), lambda i: (0, i)),
            pl.BlockSpec((OWN, PAIR), lambda i: (0, i)),
            pl.BlockSpec((1, 2, OWN), lambda i: (i, 0, 0)),
            whole((HALF, OWN)),
            whole((HALF, OWN)),
            whole((1, OWN)),
            whole((OWN, 2 * PAIR)),
            whole((OWN, 2 * PAIR)),
        ],
        out_specs=[
            pl.BlockSpec((OWN, PAIR), lambda i: (0, i)),
            pl.BlockSpec((1, SEQ, HEAD_SIZE), lambda i: (i // 4, 0, 0)),
            pl.BlockSpec((1, SEQ, HEAD_SIZE), lambda i: (i // 4, 0, 0)),
        ],
        out_shape=[
            jax.ShapeDtypeStruct((OWN, heads * HEAD_SIZE), BF16),
            jax.ShapeDtypeStruct((2, SEQ, HEAD_SIZE), F32),
            jax.ShapeDtypeStruct((2, SEQ, HEAD_SIZE), F32),
        ],
        scratch_shapes=[
            pltpu.VMEM((SEQ, OWN), F32),
            pltpu.VMEM((2, SEQ, HEAD_SIZE), BF16),
            pltpu.VMEM((2, HEAD_SIZE, SEQ), BF16),
            pltpu.VMEM((2, SEQ, HEAD_SIZE), BF16),
        ],
        compiler_params=pltpu.CompilerParams(vmem_limit_bytes=60 * 1024 * 1024),
        cost_estimate=pl.CostEstimate(flops=1000, bytes_accessed=1000, transcendentals=0),
        name="attend_back",
    )(row, qt, d_o, o, lse, cosine, sine, start, own_kv, other_kv)


def hidden_units_kernel(
    xm_ref, xo_ref, cm_ref, co_ref, gm_ref, go_ref, um_ref, uo_ref, dm_ref, do_ref, out_ref
):
    gate = dot_plain(xm_ref[...], gm_ref[...]) + dot_plain(xo_ref[...], go_ref[...])
    up = dot_plain(xm_ref[...], um_ref[...]) + dot_plain(xo_ref[...], uo_ref[...])
    d_act = dot_right(cm_ref[...], dm_ref[...]) + dot_right(co_ref[...], do_ref[...])
    sigma = jax.nn.sigmoid(gate)
    swish = gate * sigma
    out_ref[0] = (swish * up).astype(BF16)
    out_ref[1] = (d_act * up * (sigma * (1.0 + gate * (1.0 - sigma)))).astype(BF16)
    out_ref[2] = (d_act * swish).astype(BF16)


def hidden_units(first, tiles, xm, xo, cm, co, gm, go, um, uo, dm, do):
    rows, depth = xm.shape
    tile = 256
    wide = tiles * tile
    full = pl.BlockSpec((rows, depth), lambda i: (0, 0))
    column = pl.BlockSpec((depth, tile), lambda i: (0, i + first))
    line = pl.BlockSpec((tile, depth), lambda i: (i + first, 0))
    out = pl.BlockSpec((3, rows, tile), lambda i: (0, 0, i))
    return pl.pallas_call(
        hidden_units_kernel,
        grid=(tiles,),
        in_specs=[full] * 4 + [column] * 4 + [line] * 2,
        out_specs=out,
        out_shape=jax.ShapeDtypeStruct((3, rows, wide), BF16),
        compiler_params=pltpu.CompilerParams(vmem_limit_bytes=60 * 1024 * 1024),
        cost_estimate=pl.CostEstimate(flops=12 * rows * depth * wide, bytes_accessed=12 * depth * wide, transcendentals=0),
        name="hidden_units",
    )(xm, xo, cm, co, gm, go, um, uo, dm, do)


def input_grad_kernel(a_ref, b_ref, gm_ref, um_ref, go_ref, uo_ref, out_ref):
    cut = a_ref.shape[2]

    def fill(g_ref, u_ref):
        total = dot_right(a_ref[1], g_ref[:, :cut]) + dot_right(b_ref[1], g_ref[:, cut:])
        total += dot_right(a_ref[2], u_ref[:, :cut]) + dot_right(b_ref[2], u_ref[:, cut:])
        out_ref[...] = total.astype(BF16)

    step, half = pl.program_id(0), pl.num_programs(0) // 2
    pl.when(step < half)(lambda: fill(gm_ref, um_ref))
    pl.when(step >= half)(lambda: fill(go_ref, uo_ref))


def input_grad(a, b, gm, um, go, uo):
    rows = a.shape[1]
    depth, wide = gm.shape
    tile = 256
    tiles = depth // tile
    full = lambda value: pl.BlockSpec(value.shape, lambda i: (0, 0, 0))
    line_m = pl.BlockSpec((tile, wide), lambda i: (jnp.minimum(i, tiles - 1), 0))
    line_o = pl.BlockSpec((tile, wide), lambda i: (jnp.maximum(i - tiles, 0), 0))
    return pl.pallas_call(
        input_grad_kernel,
        grid=(2 * tiles,),
        in_specs=[full(a), full(b), line_m, line_m, line_o, line_o],
        out_specs=pl.BlockSpec((rows, tile), lambda i: (0, i)),
        out_shape=jax.ShapeDtypeStruct((rows, 2 * depth), BF16),
        compiler_params=pltpu.CompilerParams(vmem_limit_bytes=60 * 1024 * 1024),
        cost_estimate=pl.CostEstimate(flops=8 * rows * depth * wide, bytes_accessed=8 * depth * wide, transcendentals=0),
        name="input_grad",
    )(a, b, gm, um, go, uo)


def product_kernel(counts, *refs):
    pieces = len(counts)
    lefts, owns, others = (refs[i * pieces : (i + 1) * pieces] for i in range(3))
    send_ref, keep_ref = refs[3 * pieces :]
    step, first = pl.program_id(0), 0
    for left, own, other, count in zip(lefts, owns, others, counts):

        @pl.when((step >= first) & (step < first + count))
        def _(left=left, own=own, other=other):
            tokens, half = own.shape[1], left.shape[0] // 2
            total = dot_plain(left[:, :tokens], own[0]) + dot_plain(left[:, tokens:], other[0])
            send_ref[...] = total[:half].astype(BF16)
            keep_ref[...] = total[half:].astype(BF16)

        first += count


def product(pieces):
    tile = 256
    counts = [own.shape[2] // tile for _, own, _, _ in pieces]
    rows, tokens = pieces[0][0].shape
    owns, others = [], []
    first = 0
    for (_, own, other, index), count in zip(pieces, counts):
        place = lambda i, first=first, count=count: jnp.clip(i - first, 0, count - 1)
        owns.append(pl.BlockSpec((1, own.shape[1], tile), lambda i, index=index, place=place: (index, 0, place(i))))
        others.append(pl.BlockSpec((1, other.shape[1], tile), lambda i, index=index, place=place: (index, 0, place(i))))
        first += count
    return pl.pallas_call(
        functools.partial(product_kernel, counts),
        grid=(first,),
        in_specs=[pl.BlockSpec((rows, tokens), lambda i: (0, 0))] * len(pieces) + owns + others,
        out_specs=[pl.BlockSpec((rows // 2, tile), lambda i: (0, i))] * 2,
        out_shape=[jax.ShapeDtypeStruct((rows // 2, first * tile), BF16)] * 2,
        compiler_params=pltpu.CompilerParams(vmem_limit_bytes=60 * 1024 * 1024),
        cost_estimate=pl.CostEstimate(flops=4 * rows * tokens * first * tile, bytes_accessed=6 * rows * first * tile, transcendentals=0),
        name="product",
    )(*[p[0] for p in pieces], *[p[1] for p in pieces], *[p[2] for p in pieces])


def blend_kernel(sizes, halves, counts, transposed, *refs):
    total_a = sum(len(g) for g in sizes)
    a_refs, w_refs, out_ref = refs[:total_a], refs[total_a:-1], refs[-1]
    step, first = pl.program_id(0), 0
    for half in range(halves):

        @pl.when((step >= first) & (step < first + counts[half]))
        def _(half=half):
            total, at = None, 0
            for g, group in enumerate(sizes):
                w, low = w_refs[half * len(sizes) + g], 0
                for size in group:
                    if transposed:
                        part = dot_right(a_refs[at][0], w[:, low : low + size])
                    else:
                        part = dot_plain(a_refs[at][0], w[low : low + size, :])
                    total = part if total is None else total + part
                    low, at = low + size, at + 1
            out_ref[...] = total.astype(out_ref.dtype)

        first += counts[half]


def blend(groups, weights, transposed, dtype, flops=1000):
    tile = 256
    arrays = [v if v.ndim == 3 else v[None] for g in groups for v in g]
    sizes = [[v.shape[-1] for v in g] for g in groups]
    rows = arrays[0].shape[1]
    counts = [ws[0].shape[0 if transposed else 1] // tile for ws in weights]
    specs = [pl.BlockSpec((1, rows, v.shape[2]), lambda i: (0, 0, 0)) for v in arrays]
    first = 0
    for ws, count in zip(weights, counts):
        for w in ws:
            place = lambda i, first=first, count=count: jnp.clip(i - first, 0, count - 1)
            if transposed:
                specs.append(pl.BlockSpec((tile, w.shape[1]), lambda i, place=place: (place(i), 0)))
            else:
                specs.append(pl.BlockSpec((w.shape[0], tile), lambda i, place=place: (0, place(i))))
        first += count
    return pl.pallas_call(
        functools.partial(blend_kernel, sizes, len(weights), counts, transposed),
        grid=(first,),
        in_specs=specs,
        out_specs=pl.BlockSpec((rows, tile), lambda i: (0, i)),
        out_shape=jax.ShapeDtypeStruct((rows, first * tile), dtype),
        compiler_params=pltpu.CompilerParams(vmem_limit_bytes=60 * 1024 * 1024),
        cost_estimate=pl.CostEstimate(flops=flops, bytes_accessed=1000, transcendentals=0),
        name="blend",
    )(*arrays, *[w for ws in weights for w in ws])


def sided_kernel(side_ref, own_ref, other_ref, out_ref):
    tokens = own_ref.shape[0]
    out_ref[:, :tokens] = jnp.transpose(own_ref[...])
    out_ref[:, tokens:] = jnp.transpose(other_ref[...])


def sided(own, other, side, count):
    tokens, wide = own.shape
    width = wide // count
    if width % 128:
        blocks = jnp.concatenate([own, other], axis=0).T.reshape(count // 2, 2, width, 2 * tokens)
        near = jnp.where(side == 0, blocks[:, 0], blocks[:, 1])
        far = jnp.where(side == 0, blocks[:, 1], blocks[:, 0])
        return jnp.concatenate([far, near], axis=0).reshape(wide, 2 * tokens)
    column = pl.BlockSpec((tokens, width), lambda i, side: (0, i))
    return pl.pallas_call(
        sided_kernel,
        grid_spec=pltpu.PrefetchScalarGridSpec(
            num_scalar_prefetch=1,
            grid=(count,),
            in_specs=[column, column],
            out_specs=pl.BlockSpec(
                (width, 2 * tokens), lambda i, side: (i // 2 + jnp.where(i % 2 == side[0], count // 2, 0), 0)
            ),
        ),
        out_shape=jax.ShapeDtypeStruct((wide, 2 * tokens), BF16),
        compiler_params=pltpu.CompilerParams(vmem_limit_bytes=60 * 1024 * 1024),
        cost_estimate=pl.CostEstimate(flops=1000, bytes_accessed=1000, transcendentals=0),
        name="sided",
    )(side.astype(jnp.int32).reshape(1), own, other)


class Summed:
    def __init__(self, pieces, flip, count):
        self.pieces, self.flip, self.count = pieces, flip, count

    def begin(self, *deps):
        left, *others = self.pieces[0]
        left, *_ = tie(left, *deps)
        self.send, self.keep = product([(left, *others), *self.pieces[1:]])
        return self.keep

    def go(self, after=None):
        if after is not None:
            self.send, after.came = tie(self.send, after.came)
        self.came = self.flip(self.send)

    def scatter(self, value):
        groups = [list(range(side, self.count, 2)) for side in range(2)]
        return lax.psum_scatter(value, "dp", scatter_dimension=0, axis_index_groups=groups, tiled=True)

    def finish(self):
        total = (self.keep.astype(F32) + self.came.astype(F32)).astype(BF16)
        self.total = self.scatter(total)
        return total


def half_of(value, upper, axis=0):
    size = value.shape[axis] // 2
    return lax.slice_in_dim(value, size if upper else 0, 2 * size if upper else size, axis=axis)


def tie(*values):
    return lax.optimization_barrier(values)


def serve(value, done=(), ready=()):
    out = tie(value, *[h.came for h in done], *ready)
    for h, came in zip(done, out[1:]):
        h.came = came
    return out[0]


def shards(
    count,
    tokens,
    segment_ids,
    cotangent,
    g_attn,
    query_weight,
    key_weight,
    value_weight,
    w_o,
    g_mlp,
    w_gate,
    w_up,
    w_down,
):
    row = lax.axis_index("row")
    side = lax.axis_index("dp") & 1
    low = side == 0

    def swap(value):
        return lax.ppermute(value, "row", [(0, 1), (1, 0)])

    def cross(value):
        return lax.ppermute(value, "col", [(0, 1), (1, 0)])

    def flip(value):
        return lax.ppermute(value, "dp", [(i, i ^ 1) for i in range(count)])

    x_m = own_rows(tokens, row)
    x_o = swap(other_rows(tokens, row))
    wkv = jnp.concatenate([key_weight, value_weight], axis=1)
    wkv_o = swap(wkv)
    wq_o = swap(query_weight)
    gains = jnp.stack([g_attn, g_mlp])
    gains_o = swap(gains)
    x_m, x_o = x_m.astype(F32), x_o.astype(F32)
    square = jnp.sum(x_m * x_m, axis=-1, keepdims=True) + jnp.sum(x_o * x_o, axis=-1, keepdims=True)
    inv_one = lax.rsqrt(square / MODEL_WIDTH + EPS)
    xn_m = (x_m * inv_one * gains[0]).astype(BF16)
    xn_o = (x_o * inv_one * gains_o[0]).astype(BF16)

    start = jnp.sum((segment_ids[None, :] < segment_ids[:, None]).astype(jnp.int32), axis=1)
    index = lax.iota(jnp.int32, SEQ)
    start_own = own_rows(start, row)
    places = own_rows(index, row) - start_own
    freq = jnp.exp(jnp.arange(HALF, dtype=F32) * (-2.0 * math.log(THETA) / HEAD_SIZE))
    turn_t = freq[:, None] * places.astype(F32)[None, :]
    cosine_t, sine_t = jnp.cos(turn_t), jnp.sin(turn_t)
    cosine, sine = cosine_t.T[:, None, :], sine_t.T[:, None, :]

    kv = dot_plain(xn_m, wkv) + dot_plain(xn_o, wkv_o)
    narrow = key_weight.shape[1]
    wide = query_weight.shape[1]
    kp = kv[:, :narrow].reshape(OWN, -1, HEAD_SIZE)
    first, second = kp[..., :HALF], kp[..., HALF:]
    key = jnp.concatenate([first * cosine - second * sine, second * cosine + first * sine], axis=-1)
    own_kv = jnp.concatenate([key.reshape(OWN, narrow), kv[:, narrow:]], axis=1).astype(BF16)
    other_kv = swap(own_kv)
    xn_m, xn_o, own_kv = tie(xn_m, xn_o, own_kv)
    q = dot_plain(xn_m, query_weight) + dot_plain(xn_o, wq_o)

    cotangent, w_gate, w_up, w_down, w_o, xn_o = tie(cotangent, w_gate, w_up, w_down, w_o, xn_o)
    w_o_o = swap(w_o)
    wg_o = swap(w_gate)
    wu_o = swap(w_up)
    c_m = own_rows(cotangent, row)
    c_t = other_rows(cotangent, row)
    c_o = swap(c_t)
    wd_o = swap(w_down)
    xn_t = swap(xn_o)

    row_arg = row.astype(jnp.int32).reshape(1)
    start_arg = start_own.reshape(1, OWN)
    o, lse, qt = attend(row_arg, q, cosine_t, sine_t, start_arg, own_kv, other_kv)
    part_m = dot_plain(o, w_o).astype(BF16)
    came_m = cross(part_m)
    part_o = dot_plain(o, w_o_o).astype(BF16)
    came_o = cross(part_o)
    o_t = swap(o)
    hidden_m = x_m + (part_m.astype(F32) + came_m.astype(F32))
    hidden_o = x_o + (part_o.astype(F32) + came_o.astype(F32))
    square = jnp.sum(hidden_m * hidden_m, axis=-1, keepdims=True) + jnp.sum(
        hidden_o * hidden_o, axis=-1, keepdims=True
    )
    inv_two = lax.rsqrt(square / MODEL_WIDTH + EPS)
    unit_m, unit_o = hidden_m * inv_two, hidden_o * inv_two
    xn2_m = (unit_m * gains[1]).astype(BF16)
    xn2_o = (unit_o * gains_o[1]).astype(BF16)

    width = tokens.shape[1]
    xn2_t = swap(xn2_o)
    tiles = w_gate.shape[1] // 256
    operands = (c_m, c_o, w_gate, wg_o, w_up, wu_o, w_down, wd_o)
    one = hidden_units(0, tiles - tiles // 2, xn2_m, xn2_o, *operands)
    one_t = swap(one)
    one, xn2_m2 = tie(one, xn2_m)
    two = hidden_units(tiles - tiles // 2, tiles // 2, xn2_m2, xn2_o, *operands)
    two, one_t, xn2_t = tie(two, one_t, xn2_t)
    two_t = swap(two)

    two, xn2_m2, c_m2 = tie(two, xn2_m2, c_m)
    c_y = sided(c_m2, c_t, side, count)
    xn2_y = sided(xn2_m2, xn2_t, side, count)
    first_z = Summed([(xn2_y, one, one_t, 2)], flip, count)
    first_z.begin()
    first_z.send = first_z.scatter(first_z.send)
    first_z.keep, two_t = tie(first_z.keep, two_t)
    send_1 = Summed([(c_y, one, one_t, 0), (c_y, two, two_t, 0)], flip, count)
    send_1.begin(first_z.keep)
    send_1.go()
    send_1.keep, two_late, first_z.keep = tie(send_1.keep, two, first_z.keep)
    first_z.keep = first_z.scatter(first_z.keep)
    part = input_grad(one, two_late, w_gate, w_up, wg_o, wu_o)
    came = cross(part)
    send_2 = Summed([(xn2_y, one, one_t, 1)], flip, count)
    send_2.begin(part)
    send_3 = Summed([(xn2_y, two, two_t, 1)], flip, count)
    send_3.begin(send_2.keep)
    send_4 = Summed([(xn2_y, two, two_t, 2)], flip, count)
    send_4.begin(send_3.keep)
    one_late, xn_late, _ = tie(one, xn_m, send_4.keep)
    mix = blend([[one_late, two]], [[w_down], [wd_o]], False, BF16)
    xn_y = sided(xn_late, xn_t, side, count)
    mix_came = cross(mix)
    came, first_z.send, part = tie(came, first_z.send, part, mix, xn_y)[:3]
    came = serve(came, (send_1,))
    send_2.go(send_1)
    came, _ = tie(came, send_1.finish())

    width = tokens.shape[1]
    d_xn2 = part.astype(F32) + came.astype(F32)
    d_xn2_m, d_xn2_o = d_xn2[:, :width], d_xn2[:, width:]
    e_m, e_o = d_xn2_m * gains[1], d_xn2_o * gains_o[1]
    mean = (
        jnp.sum(e_m * unit_m, axis=-1, keepdims=True) + jnp.sum(e_o * unit_o, axis=-1, keepdims=True)
    ) / MODEL_WIDTH
    gg_mlp_m = jnp.sum(d_xn2_m * unit_m, axis=0)
    gg_mlp_o = jnp.sum(d_xn2_o * unit_o, axis=0)
    d_hid_m = c_m.astype(F32) + inv_two * (e_m - unit_m * mean)
    d_hid_o = c_o.astype(F32) + inv_two * (e_o - unit_o * mean)
    dh_m, dh_o = d_hid_m.astype(BF16), d_hid_o.astype(BF16)
    dh_t = swap(dh_o)
    d_o = blend([[dh_m], [dh_o]], [[w_o, w_o_o]], True, BF16)
    d_o, dh_t, first_z.keep = tie(d_o, dh_t, first_z.keep)
    d_o = serve(d_o, (send_2,))
    send_3.go(send_2)
    d_o, _ = tie(d_o, send_2.finish())

    d_q, d_k, d_v = attend_back(row_arg, qt, d_o, o, lse, cosine_t, sine_t, start_arg, own_kv, other_kv)
    d_q, mix_came = tie(d_q, mix_came)
    d_q = serve(d_q, (send_3,))
    send_4.go(send_3)
    d_q, d_k, _ = tie(d_q, d_k, send_3.finish())
    d_kv = jnp.concatenate([d_k[0], d_k[1], d_v[0], d_v[1]], axis=1)
    d_kv_t = swap(other_rows(d_kv, row))
    d_kv_own = own_rows(d_kv, row)
    d_kv = d_kv_own + d_kv_t
    d_key = d_kv[:, :narrow].reshape(OWN, -1, HEAD_SIZE)
    first, second = d_key[..., :HALF], d_key[..., HALF:]
    d_key = jnp.concatenate([first * cosine + second * sine, second * cosine - first * sine], axis=-1)
    d_kv = jnp.concatenate([d_key.reshape(OWN, narrow).astype(BF16), d_kv[:, narrow:].astype(BF16)], axis=1)
    d_qkv = jnp.concatenate([d_q, d_kv], axis=1)
    d_qkv_t = swap(d_qkv)
    dh_y = sided(dh_m, dh_t, side, count)
    send_5 = Summed([(dh_y, o[None], o_t[None], 0), (xn_y, d_qkv[None], d_qkv_t[None], 0)], flip, count)
    d_q_late, send_5.keep = tie(d_q, send_5.begin())
    last = blend([[d_q_late], [d_kv]], [[query_weight, wkv], [wq_o, wkv_o]], True, BF16)
    last_came = cross(last)
    last, send_1.total, send_5.keep = tie(last, send_1.total, send_5.keep)
    send_5.keep = serve(send_5.keep, (send_4,))
    send_5.go(send_4)
    first_z.go()
    send_5.keep, send_2.total, _ = tie(send_5.keep, send_2.total, send_4.finish())
    last_came, send_5.keep = tie(last_came, send_5.keep)

    last_came, send_3.total = tie(last_came, send_3.total)
    last_came = serve(last_came, (send_5,))
    last_came, _ = tie(last_came, send_5.finish())
    d_xn = last.astype(F32) + last_came.astype(F32)
    d_xn_m, d_xn_o = d_xn[:, :width], d_xn[:, width:]
    unit_m, unit_o = x_m * inv_one, x_o * inv_one
    e_m, e_o = d_xn_m * gains[0], d_xn_o * gains_o[0]
    mean = (
        jnp.sum(e_m * unit_m, axis=-1, keepdims=True) + jnp.sum(e_o * unit_o, axis=-1, keepdims=True)
    ) / MODEL_WIDTH
    gg_attn_m = jnp.sum(d_xn_m * unit_m, axis=0)
    gg_attn_o = jnp.sum(d_xn_o * unit_o, axis=0)
    d_tok_m = d_hid_m + inv_one * (e_m - unit_m * mean)
    d_tok_o = d_hid_o + inv_one * (e_o - unit_o * mean)
    d_tok_t = swap(d_tok_o)
    gg = jnp.stack([gg_attn_m, gg_mlp_m]) + swap(jnp.stack([gg_attn_o, gg_mlp_o]))
    for bit in range(count.bit_length() - 1):
        gg = gg + lax.ppermute(gg, "dp", [(i, i ^ (1 << bit)) for i in range(count)])
    gg = lax.dynamic_slice_in_dim(gg, lax.axis_index("dp") * (width // count), width // count, axis=1)
    d_tok_t, send_5.total = tie(d_tok_t, send_5.total)
    d_tokens = merge_rows(d_tok_m, d_tok_t, row)

    mixed_all = mix.astype(F32) + mix_came.astype(F32)
    out_m = (hidden_m + mixed_all[:, :width]).astype(BF16)
    out_o = (hidden_o + mixed_all[:, width:]).astype(BF16)
    mixed = merge_rows(out_m, swap(out_o), row)

    first_z.total = first_z.keep.astype(F32) + first_z.came.astype(F32)
    got = [h.total.astype(F32) for h in (send_1, send_2, send_3, first_z, send_4, send_5)]
    gw_down = got[0].T
    gw_gate = jnp.concatenate([got[1], got[2]], axis=1)
    gw_up = jnp.concatenate([got[3], got[4]], axis=1)
    gw_o, gw_qkv = got[5][:, : o.shape[1]].T, got[5][:, o.shape[1] :]
    return (
        mixed,
        d_tokens,
        gg[0],
        gw_qkv[:, :wide],
        gw_qkv[:, wide : wide + narrow],
        gw_qkv[:, wide + narrow :],
        gw_o,
        gg[1],
        gw_gate,
        gw_up,
        gw_down,
    )


def solution(mesh):
    count = mesh.shape["dp"]
    placed = (
        P("dp", "row"),
        P("dp"),
        P("dp", "row"),
        P("row"),
        P("row", "col"),
        P("row", "col"),
        P("row", "col"),
        P("col", "row"),
        P("row"),
        P("row", "col"),
        P("row", "col"),
        P("col", "row"),
    )

    def body(*args):
        return shards(count, *args)

    return jax.shard_map(
        body,
        mesh=mesh,
        in_specs=placed,
        out_specs=(
            P("dp", "row"),
            P("dp", "row"),
            P(("row", "dp")),
            P(("row", "dp"), "col"),
            P(("row", "dp"), "col"),
            P(("row", "dp"), "col"),
            P("col", ("row", "dp")),
            P(("row", "dp")),
            P(("row", "dp"), "col"),
            P(("row", "dp"), "col"),
            P("col", ("row", "dp")),
        ),
        check_vma=False,
    )
```

```python
import functools
import math

import jax
import jax.numpy as jnp
from jax import lax
from jax.experimental import pallas as pl
from jax.experimental.pallas import tpu as pltpu
from jax.sharding import PartitionSpec as P

MODEL_WIDTH = 2048
QUERY_HEADS = 32
KEY_VALUE_HEADS = 4
HEAD_SIZE = 64
SEQ = 1024

EPS = 1e-05
THETA = 10000.0
HALF = HEAD_SIZE // 2
CHUNK = SEQ // 4
OWN = SEQ // 2
PAIR = 2 * HEAD_SIZE
SCALE = HEAD_SIZE ** (-0.5)
NEG = -1e30
F32 = jnp.float32
BF16 = jnp.bfloat16


def dot_plain(left, right):
    return jnp.dot(left, right, preferred_element_type=F32)


def dot_right(left, right):
    return lax.dot_general(left, right, (((1,), (1,)), ((), ())), preferred_element_type=F32)


def dot_left(left, right):
    return lax.dot_general(left, right, (((0,), (0,)), ((), ())), preferred_element_type=F32)


def own_rows(value, row):
    a, b, c, d = (value[i * CHUNK : (i + 1) * CHUNK] for i in range(4))
    return jnp.concatenate([jnp.where(row == 0, a, b), jnp.where(row == 0, d, c)], axis=0)


def other_rows(value, row):
    a, b, c, d = (value[i * CHUNK : (i + 1) * CHUNK] for i in range(4))
    return jnp.concatenate([jnp.where(row == 0, b, a), jnp.where(row == 0, c, d)], axis=0)


def merge_rows(own, other, row):
    a, b = own[:CHUNK], own[CHUNK:]
    c, d = other[:CHUNK], other[CHUNK:]
    return jnp.concatenate(
        [
            jnp.where(row == 0, a, c),
            jnp.where(row == 0, c, a),
            jnp.where(row == 0, d, b),
            jnp.where(row == 0, b, d),
        ],
        axis=0,
    )


def chunk_bias(start_ref, bias, row):
    for c in range(2):
        place = jnp.where(row == 0, 3 * c, 1 + c) * CHUNK
        lanes = slice(c * CHUNK, (c + 1) * CHUNK)
        keys = lax.broadcasted_iota(jnp.int32, (SEQ, CHUNK), 0)
        queries = lax.broadcasted_iota(jnp.int32, (SEQ, CHUNK), 1) + place
        allowed = (keys >= start_ref[:, lanes]) & (keys <= queries)
        bias[:, lanes] = jnp.where(allowed, 0.0, NEG)


def place_keys(own_ref, other_ref, row, put):
    @pl.when(row == 0)
    def _():
        for i, (ref, half) in enumerate(((own_ref, 0), (other_ref, 0), (other_ref, 1), (own_ref, 1))):
            put(i, ref[half * CHUNK : (half + 1) * CHUNK, :])

    @pl.when(row == 1)
    def _():
        for i, (ref, half) in enumerate(((other_ref, 0), (own_ref, 0), (own_ref, 1), (other_ref, 1))):
            put(i, ref[half * CHUNK : (half + 1) * CHUNK, :])


def attend_kernel(
    row_ref, q_ref, cos_ref, sin_ref, start_ref, own_ref, other_ref, o_ref, lse_ref, qt_ref, bias, keys, values_t
):
    step = pl.program_id(0)
    kv = step // 4
    row = row_ref[0]

    @pl.when(step == 0)
    def _():
        chunk_bias(start_ref, bias, row)

        def put(i, block):
            span = slice(i * CHUNK, (i + 1) * CHUNK)
            for h in range(2):
                keys[h, span, :] = block[:, h * HEAD_SIZE : (h + 1) * HEAD_SIZE]
            turned = jnp.transpose(block[:, PAIR:].astype(F32)).astype(BF16)
            for h in range(2):
                values_t[h, :, span] = turned[h * HEAD_SIZE : (h + 1) * HEAD_SIZE]

        place_keys(own_ref, other_ref, row, put)

    turned = jnp.transpose(q_ref[...])
    cosine, sine = cos_ref[...], sin_ref[...]
    for h in range(2):
        a = turned[h * HEAD_SIZE : h * HEAD_SIZE + HALF]
        b = turned[h * HEAD_SIZE + HALF : (h + 1) * HEAD_SIZE]
        rot = jnp.concatenate([a * cosine - b * sine, b * cosine + a * sine], axis=0)
        qt_ref[h * HEAD_SIZE : (h + 1) * HEAD_SIZE, :] = (rot * SCALE).astype(BF16)

    def unit(c, blocks):
        lanes = slice(c * CHUNK, (c + 1) * CHUNK)
        count = blocks * CHUNK
        outs, sums = [], []
        for h in range(2):
            query = qt_ref[h * HEAD_SIZE : (h + 1) * HEAD_SIZE, lanes]
            scores = dot_plain(keys[kv, :count, :], query) + bias[:count, lanes]
            top = jnp.max(scores, axis=0, keepdims=True)
            expo = jnp.exp(scores - top)
            total = jnp.sum(expo, axis=0, keepdims=True)
            head = dot_plain(values_t[kv, :, :count], expo.astype(BF16))
            outs.append(head * (1.0 / total))
            sums.append(top + jnp.log(total))
        o_ref[lanes, :] = jnp.transpose(jnp.concatenate(outs, axis=0)).astype(BF16)
        lse_ref[0, :, lanes] = jnp.concatenate(sums, axis=0)

    @pl.when(row == 0)
    def _():
        unit(0, 1)
        unit(1, 4)

    @pl.when(row == 1)
    def _():
        unit(0, 2)
        unit(1, 3)


def attend(row, q, cosine, sine, start, own_kv, other_kv):
    heads = q.shape[1] // HEAD_SIZE
    pairs = heads // 2
    whole = lambda shape: pl.BlockSpec(shape, lambda i: (0,) * len(shape))
    return pl.pallas_call(
        attend_kernel,
        grid=(pairs,),
        in_specs=[
            pl.BlockSpec(memory_space=pltpu.SMEM),
            pl.BlockSpec((OWN, PAIR), lambda i: (0, i)),
            whole((HALF, OWN)),
            whole((HALF, OWN)),
            whole((1, OWN)),
            whole((OWN, 2 * PAIR)),
            whole((OWN, 2 * PAIR)),
        ],
        out_specs=[
            pl.BlockSpec((OWN, PAIR), lambda i: (0, i)),
            pl.BlockSpec((1, 2, OWN), lambda i: (i, 0, 0)),
            pl.BlockSpec((PAIR, OWN), lambda i: (i, 0)),
        ],
        out_shape=[
            jax.ShapeDtypeStruct((OWN, heads * HEAD_SIZE), BF16),
            jax.ShapeDtypeStruct((pairs, 2, OWN), F32),
            jax.ShapeDtypeStruct((heads * HEAD_SIZE, OWN), BF16),
        ],
        scratch_shapes=[
            pltpu.VMEM((SEQ, OWN), F32),
            pltpu.VMEM((2, SEQ, HEAD_SIZE), BF16),
            pltpu.VMEM((2, HEAD_SIZE, SEQ), BF16),
        ],
        compiler_params=pltpu.CompilerParams(vmem_limit_bytes=60 * 1024 * 1024),
        cost_estimate=pl.CostEstimate(flops=20_000_000_000, bytes_accessed=8_000_000, transcendentals=0),
        name="attend",
    )(row, q, cosine, sine, start, own_kv, other_kv)


def attend_back_kernel(
    row_ref,
    qt_ref,
    do_ref,
    o_ref,
    lse_ref,
    cos_ref,
    sin_ref,
    start_ref,
    own_ref,
    other_ref,
    dq_ref,
    dk_ref,
    dv_ref,
    bias,
    keys,
    keys_t,
    values,
):
    step = pl.program_id(0)
    kv = step // 4
    row = row_ref[0]

    @pl.when(step == 0)
    def _():
        chunk_bias(start_ref, bias, row)

        def put(i, block):
            span = slice(i * CHUNK, (i + 1) * CHUNK)
            for h in range(2):
                keys[h, span, :] = block[:, h * HEAD_SIZE : (h + 1) * HEAD_SIZE]
                values[h, span, :] = block[:, PAIR + h * HEAD_SIZE : PAIR + (h + 1) * HEAD_SIZE]
            turned = jnp.transpose(block[:, :PAIR].astype(F32)).astype(BF16)
            for h in range(2):
                keys_t[h, :, span] = turned[h * HEAD_SIZE : (h + 1) * HEAD_SIZE]

        place_keys(own_ref, other_ref, row, put)

    @pl.when(step % 4 == 0)
    def _():
        dk_ref[...] = jnp.zeros_like(dk_ref)
        dv_ref[...] = jnp.zeros_like(dv_ref)

    grad = do_ref[...].astype(F32)
    grad_t = jnp.transpose(grad)
    mixed_t = jnp.transpose(grad * o_ref[...].astype(F32))
    cosine, sine = cos_ref[...], sin_ref[...]

    def unit(c, blocks):
        lanes = slice(c * CHUNK, (c + 1) * CHUNK)
        count = blocks * CHUNK
        outs = []
        for h in range(2):
            rows = slice(h * HEAD_SIZE, (h + 1) * HEAD_SIZE)
            query = qt_ref[rows, lanes]
            d_head = grad_t[rows, lanes].astype(BF16)
            delta = jnp.sum(mixed_t[rows, lanes], axis=0, keepdims=True)
            scores = dot_plain(keys[kv, :count, :], query) + bias[:count, lanes]
            probs = jnp.exp(scores - lse_ref[0, h : h + 1, lanes])
            dv_ref[0, :count, :] += dot_right(probs.astype(BF16), d_head)
            d_probs = dot_plain(values[kv, :count, :], d_head)
            d_raw = (probs * (d_probs - delta)).astype(BF16)
            d_query = dot_plain(keys_t[kv, :, :count], d_raw) * SCALE
            dk_ref[0, :count, :] += dot_right(d_raw, query)
            a, b = d_query[:HALF], d_query[HALF:]
            co, si = cosine[:, lanes], sine[:, lanes]
            outs.append(a * co + b * si)
            outs.append(b * co - a * si)
        dq_ref[lanes, :] = jnp.transpose(jnp.concatenate(outs, axis=0)).astype(BF16)

    @pl.when(row == 0)
    def _():
        unit(0, 1)
        unit(1, 4)

    @pl.when(row == 1)
    def _():
        unit(0, 2)
        unit(1, 3)


def attend_back(row, qt, d_o, o, lse, cosine, sine, start, own_kv, other_kv):
    heads = qt.shape[0] // HEAD_SIZE
    pairs = heads // 2
    whole = lambda shape: pl.BlockSpec(shape, lambda i: (0,) * len(shape))
    return pl.pallas_call(
        attend_back_kernel,
        grid=(pairs,),
        in_specs=[
            pl.BlockSpec(memory_space=pltpu.SMEM),
            pl.BlockSpec((PAIR, OWN), lambda i: (i, 0)),
            pl.BlockSpec((OWN, PAIR), lambda i: (0, i)),
            pl.BlockSpec((OWN, PAIR), lambda i: (0, i)),
            pl.BlockSpec((1, 2, OWN), lambda i: (i, 0, 0)),
            whole((HALF, OWN)),
            whole((HALF, OWN)),
            whole((1, OWN)),
            whole((OWN, 2 * PAIR)),
            whole((OWN, 2 * PAIR)),
        ],
        out_specs=[
            pl.BlockSpec((OWN, PAIR), lambda i: (0, i)),
            pl.BlockSpec((1, SEQ, HEAD_SIZE), lambda i: (i // 4, 0, 0)),
            pl.BlockSpec((1, SEQ, HEAD_SIZE), lambda i: (i // 4, 0, 0)),
        ],
        out_shape=[
            jax.ShapeDtypeStruct((OWN, heads * HEAD_SIZE), BF16),
            jax.ShapeDtypeStruct((2, SEQ, HEAD_SIZE), F32),
            jax.ShapeDtypeStruct((2, SEQ, HEAD_SIZE), F32),
        ],
        scratch_shapes=[
            pltpu.VMEM((SEQ, OWN), F32),
            pltpu.VMEM((2, SEQ, HEAD_SIZE), BF16),
            pltpu.VMEM((2, HEAD_SIZE, SEQ), BF16),
            pltpu.VMEM((2, SEQ, HEAD_SIZE), BF16),
        ],
        compiler_params=pltpu.CompilerParams(vmem_limit_bytes=60 * 1024 * 1024),
        cost_estimate=pl.CostEstimate(flops=1000, bytes_accessed=1000, transcendentals=0),
        name="attend_back",
    )(row, qt, d_o, o, lse, cosine, sine, start, own_kv, other_kv)


def hidden_units_kernel(
    xm_ref, xo_ref, cm_ref, co_ref, gm_ref, go_ref, um_ref, uo_ref, dm_ref, do_ref, out_ref
):
    gate = dot_plain(xm_ref[...], gm_ref[...]) + dot_plain(xo_ref[...], go_ref[...])
    up = dot_plain(xm_ref[...], um_ref[...]) + dot_plain(xo_ref[...], uo_ref[...])
    d_act = dot_right(cm_ref[...], dm_ref[...]) + dot_right(co_ref[...], do_ref[...])
    sigma = jax.nn.sigmoid(gate)
    swish = gate * sigma
    out_ref[0] = (swish * up).astype(BF16)
    out_ref[1] = (d_act * up * (sigma * (1.0 + gate * (1.0 - sigma)))).astype(BF16)
    out_ref[2] = (d_act * swish).astype(BF16)


def hidden_units(first, tiles, xm, xo, cm, co, gm, go, um, uo, dm, do):
    rows, depth = xm.shape
    tile = 256
    wide = tiles * tile
    full = pl.BlockSpec((rows, depth), lambda i: (0, 0))
    column = pl.BlockSpec((depth, tile), lambda i: (0, i + first))
    line = pl.BlockSpec((tile, depth), lambda i: (i + first, 0))
    out = pl.BlockSpec((3, rows, tile), lambda i: (0, 0, i))
    return pl.pallas_call(
        hidden_units_kernel,
        grid=(tiles,),
        in_specs=[full] * 4 + [column] * 4 + [line] * 2,
        out_specs=out,
        out_shape=jax.ShapeDtypeStruct((3, rows, wide), BF16),
        compiler_params=pltpu.CompilerParams(vmem_limit_bytes=60 * 1024 * 1024),
        cost_estimate=pl.CostEstimate(flops=12 * rows * depth * wide, bytes_accessed=12 * depth * wide, transcendentals=0),
        name="hidden_units",
    )(xm, xo, cm, co, gm, go, um, uo, dm, do)


def input_grad_kernel(a_ref, b_ref, gm_ref, um_ref, go_ref, uo_ref, out_ref):
    cut = a_ref.shape[2]

    def fill(g_ref, u_ref):
        total = dot_right(a_ref[1], g_ref[:, :cut]) + dot_right(b_ref[1], g_ref[:, cut:])
        total += dot_right(a_ref[2], u_ref[:, :cut]) + dot_right(b_ref[2], u_ref[:, cut:])
        out_ref[...] = total.astype(BF16)

    step, half = pl.program_id(0), pl.num_programs(0) // 2
    pl.when(step < half)(lambda: fill(gm_ref, um_ref))
    pl.when(step >= half)(lambda: fill(go_ref, uo_ref))


def input_grad(a, b, gm, um, go, uo):
    rows = a.shape[1]
    depth, wide = gm.shape
    tile = 256
    tiles = depth // tile
    full = lambda value: pl.BlockSpec(value.shape, lambda i: (0, 0, 0))
    line_m = pl.BlockSpec((tile, wide), lambda i: (jnp.minimum(i, tiles - 1), 0))
    line_o = pl.BlockSpec((tile, wide), lambda i: (jnp.maximum(i - tiles, 0), 0))
    return pl.pallas_call(
        input_grad_kernel,
        grid=(2 * tiles,),
        in_specs=[full(a), full(b), line_m, line_m, line_o, line_o],
        out_specs=pl.BlockSpec((rows, tile), lambda i: (0, i)),
        out_shape=jax.ShapeDtypeStruct((rows, 2 * depth), BF16),
        compiler_params=pltpu.CompilerParams(vmem_limit_bytes=60 * 1024 * 1024),
        cost_estimate=pl.CostEstimate(flops=8 * rows * depth * wide, bytes_accessed=8 * depth * wide, transcendentals=0),
        name="input_grad",
    )(a, b, gm, um, go, uo)


def product_kernel(counts, *refs):
    pieces = len(counts)
    lefts, owns, others = (refs[i * pieces : (i + 1) * pieces] for i in range(3))
    send_ref, keep_ref = refs[3 * pieces :]
    step, first = pl.program_id(0), 0
    for left, own, other, count in zip(lefts, owns, others, counts):

        @pl.when((step >= first) & (step < first + count))
        def _(left=left, own=own, other=other):
            tokens, half = own.shape[1], left.shape[0] // 2
            total = dot_plain(left[:, :tokens], own[0]) + dot_plain(left[:, tokens:], other[0])
            send_ref[...] = total[:half].astype(BF16)
            keep_ref[...] = total[half:].astype(BF16)

        first += count


def product(pieces):
    tile = 256
    counts = [own.shape[2] // tile for _, own, _, _ in pieces]
    rows, tokens = pieces[0][0].shape
    owns, others = [], []
    first = 0
    for (_, own, other, index), count in zip(pieces, counts):
        place = lambda i, first=first, count=count: jnp.clip(i - first, 0, count - 1)
        owns.append(pl.BlockSpec((1, own.shape[1], tile), lambda i, index=index, place=place: (index, 0, place(i))))
        others.append(pl.BlockSpec((1, other.shape[1], tile), lambda i, index=index, place=place: (index, 0, place(i))))
        first += count
    return pl.pallas_call(
        functools.partial(product_kernel, counts),
        grid=(first,),
        in_specs=[pl.BlockSpec((rows, tokens), lambda i: (0, 0))] * len(pieces) + owns + others,
        out_specs=[pl.BlockSpec((rows // 2, tile), lambda i: (0, i))] * 2,
        out_shape=[jax.ShapeDtypeStruct((rows // 2, first * tile), BF16)] * 2,
        compiler_params=pltpu.CompilerParams(vmem_limit_bytes=60 * 1024 * 1024),
        cost_estimate=pl.CostEstimate(flops=4 * rows * tokens * first * tile, bytes_accessed=6 * rows * first * tile, transcendentals=0),
        name="product",
    )(*[p[0] for p in pieces], *[p[1] for p in pieces], *[p[2] for p in pieces])


def blend_kernel(sizes, halves, counts, transposed, *refs):
    total_a = sum(len(g) for g in sizes)
    a_refs, w_refs, out_ref = refs[:total_a], refs[total_a:-1], refs[-1]
    step, first = pl.program_id(0), 0
    for half in range(halves):

        @pl.when((step >= first) & (step < first + counts[half]))
        def _(half=half):
            total, at = None, 0
            for g, group in enumerate(sizes):
                w, low = w_refs[half * len(sizes) + g], 0
                for size in group:
                    if transposed:
                        part = dot_right(a_refs[at][0], w[:, low : low + size])
                    else:
                        part = dot_plain(a_refs[at][0], w[low : low + size, :])
                    total = part if total is None else total + part
                    low, at = low + size, at + 1
            out_ref[...] = total.astype(out_ref.dtype)

        first += counts[half]


def blend(groups, weights, transposed, dtype, flops=1000):
    tile = 256
    arrays = [v if v.ndim == 3 else v[None] for g in groups for v in g]
    sizes = [[v.shape[-1] for v in g] for g in groups]
    rows = arrays[0].shape[1]
    counts = [ws[0].shape[0 if transposed else 1] // tile for ws in weights]
    specs = [pl.BlockSpec((1, rows, v.shape[2]), lambda i: (0, 0, 0)) for v in arrays]
    first = 0
    for ws, count in zip(weights, counts):
        for w in ws:
            place = lambda i, first=first, count=count: jnp.clip(i - first, 0, count - 1)
            if transposed:
                specs.append(pl.BlockSpec((tile, w.shape[1]), lambda i, place=place: (place(i), 0)))
            else:
                specs.append(pl.BlockSpec((w.shape[0], tile), lambda i, place=place: (0, place(i))))
        first += count
    return pl.pallas_call(
        functools.partial(blend_kernel, sizes, len(weights), counts, transposed),
        grid=(first,),
        in_specs=specs,
        out_specs=pl.BlockSpec((rows, tile), lambda i: (0, i)),
        out_shape=jax.ShapeDtypeStruct((rows, first * tile), dtype),
        compiler_params=pltpu.CompilerParams(vmem_limit_bytes=60 * 1024 * 1024),
        cost_estimate=pl.CostEstimate(flops=flops, bytes_accessed=1000, transcendentals=0),
        name="blend",
    )(*arrays, *[w for ws in weights for w in ws])


def sided_kernel(side_ref, own_ref, other_ref, out_ref):
    tokens = own_ref.shape[0]
    out_ref[:, :tokens] = jnp.transpose(own_ref[...])
    out_ref[:, tokens:] = jnp.transpose(other_ref[...])


def sided(own, other, side, count):
    tokens, wide = own.shape
    width = wide // count
    if width % 128:
        blocks = jnp.concatenate([own, other], axis=0).T.reshape(count // 2, 2, width, 2 * tokens)
        near = jnp.where(side == 0, blocks[:, 0], blocks[:, 1])
        far = jnp.where(side == 0, blocks[:, 1], blocks[:, 0])
        return jnp.concatenate([far, near], axis=0).reshape(wide, 2 * tokens)
    column = pl.BlockSpec((tokens, width), lambda i, side: (0, i))
    return pl.pallas_call(
        sided_kernel,
        grid_spec=pltpu.PrefetchScalarGridSpec(
            num_scalar_prefetch=1,
            grid=(count,),
            in_specs=[column, column],
            out_specs=pl.BlockSpec(
                (width, 2 * tokens), lambda i, side: (i // 2 + jnp.where(i % 2 == side[0], count // 2, 0), 0)
            ),
        ),
        out_shape=jax.ShapeDtypeStruct((wide, 2 * tokens), BF16),
        compiler_params=pltpu.CompilerParams(vmem_limit_bytes=60 * 1024 * 1024),
        cost_estimate=pl.CostEstimate(flops=1000, bytes_accessed=1000, transcendentals=0),
        name="sided",
    )(side.astype(jnp.int32).reshape(1), own, other)


class Summed:
    def __init__(self, pieces, flip, count):
        self.pieces, self.flip, self.count = pieces, flip, count

    def begin(self, *deps):
        left, *others = self.pieces[0]
        left, *_ = tie(left, *deps)
        self.send, self.keep = product([(left, *others), *self.pieces[1:]])
        return self.keep

    def go(self, after=None):
        if after is not None:
            self.send, after.came = tie(self.send, after.came)
        self.came = self.flip(self.send)

    def scatter(self, value):
        groups = [list(range(side, self.count, 2)) for side in range(2)]
        return lax.psum_scatter(value, "dp", scatter_dimension=0, axis_index_groups=groups, tiled=True)

    def finish(self):
        total = (self.keep.astype(F32) + self.came.astype(F32)).astype(BF16)
        self.total = self.scatter(total)
        return total


def half_of(value, upper, axis=0):
    size = value.shape[axis] // 2
    return lax.slice_in_dim(value, size if upper else 0, 2 * size if upper else size, axis=axis)


def tie(*values):
    return lax.optimization_barrier(values)


def serve(value, done=(), ready=()):
    out = tie(value, *[h.came for h in done], *ready)
    for h, came in zip(done, out[1:]):
        h.came = came
    return out[0]


def shards(
    count,
    tokens,
    segment_ids,
    cotangent,
    g_attn,
    query_weight,
    key_weight,
    value_weight,
    w_o,
    g_mlp,
    w_gate,
    w_up,
    w_down,
):
    row = lax.axis_index("row")
    side = lax.axis_index("dp") & 1
    low = side == 0

    def swap(value):
        return lax.ppermute(value, "row", [(0, 1), (1, 0)])

    def cross(value):
        return lax.ppermute(value, "col", [(0, 1), (1, 0)])

    def flip(value):
        return lax.ppermute(value, "dp", [(i, i ^ 1) for i in range(count)])

    x_m = own_rows(tokens, row)
    x_o = swap(other_rows(tokens, row))
    wkv = jnp.concatenate([key_weight, value_weight], axis=1)
    wkv_o = swap(wkv)
    wq_o = swap(query_weight)
    gains = jnp.stack([g_attn, g_mlp])
    gains_o = swap(gains)
    x_m, x_o = x_m.astype(F32), x_o.astype(F32)
    square = jnp.sum(x_m * x_m, axis=-1, keepdims=True) + jnp.sum(x_o * x_o, axis=-1, keepdims=True)
    inv_one = lax.rsqrt(square / MODEL_WIDTH + EPS)
    xn_m = (x_m * inv_one * gains[0]).astype(BF16)
    xn_o = (x_o * inv_one * gains_o[0]).astype(BF16)

    start = jnp.sum((segment_ids[None, :] < segment_ids[:, None]).astype(jnp.int32), axis=1)
    index = lax.iota(jnp.int32, SEQ)
    start_own = own_rows(start, row)
    places = own_rows(index, row) - start_own
    freq = jnp.exp(jnp.arange(HALF, dtype=F32) * (-2.0 * math.log(THETA) / HEAD_SIZE))
    turn_t = freq[:, None] * places.astype(F32)[None, :]
    cosine_t, sine_t = jnp.cos(turn_t), jnp.sin(turn_t)
    cosine, sine = cosine_t.T[:, None, :], sine_t.T[:, None, :]

    kv = dot_plain(xn_m, wkv) + dot_plain(xn_o, wkv_o)
    narrow = key_weight.shape[1]
    wide = query_weight.shape[1]
    kp = kv[:, :narrow].reshape(OWN, -1, HEAD_SIZE)
    first, second = kp[..., :HALF], kp[..., HALF:]
    key = jnp.concatenate([first * cosine - second * sine, second * cosine + first * sine], axis=-1)
    own_kv = jnp.concatenate([key.reshape(OWN, narrow), kv[:, narrow:]], axis=1).astype(BF16)
    other_kv = swap(own_kv)
    xn_m, xn_o, own_kv = tie(xn_m, xn_o, own_kv)
    q = dot_plain(xn_m, query_weight) + dot_plain(xn_o, wq_o)

    cotangent, w_gate, w_up, w_down, w_o, xn_o = tie(cotangent, w_gate, w_up, w_down, w_o, xn_o)
    w_o_o = swap(w_o)
    wg_o = swap(w_gate)
    wu_o = swap(w_up)
    c_m = own_rows(cotangent, row)
    c_t = other_rows(cotangent, row)
    c_o = swap(c_t)
    wd_o = swap(w_down)
    xn_t = swap(xn_o)

    row_arg = row.astype(jnp.int32).reshape(1)
    start_arg = start_own.reshape(1, OWN)
    o, lse, qt = attend(row_arg, q, cosine_t, sine_t, start_arg, own_kv, other_kv)
    part_m = dot_plain(o, w_o).astype(BF16)
    came_m = cross(part_m)
    part_o = dot_plain(o, w_o_o).astype(BF16)
    came_o = cross(part_o)
    o_t = swap(o)
    c_late, xn_late, _ = tie(c_m, xn_m, part_o)
    c_y = sided(c_late, c_t, side, count)
    xn_y = sided(xn_late, xn_t, side, count)
    came_o, c_y, xn_y = tie(came_o, c_y, xn_y)
    hidden_m = x_m + (part_m.astype(F32) + came_m.astype(F32))
    hidden_o = x_o + (part_o.astype(F32) + came_o.astype(F32))
    square = jnp.sum(hidden_m * hidden_m, axis=-1, keepdims=True) + jnp.sum(
        hidden_o * hidden_o, axis=-1, keepdims=True
    )
    inv_two = lax.rsqrt(square / MODEL_WIDTH + EPS)
    unit_m, unit_o = hidden_m * inv_two, hidden_o * inv_two
    xn2_m = (unit_m * gains[1]).astype(BF16)
    xn2_o = (unit_o * gains_o[1]).astype(BF16)

    width = tokens.shape[1]
    xn2_t = swap(xn2_o)
    tiles = w_gate.shape[1] // 256
    operands = (c_m, c_o, w_gate, wg_o, w_up, wu_o, w_down, wd_o)
    one = hidden_units(0, tiles - tiles // 2, xn2_m, xn2_o, *operands)
    one_t = swap(one)
    one, xn2_m2 = tie(one, xn2_m)
    two = hidden_units(tiles - tiles // 2, tiles // 2, xn2_m2, xn2_o, *operands)
    two, one_t, xn2_t = tie(two, one_t, xn2_t)
    two_t = swap(two)

    two, xn2_m2 = tie(two, xn2_m2)
    xn2_y = sided(xn2_m2, xn2_t, side, count)
    c_y, xn2_y = tie(c_y, xn2_y)
    send_1 = Summed([(c_y, one, one_t, 0), (c_y, two, two_t, 0)], flip, count)
    send_1.begin()
    send_1.go()
    send_1.keep, two_late = tie(send_1.keep, two)
    part = input_grad(one, two_late, w_gate, w_up, wg_o, wu_o)
    came = cross(part)
    first_z = Summed([(xn2_y, one, one_t, 2)], flip, count)
    first_z.begin(part)
    first_z.send = first_z.scatter(first_z.send)
    part, first_z.keep = tie(part, first_z.keep)
    first_z.keep = first_z.scatter(first_z.keep)
    send_2 = Summed([(xn2_y, one, one_t, 1)], flip, count)
    send_2.begin(part)
    send_3 = Summed([(xn2_y, two, two_t, 1)], flip, count)
    send_3.begin(send_2.keep)
    send_4 = Summed([(xn2_y, two, two_t, 2)], flip, count)
    send_4.begin(send_3.keep)
    one_late, _ = tie(one, send_4.keep)
    mix = blend([[one_late, two]], [[w_down], [wd_o]], False, BF16)
    mix_came = cross(mix)
    came, first_z.send, part = tie(came, first_z.send, part, mix)[:3]
    came = serve(came, (send_1,))
    send_2.go(send_1)
    came, _ = tie(came, send_1.finish())

    width = tokens.shape[1]
    d_xn2 = part.astype(F32) + came.astype(F32)
    d_xn2_m, d_xn2_o = d_xn2[:, :width], d_xn2[:, width:]
    e_m, e_o = d_xn2_m * gains[1], d_xn2_o * gains_o[1]
    mean = (
        jnp.sum(e_m * unit_m, axis=-1, keepdims=True) + jnp.sum(e_o * unit_o, axis=-1, keepdims=True)
    ) / MODEL_WIDTH
    gg_mlp_m = jnp.sum(d_xn2_m * unit_m, axis=0)
    gg_mlp_o = jnp.sum(d_xn2_o * unit_o, axis=0)
    d_hid_m = c_m.astype(F32) + inv_two * (e_m - unit_m * mean)
    d_hid_o = c_o.astype(F32) + inv_two * (e_o - unit_o * mean)
    dh_m, dh_o = d_hid_m.astype(BF16), d_hid_o.astype(BF16)
    dh_t = swap(dh_o)
    d_o = blend([[dh_m], [dh_o]], [[w_o, w_o_o]], True, BF16)
    d_o, dh_t, first_z.keep = tie(d_o, dh_t, first_z.keep)
    d_o = serve(d_o, (send_2,))
    send_3.go(send_2)
    d_o, _ = tie(d_o, send_2.finish())

    d_q, d_k, d_v = attend_back(row_arg, qt, d_o, o, lse, cosine_t, sine_t, start_arg, own_kv, other_kv)
    d_q, mix_came = tie(d_q, mix_came)
    d_q = serve(d_q, (send_3,))
    send_4.go(send_3)
    d_q, d_k, _ = tie(d_q, d_k, send_3.finish())
    d_kv = jnp.concatenate([d_k[0], d_k[1], d_v[0], d_v[1]], axis=1)
    d_kv_t = swap(other_rows(d_kv, row))
    d_kv_own = own_rows(d_kv, row)
    d_kv = d_kv_own + d_kv_t
    d_key = d_kv[:, :narrow].reshape(OWN, -1, HEAD_SIZE)
    first, second = d_key[..., :HALF], d_key[..., HALF:]
    d_key = jnp.concatenate([first * cosine + second * sine, second * cosine - first * sine], axis=-1)
    d_kv = jnp.concatenate([d_key.reshape(OWN, narrow).astype(BF16), d_kv[:, narrow:].astype(BF16)], axis=1)
    d_qkv = jnp.concatenate([d_q, d_kv], axis=1)
    d_qkv_t = swap(d_qkv)
    dh_y = sided(dh_m, dh_t, side, count)
    send_5 = Summed([(dh_y, o[None], o_t[None], 0), (xn_y, d_qkv[None], d_qkv_t[None], 0)], flip, count)
    d_q_late, send_5.keep = tie(d_q, send_5.begin())
    last = blend([[d_q_late], [d_kv]], [[query_weight, wkv], [wq_o, wkv_o]], True, BF16)
    last_came = cross(last)
    last, send_1.total, send_5.keep = tie(last, send_1.total, send_5.keep)
    send_5.keep = serve(send_5.keep, (send_4,))
    send_5.go(send_4)
    first_z.go()
    send_5.keep, send_2.total, _ = tie(send_5.keep, send_2.total, send_4.finish())
    last_came, send_5.keep = tie(last_came, send_5.keep)

    last_came, send_3.total = tie(last_came, send_3.total)
    last_came = serve(last_came, (send_5,))
    last_came, mix, mix_came, first_z.keep, _ = tie(last_came, mix, mix_came, first_z.keep, send_5.finish())
    d_xn = last.astype(F32) + last_came.astype(F32)
    d_xn_m, d_xn_o = d_xn[:, :width], d_xn[:, width:]
    unit_m, unit_o = x_m * inv_one, x_o * inv_one
    e_m, e_o = d_xn_m * gains[0], d_xn_o * gains_o[0]
    mean = (
        jnp.sum(e_m * unit_m, axis=-1, keepdims=True) + jnp.sum(e_o * unit_o, axis=-1, keepdims=True)
    ) / MODEL_WIDTH
    gg_attn_m = jnp.sum(d_xn_m * unit_m, axis=0)
    gg_attn_o = jnp.sum(d_xn_o * unit_o, axis=0)
    d_tok_m = d_hid_m + inv_one * (e_m - unit_m * mean)
    d_tok_o = d_hid_o + inv_one * (e_o - unit_o * mean)
    d_tok_t = swap(d_tok_o)
    gg = jnp.stack([gg_attn_m, gg_mlp_m]) + swap(jnp.stack([gg_attn_o, gg_mlp_o]))
    for bit in range(count.bit_length() - 1):
        gg = gg + lax.ppermute(gg, "dp", [(i, i ^ (1 << bit)) for i in range(count)])
    gg, send_5.total = tie(gg, send_5.total)
    gg = lax.dynamic_slice_in_dim(gg, lax.axis_index("dp") * (width // count), width // count, axis=1)
    d_tokens = merge_rows(d_tok_m, d_tok_t, row)

    mixed_all = mix.astype(F32) + mix_came.astype(F32)
    out_m = (hidden_m + mixed_all[:, :width]).astype(BF16)
    out_o = (hidden_o + mixed_all[:, width:]).astype(BF16)
    mixed = merge_rows(out_m, swap(out_o), row)

    first_z.total = first_z.keep.astype(F32) + first_z.came.astype(F32)
    got = [h.total.astype(F32) for h in (send_1, send_2, send_3, first_z, send_4, send_5)]
    gw_down = got[0].T
    gw_gate = jnp.concatenate([got[1], got[2]], axis=1)
    gw_up = jnp.concatenate([got[3], got[4]], axis=1)
    gw_o, gw_qkv = got[5][:, : o.shape[1]].T, got[5][:, o.shape[1] :]
    return (
        mixed,
        d_tokens,
        gg[0],
        gw_qkv[:, :wide],
        gw_qkv[:, wide : wide + narrow],
        gw_qkv[:, wide + narrow :],
        gw_o,
        gg[1],
        gw_gate,
        gw_up,
        gw_down,
    )


def solution(mesh):
    count = mesh.shape["dp"]
    placed = (
        P("dp", "row"),
        P("dp"),
        P("dp", "row"),
        P("row"),
        P("row", "col"),
        P("row", "col"),
        P("row", "col"),
        P("col", "row"),
        P("row"),
        P("row", "col"),
        P("row", "col"),
        P("col", "row"),
    )

    def body(*args):
        return shards(count, *args)

    return jax.shard_map(
        body,
        mesh=mesh,
        in_specs=placed,
        out_specs=(
            P("dp", "row"),
            P("dp", "row"),
            P(("row", "dp")),
            P(("row", "dp"), "col"),
            P(("row", "dp"), "col"),
            P(("row", "dp"), "col"),
            P("col", ("row", "dp")),
            P(("row", "dp")),
            P(("row", "dp"), "col"),
            P(("row", "dp"), "col"),
            P("col", ("row", "dp")),
        ),
        check_vma=False,
    )
```

```python
import functools
import math

import jax
import jax.numpy as jnp
from jax import lax
from jax.experimental import pallas as pl
from jax.experimental.pallas import tpu as pltpu
from jax.sharding import PartitionSpec as P

MODEL_WIDTH = 2048
QUERY_HEADS = 32
KEY_VALUE_HEADS = 4
HEAD_SIZE = 64
SEQ = 1024

EPS = 1e-05
THETA = 10000.0
HALF = HEAD_SIZE // 2
CHUNK = SEQ // 4
OWN = SEQ // 2
PAIR = 2 * HEAD_SIZE
SCALE = HEAD_SIZE ** (-0.5)
NEG = -1e30
F32 = jnp.float32
BF16 = jnp.bfloat16


def dot_plain(left, right):
    return jnp.dot(left, right, preferred_element_type=F32)


def dot_right(left, right):
    return lax.dot_general(left, right, (((1,), (1,)), ((), ())), preferred_element_type=F32)


def dot_left(left, right):
    return lax.dot_general(left, right, (((0,), (0,)), ((), ())), preferred_element_type=F32)


def own_rows(value, row):
    a, b, c, d = (value[i * CHUNK : (i + 1) * CHUNK] for i in range(4))
    return jnp.concatenate([jnp.where(row == 0, a, b), jnp.where(row == 0, d, c)], axis=0)


def other_rows(value, row):
    a, b, c, d = (value[i * CHUNK : (i + 1) * CHUNK] for i in range(4))
    return jnp.concatenate([jnp.where(row == 0, b, a), jnp.where(row == 0, c, d)], axis=0)


def merge_rows(own, other, row):
    a, b = own[:CHUNK], own[CHUNK:]
    c, d = other[:CHUNK], other[CHUNK:]
    return jnp.concatenate(
        [
            jnp.where(row == 0, a, c),
            jnp.where(row == 0, c, a),
            jnp.where(row == 0, d, b),
            jnp.where(row == 0, b, d),
        ],
        axis=0,
    )


def chunk_bias(start_ref, bias, row):
    for c in range(2):
        place = jnp.where(row == 0, 3 * c, 1 + c) * CHUNK
        lanes = slice(c * CHUNK, (c + 1) * CHUNK)
        keys = lax.broadcasted_iota(jnp.int32, (SEQ, CHUNK), 0)
        queries = lax.broadcasted_iota(jnp.int32, (SEQ, CHUNK), 1) + place
        allowed = (keys >= start_ref[:, lanes]) & (keys <= queries)
        bias[:, lanes] = jnp.where(allowed, 0.0, NEG)


def place_keys(own_ref, other_ref, row, put):
    @pl.when(row == 0)
    def _():
        for i, (ref, half) in enumerate(((own_ref, 0), (other_ref, 0), (other_ref, 1), (own_ref, 1))):
            put(i, ref[half * CHUNK : (half + 1) * CHUNK, :])

    @pl.when(row == 1)
    def _():
        for i, (ref, half) in enumerate(((other_ref, 0), (own_ref, 0), (own_ref, 1), (other_ref, 1))):
            put(i, ref[half * CHUNK : (half + 1) * CHUNK, :])


def attend_kernel(
    row_ref, q_ref, cos_ref, sin_ref, start_ref, own_ref, other_ref, o_ref, lse_ref, qt_ref, bias, keys, values_t
):
    step = pl.program_id(0)
    kv = step // 4
    row = row_ref[0]

    @pl.when(step == 0)
    def _():
        chunk_bias(start_ref, bias, row)

        def put(i, block):
            span = slice(i * CHUNK, (i + 1) * CHUNK)
            for h in range(2):
                keys[h, span, :] = block[:, h * HEAD_SIZE : (h + 1) * HEAD_SIZE]
            turned = jnp.transpose(block[:, PAIR:].astype(F32)).astype(BF16)
            for h in range(2):
                values_t[h, :, span] = turned[h * HEAD_SIZE : (h + 1) * HEAD_SIZE]

        place_keys(own_ref, other_ref, row, put)

    turned = jnp.transpose(q_ref[...])
    cosine, sine = cos_ref[...], sin_ref[...]
    for h in range(2):
        a = turned[h * HEAD_SIZE : h * HEAD_SIZE + HALF]
        b = turned[h * HEAD_SIZE + HALF : (h + 1) * HEAD_SIZE]
        rot = jnp.concatenate([a * cosine - b * sine, b * cosine + a * sine], axis=0)
        qt_ref[h * HEAD_SIZE : (h + 1) * HEAD_SIZE, :] = (rot * SCALE).astype(BF16)

    def unit(c, blocks):
        lanes = slice(c * CHUNK, (c + 1) * CHUNK)
        count = blocks * CHUNK
        outs, sums = [], []
        for h in range(2):
            query = qt_ref[h * HEAD_SIZE : (h + 1) * HEAD_SIZE, lanes]
            scores = dot_plain(keys[kv, :count, :], query) + bias[:count, lanes]
            top = jnp.max(scores, axis=0, keepdims=True)
            expo = jnp.exp(scores - top)
            total = jnp.sum(expo, axis=0, keepdims=True)
            head = dot_plain(values_t[kv, :, :count], expo.astype(BF16))
            outs.append(head * (1.0 / total))
            sums.append(top + jnp.log(total))
        o_ref[lanes, :] = jnp.transpose(jnp.concatenate(outs, axis=0)).astype(BF16)
        lse_ref[0, :, lanes] = jnp.concatenate(sums, axis=0)

    @pl.when(row == 0)
    def _():
        unit(0, 1)
        unit(1, 4)

    @pl.when(row == 1)
    def _():
        unit(0, 2)
        unit(1, 3)


def attend(row, q, cosine, sine, start, own_kv, other_kv):
    heads = q.shape[1] // HEAD_SIZE
    pairs = heads // 2
    whole = lambda shape: pl.BlockSpec(shape, lambda i: (0,) * len(shape))
    return pl.pallas_call(
        attend_kernel,
        grid=(pairs,),
        in_specs=[
            pl.BlockSpec(memory_space=pltpu.SMEM),
            pl.BlockSpec((OWN, PAIR), lambda i: (0, i)),
            whole((HALF, OWN)),
            whole((HALF, OWN)),
            whole((1, OWN)),
            whole((OWN, 2 * PAIR)),
            whole((OWN, 2 * PAIR)),
        ],
        out_specs=[
            pl.BlockSpec((OWN, PAIR), lambda i: (0, i)),
            pl.BlockSpec((1, 2, OWN), lambda i: (i, 0, 0)),
            pl.BlockSpec((PAIR, OWN), lambda i: (i, 0)),
        ],
        out_shape=[
            jax.ShapeDtypeStruct((OWN, heads * HEAD_SIZE), BF16),
            jax.ShapeDtypeStruct((pairs, 2, OWN), F32),
            jax.ShapeDtypeStruct((heads * HEAD_SIZE, OWN), BF16),
        ],
        scratch_shapes=[
            pltpu.VMEM((SEQ, OWN), F32),
            pltpu.VMEM((2, SEQ, HEAD_SIZE), BF16),
            pltpu.VMEM((2, HEAD_SIZE, SEQ), BF16),
        ],
        compiler_params=pltpu.CompilerParams(vmem_limit_bytes=60 * 1024 * 1024),
        cost_estimate=pl.CostEstimate(flops=20_000_000_000, bytes_accessed=8_000_000, transcendentals=0),
        name="attend",
    )(row, q, cosine, sine, start, own_kv, other_kv)


def attend_back_kernel(
    row_ref,
    qt_ref,
    do_ref,
    o_ref,
    lse_ref,
    cos_ref,
    sin_ref,
    start_ref,
    own_ref,
    other_ref,
    dq_ref,
    dk_ref,
    dv_ref,
    bias,
    keys,
    keys_t,
    values,
):
    step = pl.program_id(0)
    kv = step // 4
    row = row_ref[0]

    @pl.when(step == 0)
    def _():
        chunk_bias(start_ref, bias, row)

        def put(i, block):
            span = slice(i * CHUNK, (i + 1) * CHUNK)
            for h in range(2):
                keys[h, span, :] = block[:, h * HEAD_SIZE : (h + 1) * HEAD_SIZE]
                values[h, span, :] = block[:, PAIR + h * HEAD_SIZE : PAIR + (h + 1) * HEAD_SIZE]
            turned = jnp.transpose(block[:, :PAIR].astype(F32)).astype(BF16)
            for h in range(2):
                keys_t[h, :, span] = turned[h * HEAD_SIZE : (h + 1) * HEAD_SIZE]

        place_keys(own_ref, other_ref, row, put)

    @pl.when(step % 4 == 0)
    def _():
        dk_ref[...] = jnp.zeros_like(dk_ref)
        dv_ref[...] = jnp.zeros_like(dv_ref)

    grad = do_ref[...].astype(F32)
    grad_t = jnp.transpose(grad)
    mixed_t = jnp.transpose(grad * o_ref[...].astype(F32))
    cosine, sine = cos_ref[...], sin_ref[...]

    def unit(c, blocks):
        lanes = slice(c * CHUNK, (c + 1) * CHUNK)
        count = blocks * CHUNK
        outs = []
        for h in range(2):
            rows = slice(h * HEAD_SIZE, (h + 1) * HEAD_SIZE)
            query = qt_ref[rows, lanes]
            d_head = grad_t[rows, lanes].astype(BF16)
            delta = jnp.sum(mixed_t[rows, lanes], axis=0, keepdims=True)
            scores = dot_plain(keys[kv, :count, :], query) + bias[:count, lanes]
            probs = jnp.exp(scores - lse_ref[0, h : h + 1, lanes])
            dv_ref[0, :count, :] += dot_right(probs.astype(BF16), d_head)
            d_probs = dot_plain(values[kv, :count, :], d_head)
            d_raw = (probs * (d_probs - delta)).astype(BF16)
            d_query = dot_plain(keys_t[kv, :, :count], d_raw) * SCALE
            dk_ref[0, :count, :] += dot_right(d_raw, query)
            a, b = d_query[:HALF], d_query[HALF:]
            co, si = cosine[:, lanes], sine[:, lanes]
            outs.append(a * co + b * si)
            outs.append(b * co - a * si)
        dq_ref[lanes, :] = jnp.transpose(jnp.concatenate(outs, axis=0)).astype(BF16)

    @pl.when(row == 0)
    def _():
        unit(0, 1)
        unit(1, 4)

    @pl.when(row == 1)
    def _():
        unit(0, 2)
        unit(1, 3)


def attend_back(row, qt, d_o, o, lse, cosine, sine, start, own_kv, other_kv):
    heads = qt.shape[0] // HEAD_SIZE
    pairs = heads // 2
    whole = lambda shape: pl.BlockSpec(shape, lambda i: (0,) * len(shape))
    return pl.pallas_call(
        attend_back_kernel,
        grid=(pairs,),
        in_specs=[
            pl.BlockSpec(memory_space=pltpu.SMEM),
            pl.BlockSpec((PAIR, OWN), lambda i: (i, 0)),
            pl.BlockSpec((OWN, PAIR), lambda i: (0, i)),
            pl.BlockSpec((OWN, PAIR), lambda i: (0, i)),
            pl.BlockSpec((1, 2, OWN), lambda i: (i, 0, 0)),
            whole((HALF, OWN)),
            whole((HALF, OWN)),
            whole((1, OWN)),
            whole((OWN, 2 * PAIR)),
            whole((OWN, 2 * PAIR)),
        ],
        out_specs=[
            pl.BlockSpec((OWN, PAIR), lambda i: (0, i)),
            pl.BlockSpec((1, SEQ, HEAD_SIZE), lambda i: (i // 4, 0, 0)),
            pl.BlockSpec((1, SEQ, HEAD_SIZE), lambda i: (i // 4, 0, 0)),
        ],
        out_shape=[
            jax.ShapeDtypeStruct((OWN, heads * HEAD_SIZE), BF16),
            jax.ShapeDtypeStruct((2, SEQ, HEAD_SIZE), F32),
            jax.ShapeDtypeStruct((2, SEQ, HEAD_SIZE), F32),
        ],
        scratch_shapes=[
            pltpu.VMEM((SEQ, OWN), F32),
            pltpu.VMEM((2, SEQ, HEAD_SIZE), BF16),
            pltpu.VMEM((2, HEAD_SIZE, SEQ), BF16),
            pltpu.VMEM((2, SEQ, HEAD_SIZE), BF16),
        ],
        compiler_params=pltpu.CompilerParams(vmem_limit_bytes=60 * 1024 * 1024),
        cost_estimate=pl.CostEstimate(flops=1000, bytes_accessed=1000, transcendentals=0),
        name="attend_back",
    )(row, qt, d_o, o, lse, cosine, sine, start, own_kv, other_kv)


def hidden_units_kernel(
    xm_ref, xo_ref, cm_ref, co_ref, gm_ref, go_ref, um_ref, uo_ref, dm_ref, do_ref, out_ref
):
    gate = dot_plain(xm_ref[...], gm_ref[...]) + dot_plain(xo_ref[...], go_ref[...])
    up = dot_plain(xm_ref[...], um_ref[...]) + dot_plain(xo_ref[...], uo_ref[...])
    d_act = dot_right(cm_ref[...], dm_ref[...]) + dot_right(co_ref[...], do_ref[...])
    sigma = jax.nn.sigmoid(gate)
    swish = gate * sigma
    out_ref[0] = (swish * up).astype(BF16)
    out_ref[1] = (d_act * up * (sigma * (1.0 + gate * (1.0 - sigma)))).astype(BF16)
    out_ref[2] = (d_act * swish).astype(BF16)


def hidden_units(first, tiles, xm, xo, cm, co, gm, go, um, uo, dm, do):
    rows, depth = xm.shape
    tile = 256
    wide = tiles * tile
    full = pl.BlockSpec((rows, depth), lambda i: (0, 0))
    column = pl.BlockSpec((depth, tile), lambda i: (0, i + first))
    line = pl.BlockSpec((tile, depth), lambda i: (i + first, 0))
    out = pl.BlockSpec((3, rows, tile), lambda i: (0, 0, i))
    return pl.pallas_call(
        hidden_units_kernel,
        grid=(tiles,),
        in_specs=[full] * 4 + [column] * 4 + [line] * 2,
        out_specs=out,
        out_shape=jax.ShapeDtypeStruct((3, rows, wide), BF16),
        compiler_params=pltpu.CompilerParams(vmem_limit_bytes=60 * 1024 * 1024),
        cost_estimate=pl.CostEstimate(flops=12 * rows * depth * wide, bytes_accessed=12 * depth * wide, transcendentals=0),
        name="hidden_units",
    )(xm, xo, cm, co, gm, go, um, uo, dm, do)


def input_grad_kernel(a_ref, b_ref, gm_ref, um_ref, go_ref, uo_ref, out_ref):
    cut = a_ref.shape[2]

    def fill(g_ref, u_ref):
        total = dot_right(a_ref[1], g_ref[:, :cut]) + dot_right(b_ref[1], g_ref[:, cut:])
        total += dot_right(a_ref[2], u_ref[:, :cut]) + dot_right(b_ref[2], u_ref[:, cut:])
        out_ref[...] = total.astype(BF16)

    step, half = pl.program_id(0), pl.num_programs(0) // 2
    pl.when(step < half)(lambda: fill(gm_ref, um_ref))
    pl.when(step >= half)(lambda: fill(go_ref, uo_ref))


def input_grad(a, b, gm, um, go, uo):
    rows = a.shape[1]
    depth, wide = gm.shape
    tile = 256
    tiles = depth // tile
    full = lambda value: pl.BlockSpec(value.shape, lambda i: (0, 0, 0))
    line_m = pl.BlockSpec((tile, wide), lambda i: (jnp.minimum(i, tiles - 1), 0))
    line_o = pl.BlockSpec((tile, wide), lambda i: (jnp.maximum(i - tiles, 0), 0))
    return pl.pallas_call(
        input_grad_kernel,
        grid=(2 * tiles,),
        in_specs=[full(a), full(b), line_m, line_m, line_o, line_o],
        out_specs=pl.BlockSpec((rows, tile), lambda i: (0, i)),
        out_shape=jax.ShapeDtypeStruct((rows, 2 * depth), BF16),
        compiler_params=pltpu.CompilerParams(vmem_limit_bytes=60 * 1024 * 1024),
        cost_estimate=pl.CostEstimate(flops=8 * rows * depth * wide, bytes_accessed=8 * depth * wide, transcendentals=0),
        name="input_grad",
    )(a, b, gm, um, go, uo)


def product_kernel(counts, *refs):
    pieces = len(counts)
    lefts, owns, others = (refs[i * pieces : (i + 1) * pieces] for i in range(3))
    send_ref, keep_ref = refs[3 * pieces :]
    step, first = pl.program_id(0), 0
    for left, own, other, count in zip(lefts, owns, others, counts):

        @pl.when((step >= first) & (step < first + count))
        def _(left=left, own=own, other=other):
            tokens, half = own.shape[1], left.shape[0] // 2
            total = dot_plain(left[:, :tokens], own[0]) + dot_plain(left[:, tokens:], other[0])
            send_ref[...] = total[:half].astype(BF16)
            keep_ref[...] = total[half:].astype(BF16)

        first += count


def product(pieces):
    tile = 256
    counts = [own.shape[2] // tile for _, own, _, _ in pieces]
    rows, tokens = pieces[0][0].shape
    owns, others = [], []
    first = 0
    for (_, own, other, index), count in zip(pieces, counts):
        place = lambda i, first=first, count=count: jnp.clip(i - first, 0, count - 1)
        owns.append(pl.BlockSpec((1, own.shape[1], tile), lambda i, index=index, place=place: (index, 0, place(i))))
        others.append(pl.BlockSpec((1, other.shape[1], tile), lambda i, index=index, place=place: (index, 0, place(i))))
        first += count
    return pl.pallas_call(
        functools.partial(product_kernel, counts),
        grid=(first,),
        in_specs=[pl.BlockSpec((rows, tokens), lambda i: (0, 0))] * len(pieces) + owns + others,
        out_specs=[pl.BlockSpec((rows // 2, tile), lambda i: (0, i))] * 2,
        out_shape=[jax.ShapeDtypeStruct((rows // 2, first * tile), BF16)] * 2,
        compiler_params=pltpu.CompilerParams(vmem_limit_bytes=60 * 1024 * 1024),
        cost_estimate=pl.CostEstimate(flops=4 * rows * tokens * first * tile, bytes_accessed=6 * rows * first * tile, transcendentals=0),
        name="product",
    )(*[p[0] for p in pieces], *[p[1] for p in pieces], *[p[2] for p in pieces])


def blend_kernel(sizes, halves, counts, transposed, *refs):
    total_a = sum(len(g) for g in sizes)
    a_refs, w_refs, out_ref = refs[:total_a], refs[total_a:-1], refs[-1]
    step, first = pl.program_id(0), 0
    for half in range(halves):

        @pl.when((step >= first) & (step < first + counts[half]))
        def _(half=half):
            total, at = None, 0
            for g, group in enumerate(sizes):
                w, low = w_refs[half * len(sizes) + g], 0
                for size in group:
                    if transposed:
                        part = dot_right(a_refs[at][0], w[:, low : low + size])
                    else:
                        part = dot_plain(a_refs[at][0], w[low : low + size, :])
                    total = part if total is None else total + part
                    low, at = low + size, at + 1
            out_ref[...] = total.astype(out_ref.dtype)

        first += counts[half]


def blend(groups, weights, transposed, dtype, flops=1000):
    tile = 256
    arrays = [v if v.ndim == 3 else v[None] for g in groups for v in g]
    sizes = [[v.shape[-1] for v in g] for g in groups]
    rows = arrays[0].shape[1]
    counts = [ws[0].shape[0 if transposed else 1] // tile for ws in weights]
    specs = [pl.BlockSpec((1, rows, v.shape[2]), lambda i: (0, 0, 0)) for v in arrays]
    first = 0
    for ws, count in zip(weights, counts):
        for w in ws:
            place = lambda i, first=first, count=count: jnp.clip(i - first, 0, count - 1)
            if transposed:
                specs.append(pl.BlockSpec((tile, w.shape[1]), lambda i, place=place: (place(i), 0)))
            else:
                specs.append(pl.BlockSpec((w.shape[0], tile), lambda i, place=place: (0, place(i))))
        first += count
    return pl.pallas_call(
        functools.partial(blend_kernel, sizes, len(weights), counts, transposed),
        grid=(first,),
        in_specs=specs,
        out_specs=pl.BlockSpec((rows, tile), lambda i: (0, i)),
        out_shape=jax.ShapeDtypeStruct((rows, first * tile), dtype),
        compiler_params=pltpu.CompilerParams(vmem_limit_bytes=60 * 1024 * 1024),
        cost_estimate=pl.CostEstimate(flops=flops, bytes_accessed=1000, transcendentals=0),
        name="blend",
    )(*arrays, *[w for ws in weights for w in ws])


def sided_kernel(side_ref, own_ref, other_ref, out_ref):
    tokens = own_ref.shape[0]
    out_ref[:, :tokens] = jnp.transpose(own_ref[...])
    out_ref[:, tokens:] = jnp.transpose(other_ref[...])


def sided(own, other, side, count):
    tokens, wide = own.shape
    width = wide // count
    if width % 128:
        blocks = jnp.concatenate([own, other], axis=0).T.reshape(count // 2, 2, width, 2 * tokens)
        near = jnp.where(side == 0, blocks[:, 0], blocks[:, 1])
        far = jnp.where(side == 0, blocks[:, 1], blocks[:, 0])
        return jnp.concatenate([far, near], axis=0).reshape(wide, 2 * tokens)
    column = pl.BlockSpec((tokens, width), lambda i, side: (0, i))
    return pl.pallas_call(
        sided_kernel,
        grid_spec=pltpu.PrefetchScalarGridSpec(
            num_scalar_prefetch=1,
            grid=(count,),
            in_specs=[column, column],
            out_specs=pl.BlockSpec(
                (width, 2 * tokens), lambda i, side: (i // 2 + jnp.where(i % 2 == side[0], count // 2, 0), 0)
            ),
        ),
        out_shape=jax.ShapeDtypeStruct((wide, 2 * tokens), BF16),
        compiler_params=pltpu.CompilerParams(vmem_limit_bytes=60 * 1024 * 1024),
        cost_estimate=pl.CostEstimate(flops=1000, bytes_accessed=1000, transcendentals=0),
        name="sided",
    )(side.astype(jnp.int32).reshape(1), own, other)


class Summed:
    def __init__(self, pieces, flip, count):
        self.pieces, self.flip, self.count = pieces, flip, count

    def begin(self, *deps):
        left, *others = self.pieces[0]
        left, *_ = tie(left, *deps)
        self.send, self.keep = product([(left, *others), *self.pieces[1:]])
        return self.keep

    def go(self, after=None):
        if after is not None:
            self.send, after.came = tie(self.send, after.came)
        self.came = self.flip(self.send)

    def scatter(self, value):
        groups = [list(range(side, self.count, 2)) for side in range(2)]
        return lax.psum_scatter(value, "dp", scatter_dimension=0, axis_index_groups=groups, tiled=True)

    def finish(self):
        total = (self.keep.astype(F32) + self.came.astype(F32)).astype(BF16)
        self.total = self.scatter(total)
        return total


def half_of(value, upper, axis=0):
    size = value.shape[axis] // 2
    return lax.slice_in_dim(value, size if upper else 0, 2 * size if upper else size, axis=axis)


def tie(*values):
    return lax.optimization_barrier(values)


def serve(value, done=(), ready=()):
    out = tie(value, *[h.came for h in done], *ready)
    for h, came in zip(done, out[1:]):
        h.came = came
    return out[0]


def shards(
    count,
    tokens,
    segment_ids,
    cotangent,
    g_attn,
    query_weight,
    key_weight,
    value_weight,
    w_o,
    g_mlp,
    w_gate,
    w_up,
    w_down,
):
    row = lax.axis_index("row")
    side = lax.axis_index("dp") & 1
    low = side == 0

    def swap(value):
        return lax.ppermute(value, "row", [(0, 1), (1, 0)])

    def cross(value):
        return lax.ppermute(value, "col", [(0, 1), (1, 0)])

    def flip(value):
        return lax.ppermute(value, "dp", [(i, i ^ 1) for i in range(count)])

    x_m = own_rows(tokens, row)
    x_o = swap(other_rows(tokens, row))
    wkv = jnp.concatenate([key_weight, value_weight], axis=1)
    wkv_o = swap(wkv)
    wq_o = swap(query_weight)
    gains = jnp.stack([g_attn, g_mlp])
    gains_o = swap(gains)
    x_m, x_o = x_m.astype(F32), x_o.astype(F32)
    square = jnp.sum(x_m * x_m, axis=-1, keepdims=True) + jnp.sum(x_o * x_o, axis=-1, keepdims=True)
    inv_one = lax.rsqrt(square / MODEL_WIDTH + EPS)
    xn_m = (x_m * inv_one * gains[0]).astype(BF16)
    xn_o = (x_o * inv_one * gains_o[0]).astype(BF16)

    start = jnp.sum((segment_ids[None, :] < segment_ids[:, None]).astype(jnp.int32), axis=1)
    index = lax.iota(jnp.int32, SEQ)
    start_own = own_rows(start, row)
    places = own_rows(index, row) - start_own
    freq = jnp.exp(jnp.arange(HALF, dtype=F32) * (-2.0 * math.log(THETA) / HEAD_SIZE))
    turn_t = freq[:, None] * places.astype(F32)[None, :]
    cosine_t, sine_t = jnp.cos(turn_t), jnp.sin(turn_t)
    cosine, sine = cosine_t.T[:, None, :], sine_t.T[:, None, :]

    kv = dot_plain(xn_m, wkv) + dot_plain(xn_o, wkv_o)
    narrow = key_weight.shape[1]
    wide = query_weight.shape[1]
    kp = kv[:, :narrow].reshape(OWN, -1, HEAD_SIZE)
    first, second = kp[..., :HALF], kp[..., HALF:]
    key = jnp.concatenate([first * cosine - second * sine, second * cosine + first * sine], axis=-1)
    own_kv = jnp.concatenate([key.reshape(OWN, narrow), kv[:, narrow:]], axis=1).astype(BF16)
    other_kv = swap(own_kv)
    xn_m, xn_o, own_kv = tie(xn_m, xn_o, own_kv)
    q = dot_plain(xn_m, query_weight) + dot_plain(xn_o, wq_o)

    cotangent, w_gate, w_up, w_down, w_o, xn_o = tie(cotangent, w_gate, w_up, w_down, w_o, xn_o)
    w_o_o = swap(w_o)
    wg_o = swap(w_gate)
    wu_o = swap(w_up)
    c_m = own_rows(cotangent, row)
    c_t = other_rows(cotangent, row)
    c_o = swap(c_t)
    wd_o = swap(w_down)
    xn_t = swap(xn_o)

    row_arg = row.astype(jnp.int32).reshape(1)
    start_arg = start_own.reshape(1, OWN)
    o, lse, qt = attend(row_arg, q, cosine_t, sine_t, start_arg, own_kv, other_kv)
    part_m = dot_plain(o, w_o).astype(BF16)
    came_m = cross(part_m)
    part_o = dot_plain(o, w_o_o).astype(BF16)
    came_o = cross(part_o)
    o_t = swap(o)
    c_late, xn_late, _ = tie(c_m, xn_m, part_o)
    c_y = sided(c_late, c_t, side, count)
    xn_y = sided(xn_late, xn_t, side, count)
    came_o, c_y, xn_y = tie(came_o, c_y, xn_y)
    hidden_m = x_m + (part_m.astype(F32) + came_m.astype(F32))
    hidden_o = x_o + (part_o.astype(F32) + came_o.astype(F32))
    square = jnp.sum(hidden_m * hidden_m, axis=-1, keepdims=True) + jnp.sum(
        hidden_o * hidden_o, axis=-1, keepdims=True
    )
    inv_two = lax.rsqrt(square / MODEL_WIDTH + EPS)
    unit_m, unit_o = hidden_m * inv_two, hidden_o * inv_two
    xn2_m = (unit_m * gains[1]).astype(BF16)
    xn2_o = (unit_o * gains_o[1]).astype(BF16)

    width = tokens.shape[1]
    xn2_t = swap(xn2_o)
    tiles = w_gate.shape[1] // 256
    operands = (c_m, c_o, w_gate, wg_o, w_up, wu_o, w_down, wd_o)
    one = hidden_units(0, tiles - tiles // 2, xn2_m, xn2_o, *operands)
    one_t = swap(one)
    one, xn2_m2 = tie(one, xn2_m)
    two = hidden_units(tiles - tiles // 2, tiles // 2, xn2_m2, xn2_o, *operands)
    two, one_t, xn2_t = tie(two, one_t, xn2_t)
    two_t = swap(two)

    two, xn2_m2 = tie(two, xn2_m2)
    xn2_y = sided(xn2_m2, xn2_t, side, count)
    c_y, xn2_y = tie(c_y, xn2_y)
    send_1 = Summed([(c_y, one, one_t, 0), (c_y, two, two_t, 0)], flip, count)
    send_1.begin()
    send_1.go()
    send_1.keep, two_late = tie(send_1.keep, two)
    part = input_grad(one, two_late, w_gate, w_up, wg_o, wu_o)
    came = cross(part)
    first_z = Summed([(xn2_y, one, one_t, 2)], flip, count)
    first_z.begin(part)
    first_z.send = first_z.scatter(first_z.send)
    part, first_z.keep = tie(part, first_z.keep)
    first_z.keep = first_z.scatter(first_z.keep)
    send_2 = Summed([(xn2_y, one, one_t, 1)], flip, count)
    send_2.begin(part)
    send_3 = Summed([(xn2_y, two, two_t, 1)], flip, count)
    send_4 = Summed([(xn2_y, two, two_t, 2)], flip, count)
    one_late, _ = tie(one, send_2.keep)
    mix = blend([[one_late, two]], [[w_down], [wd_o]], False, BF16)
    mix_came = cross(mix)
    came, first_z.send, part = tie(came, first_z.send, part, mix)[:3]
    came = serve(came, (send_1,))
    send_2.go(send_1)
    came, _ = tie(came, send_1.finish())

    width = tokens.shape[1]
    d_xn2 = part.astype(F32) + came.astype(F32)
    d_xn2_m, d_xn2_o = d_xn2[:, :width], d_xn2[:, width:]
    e_m, e_o = d_xn2_m * gains[1], d_xn2_o * gains_o[1]
    mean = (
        jnp.sum(e_m * unit_m, axis=-1, keepdims=True) + jnp.sum(e_o * unit_o, axis=-1, keepdims=True)
    ) / MODEL_WIDTH
    gg_mlp_m = jnp.sum(d_xn2_m * unit_m, axis=0)
    gg_mlp_o = jnp.sum(d_xn2_o * unit_o, axis=0)
    d_hid_m = c_m.astype(F32) + inv_two * (e_m - unit_m * mean)
    d_hid_o = c_o.astype(F32) + inv_two * (e_o - unit_o * mean)
    dh_m, dh_o = d_hid_m.astype(BF16), d_hid_o.astype(BF16)
    dh_t = swap(dh_o)
    d_o = blend([[dh_m], [dh_o]], [[w_o, w_o_o]], True, BF16)
    send_3.begin(d_o)
    send_4.begin(send_3.keep)
    d_o, dh_t, first_z.keep, send_4.keep = tie(d_o, dh_t, first_z.keep, send_4.keep)
    d_o = serve(d_o, (send_2,))
    send_3.go(send_2)
    d_o, _ = tie(d_o, send_2.finish())

    d_q, d_k, d_v = attend_back(row_arg, qt, d_o, o, lse, cosine_t, sine_t, start_arg, own_kv, other_kv)
    d_q, mix_came = tie(d_q, mix_came)
    d_q = serve(d_q, (send_3,))
    send_4.go(send_3)
    d_q, d_k, _ = tie(d_q, d_k, send_3.finish())
    d_kv = jnp.concatenate([d_k[0], d_k[1], d_v[0], d_v[1]], axis=1)
    d_kv_t = swap(other_rows(d_kv, row))
    d_kv_own = own_rows(d_kv, row)
    d_kv = d_kv_own + d_kv_t
    d_key = d_kv[:, :narrow].reshape(OWN, -1, HEAD_SIZE)
    first, second = d_key[..., :HALF], d_key[..., HALF:]
    d_key = jnp.concatenate([first * cosine + second * sine, second * cosine - first * sine], axis=-1)
    d_kv = jnp.concatenate([d_key.reshape(OWN, narrow).astype(BF16), d_kv[:, narrow:].astype(BF16)], axis=1)
    d_qkv = jnp.concatenate([d_q, d_kv], axis=1)
    d_qkv_t = swap(d_qkv)
    dh_y = sided(dh_m, dh_t, side, count)
    send_5 = Summed([(dh_y, o[None], o_t[None], 0), (xn_y, d_qkv[None], d_qkv_t[None], 0)], flip, count)
    d_q_late, send_5.keep = tie(d_q, send_5.begin())
    last = blend([[d_q_late], [d_kv]], [[query_weight, wkv], [wq_o, wkv_o]], True, BF16)
    last_came = cross(last)
    last, send_1.total, send_5.keep = tie(last, send_1.total, send_5.keep)
    send_5.keep = serve(send_5.keep, (send_4,))
    send_5.go(send_4)
    first_z.go()
    send_5.keep, send_2.total, _ = tie(send_5.keep, send_2.total, send_4.finish())
    last_came, send_5.keep = tie(last_came, send_5.keep)

    last_came, send_3.total = tie(last_came, send_3.total)
    last_came = serve(last_came, (send_5,))
    last_came, mix, mix_came, first_z.keep, _ = tie(last_came, mix, mix_came, first_z.keep, send_5.finish())
    d_xn = last.astype(F32) + last_came.astype(F32)
    d_xn_m, d_xn_o = d_xn[:, :width], d_xn[:, width:]
    unit_m, unit_o = x_m * inv_one, x_o * inv_one
    e_m, e_o = d_xn_m * gains[0], d_xn_o * gains_o[0]
    mean = (
        jnp.sum(e_m * unit_m, axis=-1, keepdims=True) + jnp.sum(e_o * unit_o, axis=-1, keepdims=True)
    ) / MODEL_WIDTH
    gg_attn_m = jnp.sum(d_xn_m * unit_m, axis=0)
    gg_attn_o = jnp.sum(d_xn_o * unit_o, axis=0)
    d_tok_m = d_hid_m + inv_one * (e_m - unit_m * mean)
    d_tok_o = d_hid_o + inv_one * (e_o - unit_o * mean)
    d_tok_t = swap(d_tok_o)
    gg = jnp.stack([gg_attn_m, gg_mlp_m]) + swap(jnp.stack([gg_attn_o, gg_mlp_o]))
    for bit in range(count.bit_length() - 1):
        gg = gg + lax.ppermute(gg, "dp", [(i, i ^ (1 << bit)) for i in range(count)])
    gg, send_5.total = tie(gg, send_5.total)
    gg = lax.dynamic_slice_in_dim(gg, lax.axis_index("dp") * (width // count), width // count, axis=1)
    d_tokens = merge_rows(d_tok_m, d_tok_t, row)

    mixed_all = mix.astype(F32) + mix_came.astype(F32)
    out_m = (hidden_m + mixed_all[:, :width]).astype(BF16)
    out_o = (hidden_o + mixed_all[:, width:]).astype(BF16)
    mixed = merge_rows(out_m, swap(out_o), row)

    first_z.total = first_z.keep.astype(F32) + first_z.came.astype(F32)
    got = [h.total.astype(F32) for h in (send_1, send_2, send_3, first_z, send_4, send_5)]
    gw_down = got[0].T
    gw_gate = jnp.concatenate([got[1], got[2]], axis=1)
    gw_up = jnp.concatenate([got[3], got[4]], axis=1)
    gw_o, gw_qkv = got[5][:, : o.shape[1]].T, got[5][:, o.shape[1] :]
    return (
        mixed,
        d_tokens,
        gg[0],
        gw_qkv[:, :wide],
        gw_qkv[:, wide : wide + narrow],
        gw_qkv[:, wide + narrow :],
        gw_o,
        gg[1],
        gw_gate,
        gw_up,
        gw_down,
    )


def solution(mesh):
    count = mesh.shape["dp"]
    placed = (
        P("dp", "row"),
        P("dp"),
        P("dp", "row"),
        P("row"),
        P("row", "col"),
        P("row", "col"),
        P("row", "col"),
        P("col", "row"),
        P("row"),
        P("row", "col"),
        P("row", "col"),
        P("col", "row"),
    )

    def body(*args):
        return shards(count, *args)

    return jax.shard_map(
        body,
        mesh=mesh,
        in_specs=placed,
        out_specs=(
            P("dp", "row"),
            P("dp", "row"),
            P(("row", "dp")),
            P(("row", "dp"), "col"),
            P(("row", "dp"), "col"),
            P(("row", "dp"), "col"),
            P("col", ("row", "dp")),
            P(("row", "dp")),
            P(("row", "dp"), "col"),
            P(("row", "dp"), "col"),
            P("col", ("row", "dp")),
        ),
        check_vma=False,
    )
```
